32 devices in a mesh: grp: 2 (over y), tm: 8 (over z, x), head: 2 (over core).
Axes of the slice: x: 2, y: 2, z: 4, core: 2. Of those that a mesh axis runs over, the one named last changes fastest.
Arguments:
- frames: bfloat16 [8192, 1024], P(('grp', 'tm'), 'head'), parts along dimension 0
- segment_ids: int32 [8192], P(('grp', 'tm')), parts along dimension 0, may hold values from 0 to 15, never falling along the last dimension, each value on 1 to 2048 neighbouring positions
- utt_valid: int32 [32], P('grp'), parts along dimension 0, may hold values from 64 to 2047
- attn_gain: float32 [1024], replicated, may hold values from 0.1 to 1.9
- qkv_weight: bfloat16 [1024, 3, 512], P(None, None, 'head')
- out_weight: bfloat16 [512, 1024], P('head'), may hold values from -0.25 to 0.25
- conv_gain: float32 [1024], replicated, may hold values from 0.1 to 1.9
- pointwise_in: bfloat16 [1024, 2, 512], P(None, None, 'head'), may hold values from -0.1875 to 0.1875
- depthwise: float32 [31, 512], P(None, 'head')
- mid_gain: float32 [512], P('head'), may hold values from 0.1 to 1.9
- pointwise_out: bfloat16 [512, 1024], P('head'), may hold values from -0.25 to 0.25
Outputs:
- block_out: bfloat16 [8192, 1024], P(('grp', 'tm'), 'head'), parts along dimension 0
The draws below stay inside these ranges and needn't reach their ends.
There are 2 independent parts, one for each index of `grp`. The reference program is written for one: setup_inputs(seed, part) draws one part's arguments, and reference() takes and returns one part's arrays. A program takes and returns all parts, laid end to end along the dimension named above; an argument that names none is the same for every part. Nothing has to cross between parts.
Inputs may be any that keep to these rules, and one draw needn't show every extreme that they name: `segment_ids`: segment ids never fall along the frames; each utterance holds 1 to 2048 frames, one exactly 2048.
All inputs are finite; a program needn't handle non-finite values.
Results may differ from the reference program's by a relative error of at most 0.015.
Values may be sent and summed in bfloat16 or wider, within the bound.
No kernel may reach another device: no remote copies, remote signals or barrier semaphores. Data moves between devices by JAX's collectives and lax.ppermute only.
A program may use at most 64 MiB of HBM per device.

```python
import math
import jax
import jax.numpy as jnp
import numpy as np
from jax import lax

D = 1024
HEADS = 8
HEAD_DIM = 64
CONV_CH = 512
KERNEL = 31
UTTS = 16
FR_DEV = 512
WIN = 512
TOKENS = 4096
N_HEAD = 2


def draw_frames(key, part):
    key = jax.random.fold_in(key, 3)
    first, second = jax.random.split(key, 2)
    scales = jnp.exp(jax.random.uniform(second, (D,), jnp.float32, math.log(0.3), math.log(3.0)))
    base = jax.random.normal(first, (TOKENS, D), jnp.float32)
    return (base * scales).astype(jnp.bfloat16)


def draw_qkv_weight(key, part):
    key = jax.random.fold_in(key, 5)
    width = HEADS * HEAD_DIM
    base = jax.random.normal(key, (D, 3, width), jnp.float32) * D ** (-0.5)
    return base.astype(jnp.bfloat16)


def draw_depthwise(key, part):
    key = jax.random.fold_in(key, 7)
    first, second = jax.random.split(key, 2)
    ramp = jnp.arange(CONV_CH, dtype=jnp.float32) / (CONV_CH - 1)
    jitter = jnp.exp(jax.random.uniform(second, (CONV_CH,), jnp.float32, math.log(0.7), math.log(1.4)))
    scales = jnp.exp(math.log(0.3) + ramp * math.log(10.0)) * jitter
    base = jax.random.normal(first, (KERNEL, CONV_CH), jnp.float32)
    return (base * scales * KERNEL ** (-0.5)).astype(jnp.float32)


def set_ends(result, stream_key, smallest, top_value):
    longest = result.shape.index(max(result.shape))
    spots = []
    for shift in (0, 1):
        where = [jax.random.randint(jax.random.fold_in(stream_key, axis), (), 0, length) for axis, length in enumerate(result.shape)]
        where[longest] = (where[longest] + shift) % result.shape[longest]
        spots.append(tuple(where))
    return result.at[spots[0]].set(smallest).at[spots[1]].set(top_value)


def shard_levels(stream_key, dims, cuts, low, largest):
    def one(dim, blocks):
        steps = jax.random.uniform(jax.random.fold_in(jax.random.fold_in(stream_key, 6), dim), (blocks,), jnp.float32, low / len(cuts), largest / len(cuts))
        return jnp.repeat(jnp.exp(steps), dims[dim] // blocks).reshape((-1,) + (1,) * (len(dims) - dim - 1))

    loudness = one(*cuts[0])
    for cut in cuts[1:]:
        loudness = loudness * one(*cut)
    return loudness


def profile(amount, total, most, skew):
    loads = [(1 << 20) // math.isqrt(standing ** skew) + 1 for standing in range(2, amount + 1)]
    surplus, holding = total - most - (amount - 1), [1] * (amount - 1)
    while surplus > 0:
        free = [i for i in range(amount - 1) if holding[i] < most]
        pool, remaining = sum([loads[i] for i in free]), surplus
        for i in free:
            extra = min(most - holding[i], max(1, remaining * loads[i] // pool), surplus)
            holding[i] = holding[i] + extra
            surplus = surplus - extra
    return np.array([most] + holding)


def ragged_sizes(key, count, total, most, slope):
    if count == 2:
        one = jax.random.randint(key, (), max(1, total - most), min(most, total - 1) + 1)
        return jnp.stack([one, total - one])
    tallies = jnp.asarray(profile(count, total, most, slope), jnp.int32)
    couples = (count - 1) // 2
    giver, receiver = tallies[1:1 + 2 * couples:2], tallies[2:2 + 2 * couples:2]
    slack = jnp.minimum(giver - 1, most - receiver)
    moved = jax.random.randint(jax.random.fold_in(key, 1), (couples,), 0, 1 << 20) % (slack + 1)
    tallies = tallies.at[1:1 + 2 * couples:2].set(giver - moved).at[2:2 + 2 * couples:2].set(receiver + moved)
    return tallies[jax.random.permutation(jax.random.fold_in(key, 2), count)]


def bell_draw(own_key, extent, scale, most, cuts=(), kind=jnp.bfloat16):
    level = shard_levels(own_key, extent, cuts, -0.22, 0.18) if cuts else 1.0
    result = jax.random.normal(own_key, extent, jnp.float32) * scale * level
    return jnp.minimum(jnp.maximum(result, -most), most).astype(kind)


def setup_inputs(seed: int = 0, part: int = 0) -> dict:
    key_list = jax.random.split(jax.random.key(seed), 12)
    part_splits = jax.random.split(jax.random.fold_in(key_list[11], part), 12)
    frames = draw_frames(jax.random.fold_in(jax.random.fold_in(key_list[11], part), 71), part)
    segment_ids = jnp.searchsorted(jnp.cumsum(ragged_sizes(part_splits[1], UTTS, TOKENS, TOKENS // 2, 2)), jnp.arange(TOKENS), side="right").astype(jnp.int32)
    utt_valid = set_ends(jax.random.randint(part_splits[2], (UTTS,), TOKENS // 64, TOKENS // 2), jax.random.fold_in(part_splits[2], 1), TOKENS // 64, (TOKENS // 2) - 1).astype(jnp.int32)
    attn_gain = jnp.clip(1.0 + 0.18 * jax.random.normal(key_list[3], (D,), jnp.float32), 0.1, 1.9)
    qkv_weight = draw_qkv_weight(jax.random.fold_in(key_list[11], 71), part)
    out_weight = bell_draw(key_list[5], (HEADS * HEAD_DIM, D), (HEADS * HEAD_DIM) ** -0.5, 0.25, ((0, 2),))
    conv_gain = jnp.clip(1.0 + 0.18 * jax.random.normal(key_list[6], (D,), jnp.float32), 0.1, 1.9)
    pointwise_in = bell_draw(key_list[7], (D, 2, CONV_CH), D ** -0.5, 0.1875, ((2, 2),))
    depthwise = draw_depthwise(jax.random.fold_in(key_list[11], 71), part)
    mid_gain = jnp.clip(1.0 + 0.18 * jax.random.normal(key_list[9], (CONV_CH,), jnp.float32), 0.1, 1.9)
    pointwise_out = bell_draw(key_list[10], (CONV_CH, D), CONV_CH ** -0.5, 0.25, ((0, 2),))
    return dict(frames=frames, segment_ids=segment_ids, utt_valid=utt_valid, attn_gain=attn_gain, qkv_weight=qkv_weight, out_weight=out_weight, conv_gain=conv_gain, pointwise_in=pointwise_in, depthwise=depthwise, mid_gain=mid_gain, pointwise_out=pointwise_out)


def normalize(values, gain):
    mean = lax.optimization_barrier(jnp.mean(values, axis=-1, keepdims=True))
    centred = values - mean
    spread = lax.optimization_barrier(jnp.mean(centred * centred, axis=-1, keepdims=True))
    return centred * lax.rsqrt(spread + 1e-05) * gain

def attend(query, keys, values, allowed):
    scores = jnp.einsum('qhe,khe->hqk', query.astype(jnp.float32), keys.astype(jnp.float32)) * HEAD_DIM ** (-0.5)
    masked = jnp.where(allowed[None], scores, -jnp.inf)
    peak = lax.optimization_barrier(jnp.max(masked, axis=-1, keepdims=True))
    peak = jnp.where(jnp.isfinite(peak), peak, 0.0)
    expw = jnp.where(allowed[None], jnp.exp(scores - peak), 0.0)
    total = lax.optimization_barrier(jnp.sum(expw, axis=-1))
    weights = expw.astype(jnp.bfloat16)
    context = jnp.einsum('hqk,khe->qhe', weights.astype(jnp.float32), values.astype(jnp.float32))
    return context / jnp.maximum(total, 1.0).T[:, :, None]

def reference(frames, segment_ids, utt_valid, attn_gain, qkv_weight, out_weight, conv_gain, pointwise_in, depthwise, mid_gain, pointwise_out):
    width = HEADS * HEAD_DIM
    x = frames.astype(jnp.float32)
    normed = normalize(x, attn_gain).astype(jnp.bfloat16)
    ids = jnp.arange(UTTS, dtype=jnp.int32)
    onehot = segment_ids[:, None] == ids[None, :]
    counts = lax.optimization_barrier(jnp.sum(onehot.astype(jnp.int32), axis=0))
    starts = jnp.cumsum(counts) - counts
    position = jnp.arange(TOKENS, dtype=jnp.int32)
    start_of = lax.optimization_barrier(jnp.sum(jnp.where(onehot, starts[None, :], 0), axis=1))
    limit = lax.optimization_barrier(jnp.sum(jnp.where(onehot, utt_valid[None, :], 0), axis=1))
    mark = jnp.where(position - start_of < limit, segment_ids + 1, 0).astype(jnp.int32)
    projected = jnp.dot(normed, qkv_weight.reshape(D, 3 * width), preferred_element_type=jnp.float32)
    projected = projected.reshape(TOKENS, 3, width).astype(jnp.bfloat16)
    query = projected[:, 0].reshape(TOKENS, HEADS, HEAD_DIM)
    keys = projected[:, 1].reshape(TOKENS, HEADS, HEAD_DIM)
    values = projected[:, 2].reshape(TOKENS, HEADS, HEAD_DIM)
    key_pad = jnp.pad(keys, ((WIN, WIN), (0, 0), (0, 0)))
    value_pad = jnp.pad(values, ((WIN, WIN), (0, 0), (0, 0)))
    mark_pad = jnp.pad(mark, (WIN, WIN))
    offsets = jnp.arange(FR_DEV + 2 * WIN, dtype=jnp.int32)[None, :] - jnp.arange(FR_DEV, dtype=jnp.int32)[:, None]
    near = (offsets >= 0) & (offsets <= 2 * WIN)

    def block(index):
        start = (index * FR_DEV).astype(jnp.int32)
        query_block = lax.dynamic_slice_in_dim(query, start, FR_DEV, 0)
        key_block = lax.dynamic_slice_in_dim(key_pad, start, FR_DEV + 2 * WIN, 0)
        value_block = lax.dynamic_slice_in_dim(value_pad, start, FR_DEV + 2 * WIN, 0)
        mark_query = lax.dynamic_slice_in_dim(mark, start, FR_DEV, 0)
        mark_key = lax.dynamic_slice_in_dim(mark_pad, start, FR_DEV + 2 * WIN, 0)
        allowed = near & (mark_query[:, None] == mark_key[None, :]) & (mark_query[:, None] > 0)
        return attend(query_block, key_block, value_block, allowed).reshape(FR_DEV, width).astype(jnp.bfloat16)
    context = lax.map(block, jnp.arange(TOKENS // FR_DEV, dtype=jnp.int32)).reshape(TOKENS, width)
    group_width = width // N_HEAD
    attn_sum = jnp.zeros((TOKENS, D), jnp.float32)
    for group in range(N_HEAD):
        part_sum = jnp.dot(context[:, group * group_width:(group + 1) * group_width], out_weight[group * group_width:(group + 1) * group_width], preferred_element_type=jnp.float32)
        attn_sum = attn_sum + part_sum.astype(jnp.bfloat16).astype(jnp.float32)
    mid = (x + attn_sum).astype(jnp.bfloat16)
    mid_f = mid.astype(jnp.float32)
    normed2 = normalize(mid_f, conv_gain).astype(jnp.bfloat16)
    pre = jnp.dot(normed2, pointwise_in.reshape(D, 2 * CONV_CH), preferred_element_type=jnp.float32).reshape(TOKENS, 2, CONV_CH)
    glu = pre[:, 0] * jax.nn.sigmoid(pre[:, 1])
    glu = jnp.where((mark > 0)[:, None], glu, 0.0).astype(jnp.bfloat16)
    reach = KERNEL // 2
    glu_pad = jnp.pad(glu.astype(jnp.float32), ((reach, reach), (0, 0)))
    mark_conv = jnp.pad(mark, (reach, reach))
    convolved = jnp.zeros((TOKENS, CONV_CH), jnp.float32)
    for tap in range(KERNEL):
        same = (mark_conv[tap:tap + TOKENS] == mark)[:, None]
        convolved = convolved + jnp.where(same, glu_pad[tap:tap + TOKENS], 0.0) * depthwise[tap]
    mean = lax.optimization_barrier(jnp.sum(convolved, axis=-1, keepdims=True)) / CONV_CH
    square = lax.optimization_barrier(jnp.sum(convolved * convolved, axis=-1, keepdims=True)) / CONV_CH
    scaled = (convolved - mean) * lax.rsqrt(square - mean * mean + 1e-05) * mid_gain
    act = (scaled * jax.nn.sigmoid(scaled)).astype(jnp.bfloat16)
    chan_width = CONV_CH // N_HEAD
    conv_sum = jnp.zeros((TOKENS, D), jnp.float32)
    for group in range(N_HEAD):
        part_sum = jnp.dot(act[:, group * chan_width:(group + 1) * chan_width], pointwise_out[group * chan_width:(group + 1) * chan_width], preferred_element_type=jnp.float32)
        conv_sum = conv_sum + part_sum.astype(jnp.bfloat16).astype(jnp.float32)
    return (mid_f + conv_sum).astype(jnp.bfloat16)
```

```python
import jax
import jax.numpy as jnp
from jax import lax
from jax.sharding import PartitionSpec as P

HEAD_DIM = 64
CONV_CH = 512
KERNEL = 31
WIN = 512


def with_halo(block, sides, width):
    for axis, dim in sides:
        count = lax.axis_size(axis)
        forward = [(i, i + 1) for i in range(count - 1)]
        backward = [(target, source) for source, target in forward]
        low = lax.ppermute(
            lax.slice_in_dim(block, block.shape[dim] - width, None, axis=dim), axis, forward
        )
        high = lax.ppermute(lax.slice_in_dim(block, 0, width, axis=dim), axis, backward)
        block = jnp.concatenate([low, block, high], axis=dim)
    return block


def normalize(values, gain):
    mean = jnp.mean(values, axis=-1, keepdims=True)
    centred = values - mean
    spread = jnp.mean(centred * centred, axis=-1, keepdims=True)
    return centred * lax.rsqrt(spread + 1e-05) * gain


def attend(query, keys, values, allowed):
    scores = jnp.einsum(
        "qhe,khe->hqk", query, keys, preferred_element_type=jnp.float32
    ) * HEAD_DIM ** (-0.5)
    masked = jnp.where(allowed[None], scores, -jnp.inf)
    peak = jnp.max(masked, axis=-1, keepdims=True)
    peak = jnp.where(jnp.isfinite(peak), peak, 0.0)
    expw = jnp.where(allowed[None], jnp.exp(scores - peak), 0.0)
    total = jnp.sum(expw, axis=-1)
    weights = expw.astype(jnp.bfloat16)
    context = jnp.einsum("hqk,khe->qhe", weights, values, preferred_element_type=jnp.float32)
    return context / jnp.maximum(total, 1.0).T[:, :, None]


def local(
    frames,
    segment_ids,
    utt_valid,
    attn_gain,
    qkv_weight,
    out_weight,
    conv_gain,
    pointwise_in,
    depthwise,
    mid_gain,
    pointwise_out,
):
    rows, own_width = frames.shape
    width = qkv_weight.shape[2]
    chan = pointwise_in.shape[2]
    swap = [(0, 1), (1, 0)]
    other = lax.ppermute(frames, "head", swap)
    me = lax.axis_index("head")
    whole = jnp.where(
        me == 0,
        jnp.concatenate([frames, other], axis=1),
        jnp.concatenate([other, frames], axis=1),
    )
    x_full = whole.astype(jnp.float32)
    normed = normalize(x_full, attn_gain).astype(jnp.bfloat16)
    ids = jnp.arange(utt_valid.shape[0], dtype=jnp.int32)
    onehot = segment_ids[:, None] == ids[None, :]
    local_counts = jnp.sum(onehot.astype(jnp.int32), axis=0)
    counts = lax.psum(local_counts, "tm")
    starts = jnp.cumsum(counts) - counts
    ends = starts + counts
    total_frames = rows * lax.axis_size("tm")
    position = lax.axis_index("tm") * rows + jnp.arange(rows, dtype=jnp.int32)
    start_of = jnp.sum(jnp.where(onehot, starts[None, :], 0), axis=1)
    limit = jnp.sum(jnp.where(onehot, utt_valid[None, :], 0), axis=1)
    mark = jnp.where(position - start_of < limit, segment_ids + 1, 0)
    wide_pos = lax.axis_index("tm") * rows - WIN + jnp.arange(rows + 2 * WIN, dtype=jnp.int32)
    wide_seg = jnp.sum((wide_pos[:, None] >= ends[None, :]).astype(jnp.int32), axis=1)
    wide_hot = wide_seg[:, None] == ids[None, :]
    wide_start = jnp.sum(jnp.where(wide_hot, starts[None, :], 0), axis=1)
    wide_limit = jnp.sum(jnp.where(wide_hot, utt_valid[None, :], 0), axis=1)
    inside = (wide_pos >= 0) & (wide_pos < total_frames)
    mark_ext = jnp.where(inside & (wide_pos - wide_start < wide_limit), wide_seg + 1, 0)
    projected = jnp.dot(
        normed, qkv_weight.reshape(normed.shape[1], 3 * width), preferred_element_type=jnp.float32
    )
    projected = projected.reshape(rows, 3, width).astype(jnp.bfloat16)
    query = projected[:, 0].reshape(rows, -1, HEAD_DIM)
    paired = projected[:, 1:].reshape(rows, 2 * width)
    paired_ext = with_halo(paired, (("tm", 0),), WIN)
    span = paired_ext.shape[0]
    keys = paired_ext[:, :width].reshape(span, -1, HEAD_DIM)
    values = paired_ext[:, width:].reshape(span, -1, HEAD_DIM)
    offsets = (
        jnp.arange(span, dtype=jnp.int32)[None, :] - jnp.arange(rows, dtype=jnp.int32)[:, None]
    )
    near = (offsets >= 0) & (offsets <= 2 * WIN)
    allowed = near & (mark[:, None] == mark_ext[None, :]) & (mark[:, None] > 0)
    context = attend(query, keys, values, allowed)
    context = context.reshape(rows, width).astype(jnp.bfloat16)
    partial_attn = jnp.dot(context, out_weight, preferred_element_type=jnp.float32)
    partial_attn = partial_attn.astype(jnp.bfloat16)
    attn_sum = partial_attn.astype(jnp.float32) + lax.ppermute(
        partial_attn, "head", swap
    ).astype(jnp.float32)
    mid_full = (x_full + attn_sum).astype(jnp.bfloat16)
    mid_own = lax.dynamic_slice_in_dim(mid_full, lax.axis_index("head") * own_width, own_width, 1)
    normed2 = normalize(mid_full.astype(jnp.float32), conv_gain).astype(jnp.bfloat16)
    pre = jnp.dot(
        normed2,
        pointwise_in.reshape(normed2.shape[1], 2 * chan),
        preferred_element_type=jnp.float32,
    ).reshape(rows, 2, chan)
    glu = pre[:, 0] * jax.nn.sigmoid(pre[:, 1])
    glu = jnp.where((mark > 0)[:, None], glu, 0.0).astype(jnp.bfloat16)
    reach = KERNEL // 2
    glu_ext = with_halo(glu, (("tm", 0),), reach)
    mark_conv = mark_ext[WIN - reach : WIN + rows + reach]
    convolved = jnp.zeros((rows, chan), jnp.float32)
    for tap in range(KERNEL):
        same = (mark_conv[tap : tap + rows] == mark)[:, None]
        convolved = (
            convolved
            + jnp.where(same, glu_ext[tap : tap + rows].astype(jnp.float32), 0.0) * depthwise[tap]
        )
    sum_first, sum_second = lax.psum(
        (jnp.sum(convolved, axis=-1), jnp.sum(convolved * convolved, axis=-1)), "head"
    )
    mean = (sum_first / CONV_CH)[:, None]
    square = (sum_second / CONV_CH)[:, None]
    scaled = (convolved - mean) * lax.rsqrt(square - mean * mean + 1e-05) * mid_gain
    act = (scaled * jax.nn.sigmoid(scaled)).astype(jnp.bfloat16)
    partial_conv = jnp.dot(act, pointwise_out, preferred_element_type=jnp.float32)
    partial_conv = partial_conv.astype(jnp.bfloat16)
    conv_keep = lax.dynamic_slice_in_dim(partial_conv, me * own_width, own_width, 1)
    conv_send = lax.dynamic_slice_in_dim(partial_conv, (1 - me) * own_width, own_width, 1)
    conv_own = conv_keep.astype(jnp.float32) + lax.ppermute(conv_send, "head", swap).astype(
        jnp.float32
    )
    return (mid_own.astype(jnp.float32) + conv_own).astype(jnp.bfloat16)


def solution(mesh):
    in_specs = (
        P(("grp", "tm"), "head"),
        P(("grp", "tm")),
        P("grp"),
        P(),
        P(None, None, "head"),
        P("head", None),
        P(),
        P(None, None, "head"),
        P(None, "head"),
        P("head"),
        P("head", None),
    )
    out_specs = P(("grp", "tm"), "head")
    return jax.shard_map(local, mesh=mesh, in_specs=in_specs, out_specs=out_specs, check_vma=False)
```

```python
import functools
import math

import jax
import jax.numpy as jnp
from jax import lax
from jax.experimental import pallas as pl
from jax.experimental.pallas import tpu as pltpu
from jax.sharding import PartitionSpec as P

HEAD_DIM = 64
CONV_CH = 512
KERNEL = 31
WIN = 512
EDGE = 16
NEG = -1e30
EXP_SCALE = HEAD_DIM ** (-0.5) * math.log2(math.e)
F32 = jnp.float32
BF16 = jnp.bfloat16
VMEM_LIMIT = 28 * 1024 * 1024


def dot(a, b):
    return jnp.dot(a, b, preferred_element_type=F32)


def normalize_halves(own, other, gain_own, gain_other):
    width = own.shape[1] + other.shape[1]
    mean = (
        jnp.sum(own, axis=1, keepdims=True) + jnp.sum(other, axis=1, keepdims=True)
    ) / width
    own = own - mean
    other = other - mean
    spread = (
        jnp.sum(own * own, axis=1, keepdims=True) + jnp.sum(other * other, axis=1, keepdims=True)
    ) / width
    scale = lax.rsqrt(spread + 1e-05)
    return (own * scale * gain_own).astype(BF16), (other * scale * gain_other).astype(BF16)


def qkv_kernel(head, own_ref, other_ref, gain_own, gain_other, w_own, w_other, q_ref, kv_ref):
    n_own, n_other = normalize_halves(
        own_ref[...].astype(F32), other_ref[...].astype(F32), gain_own[0], gain_other[0]
    )
    width = q_ref.shape[1]
    for part in range(3):
        value = (dot(n_own, w_own[part, 0]) + dot(n_other, w_other[part, 0])).astype(BF16)
        if part == 0:
            q_ref[...] = value
        else:
            kv_ref[:, (part - 1) * width : part * width] = value


def project(head, frames, other, gain, weight):
    rows, half = frames.shape
    width = weight.shape[2]
    tile = 256
    w = weight.transpose(1, 0, 2).reshape(3, 2, half, width)
    g = gain.reshape(2, 1, half)
    grid_spec = pltpu.PrefetchScalarGridSpec(
        num_scalar_prefetch=1,
        grid=(rows // tile,),
        in_specs=[
            pl.BlockSpec((tile, half), lambda i, s: (i, 0)),
            pl.BlockSpec((tile, half), lambda i, s: (i, 0)),
            pl.BlockSpec((1, 1, half), lambda i, s: (s[0], 0, 0)),
            pl.BlockSpec((1, 1, half), lambda i, s: (1 - s[0], 0, 0)),
            pl.BlockSpec((3, 1, half, width), lambda i, s: (0, s[0], 0, 0)),
            pl.BlockSpec((3, 1, half, width), lambda i, s: (0, 1 - s[0], 0, 0)),
        ],
        out_specs=[
            pl.BlockSpec((tile, width), lambda i, s: (i, 0)),
            pl.BlockSpec((tile, 2 * width), lambda i, s: (i, 0)),
        ],
    )
    return pl.pallas_call(
        qkv_kernel,
        grid_spec=grid_spec,
        out_shape=[
            jax.ShapeDtypeStruct((rows, width), BF16),
            jax.ShapeDtypeStruct((rows, 2 * width), BF16),
        ],
        compiler_params=pltpu.CompilerParams(vmem_limit_bytes=VMEM_LIMIT),
        name="project",
    )(head, frames, other, g, g, w, w)


def attend_kernel(q_ref, own_ref, low_ref, high_ref, lo_ref, hi_ref, out_ref):
    rows, width = q_ref.shape
    tile = rows // 2
    half = WIN // 2
    lane = lax.broadcasted_iota(jnp.int32, (tile, 128), 1)
    for block in range(2):
        at = block * tile
        pieces = (
            ((low_ref, 0, WIN, -WIN), (own_ref, 0, rows, 0), (high_ref, 0, half, rows))
            if block == 0
            else ((low_ref, half, half, -WIN), (own_ref, 0, rows, 0), (high_ref, 0, WIN, rows))
        )
        lo = lo_ref[at : at + tile, :]
        hi = hi_ref[at : at + tile, :]
        biases = []
        for _, first, size, origin in pieces:
            u = lax.broadcasted_iota(jnp.int32, (tile, size), 1) + (origin + first)
            biases.append(jnp.where((u >= lo) & (u < hi), 0.0, NEG))
        for pair in range(width // 128):
            cols = slice(pair * 128, pair * 128 + 128)
            vcols = slice(width + pair * 128, width + pair * 128 + 128)
            q = q_ref[at : at + tile, cols]
            outs = []
            for sub in range(2):
                q_sub = jnp.where((lane >= 64) == (sub == 1), q, jnp.zeros_like(q))
                scores = []
                for (ref, first, size, _), bias in zip(pieces, biases):
                    k = ref[first : first + size, cols]
                    s = lax.dot_general(
                        q_sub, k, (((1,), (1,)), ((), ())), preferred_element_type=F32
                    )
                    scores.append(s + bias)
                peak = functools.reduce(
                    jnp.maximum, [jnp.max(s, axis=1, keepdims=True) for s in scores]
                )
                total = jnp.zeros((tile, 1), F32)
                context = jnp.zeros((tile, 128), F32)
                for (ref, first, size, _), s in zip(pieces, scores):
                    expw = jnp.exp2((s - peak) * EXP_SCALE)
                    total = total + jnp.sum(expw, axis=1, keepdims=True)
                    context = context + dot(
                        expw.astype(BF16), ref[first : first + size, vcols]
                    )
                outs.append(context / jnp.maximum(total, 1.0))
            joined = jnp.where(lane >= 64, outs[1], outs[0])
            out_ref[at : at + tile, cols] = jnp.where(hi > lo, joined, 0.0).astype(BF16)


def attend(q, own, low, high, lo, hi):
    return pl.pallas_call(
        attend_kernel,
        out_shape=jax.ShapeDtypeStruct(q.shape, BF16),
        compiler_params=pltpu.CompilerParams(vmem_limit_bytes=VMEM_LIMIT),
        name="attend",
    )(q, own, low, high, lo, hi)


def gate_kernel(
    head,
    ctx_own, ctx_other,
    x_own, x_other,
    out_own, out_other,
    gain_ref,
    in_own, in_other,
    valid_ref,
    glu_ref, edge_ref, mid_keep, mid_send,
):
    h = head[0]
    half = x_own.shape[1]
    rows = glu_ref.shape[0]
    here = pl.ds(pl.multiple_of(h * (rows - 2 * EDGE), EDGE), rows)
    c_own = ctx_own[here, :]
    c_other = ctx_other[here, :]
    own_cols = pl.ds(pl.multiple_of(h * half, half), half)
    other_cols = pl.ds(pl.multiple_of((1 - h) * half, half), half)

    def mid(cols, x_ref):
        first = dot(c_own, out_own[:, cols]).astype(BF16).astype(F32)
        second = dot(c_other, out_other[:, cols]).astype(BF16).astype(F32)
        return (x_ref[here, :].astype(F32) + (first + second)).astype(BF16)

    m_own = mid(own_cols, x_own)
    m_other = mid(other_cols, x_other)
    keep = rows - EDGE

    @pl.when(h == 0)
    def _():
        mid_keep[...] = m_own[:keep]
        mid_send[...] = m_other[:keep]

    @pl.when(h == 1)
    def _():
        mid_keep[...] = m_own[EDGE:]
        mid_send[...] = m_other[EDGE:]

    n_own, n_other = normalize_halves(
        m_own.astype(F32), m_other.astype(F32), gain_ref[h], gain_ref[1 - h]
    )
    valid = valid_ref[here, :] > 0
    glus = []
    for w_ref in (in_own, in_other):
        value = dot(n_own, w_ref[0, own_cols, :]) + dot(n_other, w_ref[0, other_cols, :])
        gate = dot(n_own, w_ref[1, own_cols, :]) + dot(n_other, w_ref[1, other_cols, :])
        glu = value / (1.0 + jnp.exp(-gate))
        glus.append(jnp.where(valid, glu, 0.0).astype(BF16))
    chan = glus[0].shape[1]
    glu_ref[:, :chan] = glus[0]
    glu_ref[:, chan:] = glus[1]

    @pl.when(h == 0)
    def _():
        edge_ref[:, :chan] = glus[1][:EDGE]
        edge_ref[:, chan:] = glus[0][:EDGE]

    @pl.when(h == 1)
    def _():
        edge_ref[:, :chan] = glus[1][rows - EDGE :]
        edge_ref[:, chan:] = glus[0][rows - EDGE :]


def gated(head, ctx_own, ctx_other, x_own, x_other, out_own, out_other, gain, in_own, in_other, valid):
    rows = x_own.shape[0] // 2 + EDGE
    half = x_own.shape[1]
    chan = in_own.shape[2]
    vmem = pl.BlockSpec(memory_space=pltpu.VMEM)
    return pl.pallas_call(
        gate_kernel,
        in_specs=[pl.BlockSpec(memory_space=pltpu.SMEM)] + [vmem] * 10,
        out_specs=[vmem] * 4,
        out_shape=[
            jax.ShapeDtypeStruct((rows, 2 * chan), BF16),
            jax.ShapeDtypeStruct((EDGE, 2 * chan), BF16),
            jax.ShapeDtypeStruct((rows - EDGE, half), BF16),
            jax.ShapeDtypeStruct((rows - EDGE, half), BF16),
        ],
        compiler_params=pltpu.CompilerParams(vmem_limit_bytes=VMEM_LIMIT),
        name="gated",
    )(head, ctx_own, ctx_other, x_own, x_other, out_own, out_other,
      gain.reshape(2, 1, half), in_own, in_other, valid)


def conv_kernel(head, glu_ref, edge_ref, lo_ref, hi_ref, dw_own, dw_other, g_own, g_other,
                act_ref, ext):
    h = head[0]
    rows, width = act_ref.shape
    chan = width // 2
    got = glu_ref.shape[0]
    ext[pl.ds(pl.multiple_of((1 - h) * EDGE, EDGE), got), :] = glu_ref[...].astype(F32)
    ext[pl.ds(pl.multiple_of(h * got, EDGE), EDGE), :] = edge_ref[...].astype(F32)
    first = pl.multiple_of(h * rows, rows)
    at = lax.broadcasted_iota(jnp.int32, (rows, 1), 0) + first
    low = lo_ref[pl.ds(first, rows), :] - at
    high = hi_ref[pl.ds(first, rows), :] - at
    reach = KERNEL // 2
    step = 64
    for base in range(0, rows, step):
        low_b = jnp.broadcast_to(low[base : base + step], (step, 128))
        high_b = jnp.broadcast_to(high[base : base + step], (step, 128))
        sums = jnp.zeros((step, 128), F32)
        squares = jnp.zeros((step, 128), F32)
        results = []
        for col in range(0, width, 128):
            dw_ref, c = (dw_own, col) if col < chan else (dw_other, col - chan)
            total = jnp.zeros((step, 128), F32)
            for tap in range(KERNEL):
                shift = tap - reach
                row = base + EDGE + shift
                piece = ext[row : row + step, col : col + 128]
                same = (low_b <= shift) & (high_b > shift)
                total = total + jnp.where(same, piece, 0.0) * dw_ref[tap : tap + 1, c : c + 128]
            sums = sums + total
            squares = squares + total * total
            results.append(total)
        mean = jnp.sum(sums, axis=1, keepdims=True) / CONV_CH
        square = jnp.sum(squares, axis=1, keepdims=True) / CONV_CH
        scale = lax.rsqrt(square - mean * mean + 1e-05)
        for col, total in zip(range(0, width, 128), results):
            g_ref, c = (g_own, col) if col < chan else (g_other, col - chan)
            y = (total - mean) * scale * g_ref[:, c : c + 128]
            act_ref[base : base + step, col : col + 128] = (y / (1.0 + jnp.exp(-y))).astype(BF16)


def convolve(head, glu, edge, lo, hi, dw_own, dw_other, g_own, g_other):
    rows = glu.shape[0] - EDGE
    width = glu.shape[1]
    vmem = pl.BlockSpec(memory_space=pltpu.VMEM)
    return pl.pallas_call(
        conv_kernel,
        in_specs=[pl.BlockSpec(memory_space=pltpu.SMEM)] + [vmem] * 8,
        out_specs=vmem,
        out_shape=jax.ShapeDtypeStruct((rows, width), BF16),
        scratch_shapes=[pltpu.VMEM((rows + 2 * EDGE, width), F32)],
        compiler_params=pltpu.CompilerParams(vmem_limit_bytes=VMEM_LIMIT),
        name="convolve",
    )(head, glu, edge, lo, hi, dw_own, dw_other, g_own.reshape(1, -1), g_other.reshape(1, -1))


def finish_kernel(head, act_own, act_other, mid_own, mid_other, w_own, w_other, out_ref):
    h = head[0]
    rows, chan2 = act_own.shape
    chan = chan2 // 2
    half = out_ref.shape[1]
    cols = pl.ds(pl.multiple_of(h * half, half), half)
    w_a = w_own[:, cols]
    w_b = w_other[:, cols]

    def rows_of(act, mid, flip):
        first = dot(act[:, :chan], w_b if flip else w_a).astype(BF16).astype(F32)
        second = dot(act[:, chan:], w_a if flip else w_b).astype(BF16).astype(F32)
        return (mid[...].astype(F32) + (first + second)).astype(BF16)

    out_ref[pl.ds(pl.multiple_of(h * rows, rows), rows), :] = rows_of(act_own, mid_own, False)
    out_ref[pl.ds(pl.multiple_of((1 - h) * rows, rows), rows), :] = rows_of(
        act_other, mid_other, True
    )


def finish(head, act_own, act_other, mid_own, mid_other, w_own, w_other):
    rows, half = mid_own.shape
    vmem = pl.BlockSpec(memory_space=pltpu.VMEM)
    return pl.pallas_call(
        finish_kernel,
        in_specs=[pl.BlockSpec(memory_space=pltpu.SMEM)] + [vmem] * 6,
        out_specs=vmem,
        out_shape=jax.ShapeDtypeStruct((2 * rows, half), BF16),
        compiler_params=pltpu.CompilerParams(vmem_limit_bytes=VMEM_LIMIT),
        name="finish",
    )(head, act_own, act_other, mid_own, mid_other, w_own, w_other)


def local(
    blocks,
    frames,
    segment_ids,
    utt_valid,
    attn_gain,
    qkv_weight,
    out_weight,
    conv_gain,
    pointwise_in,
    depthwise,
    mid_gain,
    pointwise_out,
):
    rows = frames.shape[0]

    def swap(value):
        return lax.ppermute(value, "head", [(0, 1), (1, 0)])

    head = lax.axis_index("head").astype(jnp.int32).reshape(1)
    block = lax.axis_index("tm")
    other = swap(frames)
    q, kv = project(head, frames, other, attn_gain, qkv_weight)
    low = lax.ppermute(kv, "tm", [(i, i + 1) for i in range(blocks - 1)])
    high = lax.ppermute(kv, "tm", [(i + 1, i) for i in range(blocks - 1)])

    pointwise = pointwise_in.transpose(1, 0, 2)
    mine, segment_ids = lax.optimization_barrier(
        ((out_weight, pointwise, depthwise, mid_gain, pointwise_out, kv), segment_ids)
    )
    out_weight, pointwise, depthwise, mid_gain, pointwise_out, _ = mine
    out_other = swap(out_weight)
    pointwise_other = swap(pointwise)
    depthwise_other = swap(depthwise)
    mid_gain_other = swap(mid_gain)
    pointwise_out_other = swap(pointwise_out)

    ids = jnp.arange(utt_valid.shape[0], dtype=jnp.int32)
    onehot = segment_ids[:, None] == ids[None, :]
    counts = lax.psum(jnp.sum(onehot.astype(jnp.int32), axis=0), "tm")
    starts = jnp.cumsum(counts) - counts
    stops = starts + jnp.minimum(counts, utt_valid)
    origin = block * rows
    position = jnp.arange(rows, dtype=jnp.int32)
    lo = jnp.sum(jnp.where(onehot, starts[None, :] - origin, 0), axis=1)
    hi = jnp.sum(jnp.where(onehot, stops[None, :] - origin, 0), axis=1)
    valid = position < hi
    lo = jnp.where(valid, lo, 0)
    hi = jnp.where(valid, hi, 0)
    near_lo = jnp.where(valid, jnp.maximum(lo, position - WIN), 0)
    near_hi = jnp.where(valid, jnp.minimum(hi, position + (WIN + 1)), 0)

    context = attend(q, kv, low, high, near_lo[:, None], near_hi[:, None])
    context_other = swap(context)
    glu, edge, mid_keep, mid_send = gated(
        head, context, context_other, frames, other, out_weight, out_other, conv_gain,
        pointwise, pointwise_other, valid.astype(jnp.int32)[:, None],
    )
    edges = [(2 * i, 2 * (i - 1) + 1) for i in range(1, blocks)]
    edges += [(2 * i + 1, 2 * (i + 1)) for i in range(blocks - 1)]
    edge = lax.ppermute(edge, ("tm", "head"), edges)
    mid_other = swap(mid_send)
    act = convolve(
        head, glu, edge, lo[:, None], hi[:, None], depthwise, depthwise_other, mid_gain,
        mid_gain_other,
    )
    act_other = swap(act)
    return finish(
        head, act, act_other, mid_keep, mid_other, pointwise_out, pointwise_out_other
    )


def solution(mesh):
    in_specs = (
        P(("grp", "tm"), "head"),
        P(("grp", "tm")),
        P("grp"),
        P(),
        P(None, None, "head"),
        P("head", None),
        P(),
        P(None, None, "head"),
        P(None, "head"),
        P("head"),
        P("head", None),
    )
    out_specs = P(("grp", "tm"), "head")
    return jax.shard_map(
        functools.partial(local, mesh.shape["tm"]),
        mesh=mesh,
        in_specs=in_specs,
        out_specs=out_specs,
        check_vma=False,
    )
```

```python
import functools
import math

import jax
import jax.numpy as jnp
from jax import lax
from jax.experimental import pallas as pl
from jax.experimental.pallas import tpu as pltpu
from jax.sharding import PartitionSpec as P

HEAD_DIM = 64
CONV_CH = 512
KERNEL = 31
WIN = 512
EDGE = 16
NEG = -1e30
EXP_SCALE = HEAD_DIM ** (-0.5) * math.log2(math.e)
F32 = jnp.float32
BF16 = jnp.bfloat16
VMEM_LIMIT = 28 * 1024 * 1024


def dot(a, b):
    return jnp.dot(a, b, preferred_element_type=F32)


def normalize_halves(own, other, gain_own, gain_other):
    width = own.shape[1] + other.shape[1]
    mean = (
        jnp.sum(own, axis=1, keepdims=True) + jnp.sum(other, axis=1, keepdims=True)
    ) / width
    own = own - mean
    other = other - mean
    spread = (
        jnp.sum(own * own, axis=1, keepdims=True) + jnp.sum(other * other, axis=1, keepdims=True)
    ) / width
    scale = lax.rsqrt(spread + 1e-05)
    return (own * scale * gain_own).astype(BF16), (other * scale * gain_other).astype(BF16)


def qkv_kernel(
    meta, own_ref, other_ref, gain_own, gain_other, w_own, w_other,
    keep_ref, query_ref, send_ref, pass_ref,
):
    first = meta[1] == 0
    n_own, n_other = normalize_halves(
        own_ref[...].astype(F32), other_ref[...].astype(F32), gain_own[0], gain_other[0]
    )
    for slot, part in enumerate((1, 2, 0)):
        value = (dot(n_own, w_own[part, 0]) + dot(n_other, w_other[part, 0])).astype(BF16)
        sub = value.shape[1] // 2
        cols = slice(slot * sub, slot * sub + sub)
        keep = jnp.where(first, value[:, :sub], value[:, sub:])
        send = jnp.where(first, value[:, sub:], value[:, :sub])
        send_ref[:, cols] = send
        if slot < 2:
            keep_ref[:, cols] = keep
            pass_ref[:, cols] = send
        else:
            query_ref[...] = keep


def project(meta, frames, other, gain, weight):
    rows, half = frames.shape
    width = weight.shape[2]
    tile = 256
    w = weight.transpose(1, 0, 2).reshape(3, 2, half, width)
    g = gain.reshape(2, 1, half)
    grid_spec = pltpu.PrefetchScalarGridSpec(
        num_scalar_prefetch=1,
        grid=(rows // tile,),
        in_specs=[
            pl.BlockSpec((tile, half), lambda i, s: (i, 0)),
            pl.BlockSpec((tile, half), lambda i, s: (i, 0)),
            pl.BlockSpec((1, 1, half), lambda i, s: (s[0], 0, 0)),
            pl.BlockSpec((1, 1, half), lambda i, s: (1 - s[0], 0, 0)),
            pl.BlockSpec((3, 1, half, width), lambda i, s: (0, s[0], 0, 0)),
            pl.BlockSpec((3, 1, half, width), lambda i, s: (0, 1 - s[0], 0, 0)),
        ],
        out_specs=[
            pl.BlockSpec((tile, width), lambda i, s: (i, 0)),
            pl.BlockSpec((tile, width // 2), lambda i, s: (i, 0)),
            pl.BlockSpec((tile, 3 * width // 2), lambda i, s: (i, 0)),
            pl.BlockSpec((tile, width), lambda i, s: (i, 0)),
        ],
    )
    return pl.pallas_call(
        qkv_kernel,
        grid_spec=grid_spec,
        out_shape=[
            jax.ShapeDtypeStruct((rows, width), BF16),
            jax.ShapeDtypeStruct((rows, width // 2), BF16),
            jax.ShapeDtypeStruct((rows, 3 * width // 2), BF16),
            jax.ShapeDtypeStruct((rows, width), BF16),
        ],
        compiler_params=pltpu.CompilerParams(vmem_limit_bytes=VMEM_LIMIT),
        name="project",
    )(meta, frames, other, g, g, w, w)


def bounds_kernel(meta, counts, valid, lo_own, hi_own, lo_pair, hi_pair):
    utts = valid.shape[0]
    spans = []
    start = jnp.int32(0)
    for s in range(utts):
        count = lax.fori_loop(
            0, counts.shape[0], lambda b, acc, s=s: acc + counts[b, s], jnp.int32(0)
        )
        spans.append((start, start + jnp.minimum(count, valid[s])))
        start = start + count
    for slot, (lo_ref, hi_ref) in enumerate(((lo_own, hi_own), (lo_pair, hi_pair))):
        origin = meta[2 + slot]
        at = lax.broadcasted_iota(jnp.int32, lo_ref.shape, 0)
        lo = jnp.zeros(lo_ref.shape, jnp.int32)
        hi = jnp.zeros(lo_ref.shape, jnp.int32)
        for begin, end in spans:
            inside = (at >= begin - origin) & (at < end - origin)
            lo = jnp.where(inside, begin - origin, lo)
            hi = jnp.where(inside, end - origin, hi)
        lo_ref[...] = lo
        hi_ref[...] = hi


def bounds(meta, counts, valid, rows):
    smem = pl.BlockSpec(memory_space=pltpu.SMEM)
    vmem = pl.BlockSpec(memory_space=pltpu.VMEM)
    return pl.pallas_call(
        bounds_kernel,
        in_specs=[smem] * 3,
        out_specs=[vmem] * 4,
        out_shape=[jax.ShapeDtypeStruct((rows, 128), jnp.int32)] * 4,
        compiler_params=pltpu.CompilerParams(vmem_limit_bytes=VMEM_LIMIT),
        name="bounds",
    )(meta, counts, valid)


def attend_kernel(a_high, query, center, side_a, side_b, lo_ref, hi_ref, out_ref, ext, q_ref, sems):
    rows, width = q_ref.shape
    flip = a_high[0]
    at_a = pl.multiple_of(flip * 2 * rows, rows)
    at_b = pl.multiple_of((1 - flip) * 2 * rows, rows)
    both = pl.ds(0, 2 * width)
    copies = [
        pltpu.make_async_copy(center.at[:, both], ext.at[pl.ds(rows, rows)], sems.at[0]),
        pltpu.make_async_copy(query.at[:, pl.ds(query.shape[1] - width, width)], q_ref, sems.at[1]),
        pltpu.make_async_copy(side_a.at[:, both], ext.at[pl.ds(at_a, rows)], sems.at[2]),
        pltpu.make_async_copy(side_b.at[:, both], ext.at[pl.ds(at_b, rows)], sems.at[3]),
    ]
    for copy in copies:
        copy.start()
    for copy in copies:
        copy.wait()
    tile = rows // 2
    span = tile + 2 * WIN
    lane = lax.broadcasted_iota(jnp.int32, (tile, width), 1)
    for block in range(2):
        at = block * tile
        position = lax.broadcasted_iota(jnp.int32, (tile, 1), 0) + at
        lo = lo_ref[at : at + tile, :1]
        hi = hi_ref[at : at + tile, :1]
        near_lo = jnp.maximum(lo, position - WIN)
        near_hi = jnp.minimum(hi, position + (WIN + 1))
        u = lax.broadcasted_iota(jnp.int32, (tile, span), 1) + (at - WIN)
        bias = jnp.where((u >= near_lo) & (u < near_hi), 0.0, NEG)
        first = at + rows - WIN
        k = ext[first : first + span, :width]
        v = ext[first : first + span, width:]
        q = q_ref[at : at + tile, :]
        outs = []
        for sub in range(2):
            q_sub = jnp.where((lane >= HEAD_DIM) == (sub == 1), q, jnp.zeros_like(q))
            scores = (
                lax.dot_general(q_sub, k, (((1,), (1,)), ((), ())), preferred_element_type=F32)
                + bias
            )
            peak = jnp.max(scores, axis=1, keepdims=True)
            expw = jnp.exp2((scores - peak) * EXP_SCALE)
            total = jnp.sum(expw, axis=1, keepdims=True)
            outs.append(dot(expw.astype(BF16), v) / jnp.maximum(total, 1.0))
        joined = jnp.where(lane >= HEAD_DIM, outs[1], outs[0])
        out_ref[at : at + tile, :] = jnp.where(hi > lo, joined, 0.0).astype(BF16)


def attend(a_high, query, center, side_a, side_b, lo, hi):
    rows, width = side_b.shape[0], side_b.shape[1] // 2
    vmem = pl.BlockSpec(memory_space=pltpu.VMEM)
    anywhere = pl.BlockSpec(memory_space=pl.ANY)
    return pl.pallas_call(
        attend_kernel,
        in_specs=[pl.BlockSpec(memory_space=pltpu.SMEM)] + [anywhere] * 4 + [vmem] * 2,
        out_specs=vmem,
        out_shape=jax.ShapeDtypeStruct((rows, width), BF16),
        scratch_shapes=[
            pltpu.VMEM((3 * rows, 2 * width), BF16),
            pltpu.VMEM((rows, width), BF16),
            pltpu.SemaphoreType.DMA((4,)),
        ],
        compiler_params=pltpu.CompilerParams(vmem_limit_bytes=VMEM_LIMIT),
        name="attend",
    )(a_high, query, center, side_a, side_b, lo, hi)


def gate_kernel(
    meta,
    mine_own, pair_own, mine_other, pair_other,
    x_own, x_other,
    out_own, out_other,
    gain_ref,
    in_own, in_other,
    lo_ref, hi_ref,
    glu_ref, edge_ref, mid_keep, mid_send,
):
    h = meta[0]
    first = meta[1] == 0
    half = x_own.shape[1]
    rows = glu_ref.shape[0]
    here = pl.ds(pl.multiple_of(h * (rows - 2 * EDGE), EDGE), rows)

    def joined(mine, pair):
        mine = mine[here, :]
        pair = pair[here, :]
        return jnp.concatenate(
            [jnp.where(first, mine, pair), jnp.where(first, pair, mine)], axis=1
        )

    c_own = joined(mine_own, pair_own)
    c_other = joined(mine_other, pair_other)
    own_cols = pl.ds(pl.multiple_of(h * half, half), half)
    other_cols = pl.ds(pl.multiple_of((1 - h) * half, half), half)

    def mid(cols, x_ref):
        first = dot(c_own, out_own[:, cols]).astype(BF16).astype(F32)
        second = dot(c_other, out_other[:, cols]).astype(BF16).astype(F32)
        return (x_ref[here, :].astype(F32) + (first + second)).astype(BF16)

    m_own = mid(own_cols, x_own)
    m_other = mid(other_cols, x_other)
    keep = rows - EDGE

    @pl.when(h == 0)
    def _():
        mid_keep[...] = m_own[:keep]
        mid_send[...] = m_other[:keep]

    @pl.when(h == 1)
    def _():
        mid_keep[...] = m_own[EDGE:]
        mid_send[...] = m_other[EDGE:]

    n_own, n_other = normalize_halves(
        m_own.astype(F32), m_other.astype(F32), gain_ref[h], gain_ref[1 - h]
    )
    valid = (hi_ref[here, :] > lo_ref[here, :])[:, :1]
    glus = []
    for w_ref in (in_own, in_other):
        value = dot(n_own, w_ref[0, own_cols, :]) + dot(n_other, w_ref[0, other_cols, :])
        gate = dot(n_own, w_ref[1, own_cols, :]) + dot(n_other, w_ref[1, other_cols, :])
        glu = value / (1.0 + jnp.exp(-gate))
        glus.append(jnp.where(valid, glu, 0.0).astype(BF16))
    chan = glus[0].shape[1]
    glu_ref[:, :chan] = glus[0]
    glu_ref[:, chan:] = glus[1]

    @pl.when(h == 0)
    def _():
        edge_ref[:, :chan] = glus[1][:EDGE]
        edge_ref[:, chan:] = glus[0][:EDGE]

    @pl.when(h == 1)
    def _():
        edge_ref[:, :chan] = glus[1][rows - EDGE :]
        edge_ref[:, chan:] = glus[0][rows - EDGE :]


def gated(meta, contexts, x_own, x_other, out_own, out_other, gain, in_own, in_other, lo, hi):
    rows = x_own.shape[0] // 2 + EDGE
    half = x_own.shape[1]
    chan = in_own.shape[2]
    vmem = pl.BlockSpec(memory_space=pltpu.VMEM)
    return pl.pallas_call(
        gate_kernel,
        in_specs=[pl.BlockSpec(memory_space=pltpu.SMEM)] + [vmem] * 13,
        out_specs=[vmem] * 4,
        out_shape=[
            jax.ShapeDtypeStruct((rows, 2 * chan), BF16),
            jax.ShapeDtypeStruct((EDGE, 2 * chan), BF16),
            jax.ShapeDtypeStruct((rows - EDGE, half), BF16),
            jax.ShapeDtypeStruct((rows - EDGE, half), BF16),
        ],
        compiler_params=pltpu.CompilerParams(vmem_limit_bytes=VMEM_LIMIT),
        name="gated",
    )(meta, *contexts, x_own, x_other, out_own, out_other,
      gain.reshape(2, 1, half), in_own, in_other, lo, hi)


def conv_kernel(meta, glu_ref, edge_ref, lo_ref, hi_ref, dw_own, dw_other, g_own, g_other,
                act_ref, ext):
    h = meta[0]
    rows, width = act_ref.shape
    chan = width // 2
    got = glu_ref.shape[0]
    ext[pl.ds(pl.multiple_of((1 - h) * EDGE, EDGE), got), :] = glu_ref[...].astype(F32)
    ext[pl.ds(pl.multiple_of(h * got, EDGE), EDGE), :] = edge_ref[...].astype(F32)
    first = pl.multiple_of(h * rows, rows)
    at = lax.broadcasted_iota(jnp.int32, (rows, 128), 0) + first
    low = lo_ref[pl.ds(first, rows), :] - at
    high = hi_ref[pl.ds(first, rows), :] - at
    reach = KERNEL // 2
    step = 64
    for base in range(0, rows, step):
        low_b = low[base : base + step]
        high_b = high[base : base + step]
        sums = jnp.zeros((step, 128), F32)
        squares = jnp.zeros((step, 128), F32)
        results = []
        for col in range(0, width, 128):
            dw_ref, c = (dw_own, col) if col < chan else (dw_other, col - chan)
            total = jnp.zeros((step, 128), F32)
            for tap in range(KERNEL):
                shift = tap - reach
                row = base + EDGE + shift
                piece = ext[row : row + step, col : col + 128]
                same = (low_b <= shift) & (high_b > shift)
                total = total + jnp.where(same, piece, 0.0) * dw_ref[tap : tap + 1, c : c + 128]
            sums = sums + total
            squares = squares + total * total
            results.append(total)
        mean = jnp.sum(sums, axis=1, keepdims=True) / CONV_CH
        square = jnp.sum(squares, axis=1, keepdims=True) / CONV_CH
        scale = lax.rsqrt(square - mean * mean + 1e-05)
        for col, total in zip(range(0, width, 128), results):
            g_ref, c = (g_own, col) if col < chan else (g_other, col - chan)
            y = (total - mean) * scale * g_ref[:, c : c + 128]
            act_ref[base : base + step, col : col + 128] = (y / (1.0 + jnp.exp(-y))).astype(BF16)


def convolve(meta, glu, edge, lo, hi, dw_own, dw_other, g_own, g_other):
    rows = glu.shape[0] - EDGE
    width = glu.shape[1]
    vmem = pl.BlockSpec(memory_space=pltpu.VMEM)
    return pl.pallas_call(
        conv_kernel,
        in_specs=[pl.BlockSpec(memory_space=pltpu.SMEM)] + [vmem] * 8,
        out_specs=vmem,
        out_shape=jax.ShapeDtypeStruct((rows, width), BF16),
        scratch_shapes=[pltpu.VMEM((rows + 2 * EDGE, width), F32)],
        compiler_params=pltpu.CompilerParams(vmem_limit_bytes=VMEM_LIMIT),
        name="convolve",
    )(meta, glu, edge, lo, hi, dw_own, dw_other, g_own.reshape(1, -1), g_other.reshape(1, -1))


def finish_kernel(meta, act_own, act_other, mid_own, mid_other, w_own, w_other, out_ref):
    h = meta[0]
    rows, chan2 = act_own.shape
    chan = chan2 // 2
    half = out_ref.shape[1]
    cols = pl.ds(pl.multiple_of(h * half, half), half)
    w_a = w_own[:, cols]
    w_b = w_other[:, cols]

    def rows_of(act, mid, flip):
        first = dot(act[:, :chan], w_b if flip else w_a).astype(BF16).astype(F32)
        second = dot(act[:, chan:], w_a if flip else w_b).astype(BF16).astype(F32)
        return (mid[...].astype(F32) + (first + second)).astype(BF16)

    out_ref[pl.ds(pl.multiple_of(h * rows, rows), rows), :] = rows_of(act_own, mid_own, False)
    out_ref[pl.ds(pl.multiple_of((1 - h) * rows, rows), rows), :] = rows_of(
        act_other, mid_other, True
    )


def finish(meta, act_own, act_other, mid_own, mid_other, w_own, w_other):
    rows, half = mid_own.shape
    vmem = pl.BlockSpec(memory_space=pltpu.VMEM)
    return pl.pallas_call(
        finish_kernel,
        in_specs=[pl.BlockSpec(memory_space=pltpu.SMEM)] + [vmem] * 6,
        out_specs=vmem,
        out_shape=jax.ShapeDtypeStruct((2 * rows, half), BF16),
        compiler_params=pltpu.CompilerParams(vmem_limit_bytes=VMEM_LIMIT),
        name="finish",
    )(meta, act_own, act_other, mid_own, mid_other, w_own, w_other)


def local(
    blocks,
    frames,
    segment_ids,
    utt_valid,
    attn_gain,
    qkv_weight,
    out_weight,
    conv_gain,
    pointwise_in,
    depthwise,
    mid_gain,
    pointwise_out,
):
    rows = frames.shape[0]

    def swap(value):
        return lax.ppermute(value, "head", [(0, 1), (1, 0)])

    def shift(value, step):
        pairs = [(i, i - step if i % 2 == 0 else i + step) for i in range(blocks)]
        return lax.ppermute(value, "tm", [p for p in pairs if 0 <= p[1] < blocks])

    def exchange(value):
        return lax.ppermute(value, "tm", [(i, i ^ 1) for i in range(blocks)])

    block = lax.axis_index("tm").astype(jnp.int32)
    column = block % 2
    meta = jnp.stack([
        lax.axis_index("head").astype(jnp.int32),
        column,
        block * rows,
        (block + 1 - 2 * column) * rows,
    ])
    ids = jnp.arange(utt_valid.shape[0], dtype=jnp.int32)
    counts = jnp.sum((segment_ids[None, :] == ids[:, None]).astype(jnp.int32), axis=1)
    counts = lax.all_to_all(
        jnp.broadcast_to(counts[None, :], (blocks, counts.shape[0])), "tm", 0, 0
    )
    other = swap(frames)
    keep, query, send, passed = project(meta, frames, other, attn_gain, qkv_weight)
    pair = exchange(send)
    far_pair = shift(keep, 2)
    far_own = shift(passed, 1)

    pointwise = pointwise_in.transpose(1, 0, 2)
    out_weight, pointwise, depthwise, mid_gain, pointwise_out, _ = lax.optimization_barrier(
        (out_weight, pointwise, depthwise, mid_gain, pointwise_out, keep)
    )
    out_other = swap(out_weight)
    pointwise_other = swap(pointwise)
    depthwise_other = swap(depthwise)
    mid_gain_other = swap(mid_gain)
    pointwise_out_other = swap(pointwise_out)
    lo_own, hi_own, lo_pair, hi_pair = bounds(meta, counts, utt_valid, rows)
    pair, out_other, pointwise_other, depthwise_other, mid_gain_other, pointwise_out_other = (
        lax.optimization_barrier(
            (pair, out_other, pointwise_other, depthwise_other, mid_gain_other,
             pointwise_out_other)
        )
    )

    pair_context = attend(column.reshape(1), pair, pair, keep, far_pair, lo_pair, hi_pair)
    pair_context = exchange(pair_context)
    context = attend((1 - column).reshape(1), query, keep, pair, far_own, lo_own, hi_own)
    contexts = (context, pair_context, swap(context), swap(pair_context))
    glu, edge, mid_keep, mid_send = gated(
        meta, contexts, frames, other, out_weight, out_other, conv_gain,
        pointwise, pointwise_other, lo_own, hi_own,
    )
    edges = [(2 * i, 2 * (i - 1) + 1) for i in range(1, blocks)]
    edges += [(2 * i + 1, 2 * (i + 1)) for i in range(blocks - 1)]
    edge = lax.ppermute(edge, ("tm", "head"), edges)
    mid_other = swap(mid_send)
    act = convolve(
        meta, glu, edge, lo_own, hi_own, depthwise, depthwise_other, mid_gain, mid_gain_other
    )
    act_other = swap(act)
    return finish(
        meta, act, act_other, mid_keep, mid_other, pointwise_out, pointwise_out_other
    )


def solution(mesh):
    in_specs = (
        P(("grp", "tm"), "head"),
        P(("grp", "tm")),
        P("grp"),
        P(),
        P(None, None, "head"),
        P("head", None),
        P(),
        P(None, None, "head"),
        P(None, "head"),
        P("head"),
        P("head", None),
    )
    out_specs = P(("grp", "tm"), "head")
    return jax.shard_map(
        functools.partial(local, mesh.shape["tm"]),
        mesh=mesh,
        in_specs=in_specs,
        out_specs=out_specs,
        check_vma=False,
    )
```

```python
import functools
import math

import jax
import jax.numpy as jnp
from jax import lax
from jax.experimental import pallas as pl
from jax.experimental.pallas import tpu as pltpu
from jax.sharding import PartitionSpec as P

HEAD_DIM = 64
CONV_CH = 512
KERNEL = 31
WIN = 512
EDGE = 16
NEG = -1e30
EXP_SCALE = HEAD_DIM ** (-0.5) * math.log2(math.e)
F32 = jnp.float32
BF16 = jnp.bfloat16
VMEM_LIMIT = 16 * 1024 * 1024


def dot(a, b):
    return jnp.dot(a, b, preferred_element_type=F32)


def normalize_halves(own, other, gain_own, gain_other):
    width = own.shape[1] + other.shape[1]
    mean = (
        jnp.sum(own, axis=1, keepdims=True) + jnp.sum(other, axis=1, keepdims=True)
    ) / width
    own = own - mean
    other = other - mean
    spread = (
        jnp.sum(own * own, axis=1, keepdims=True) + jnp.sum(other * other, axis=1, keepdims=True)
    ) / width
    scale = lax.rsqrt(spread + 1e-05)
    return (own * scale * gain_own).astype(BF16), (other * scale * gain_other).astype(BF16)


def qkv_kernel(
    meta, own_ref, other_ref, gain_ref, w_ref, keep_ref, query_ref, send_ref, pass_ref
):
    h = meta[0]
    first = meta[1] == 0
    rows = own_ref.shape[0]
    tile = 256
    for at in range(0, rows, tile):
        here = slice(at, at + tile)
        n_own, n_other = normalize_halves(
            own_ref[here, :].astype(F32), other_ref[here, :].astype(F32),
            gain_ref[h], gain_ref[1 - h],
        )
        for slot, part in enumerate((1, 2, 0)):
            value = (dot(n_own, w_ref[part, h]) + dot(n_other, w_ref[part, 1 - h])).astype(BF16)
            sub = value.shape[1] // 2
            cols = slice(slot * sub, slot * sub + sub)
            keep = jnp.where(first, value[:, :sub], value[:, sub:])
            send = jnp.where(first, value[:, sub:], value[:, :sub])
            send_ref[here, cols] = send
            if slot < 2:
                keep_ref[here, cols] = keep
                pass_ref[here, cols] = send
            else:
                query_ref[here, :] = keep


def project(meta, frames, other, gain, weight):
    rows, half = frames.shape
    width = weight.shape[2]
    vmem = pl.BlockSpec(memory_space=pltpu.VMEM)
    return pl.pallas_call(
        qkv_kernel,
        in_specs=[pl.BlockSpec(memory_space=pltpu.SMEM)] + [vmem] * 4,
        out_specs=[vmem] * 4,
        out_shape=[
            jax.ShapeDtypeStruct((rows, width), BF16),
            jax.ShapeDtypeStruct((rows, width // 2), BF16),
            jax.ShapeDtypeStruct((rows, 3 * width // 2), BF16),
            jax.ShapeDtypeStruct((rows, width), BF16),
        ],
        compiler_params=pltpu.CompilerParams(vmem_limit_bytes=VMEM_LIMIT),
        name="project",
    )(meta, frames, other, gain.reshape(2, 1, half),
      weight.transpose(1, 0, 2).reshape(3, 2, half, width))


def bounds_kernel(meta, counts, valid, own_ref, pair_ref):
    utts = valid.shape[1]
    rows = own_ref.shape[0]
    square = (utts, utts)
    sub = lax.broadcasted_iota(jnp.int32, square, 0)
    lane = lax.broadcasted_iota(jnp.int32, square, 1)
    total = jnp.sum(counts[...].astype(F32), axis=0, keepdims=True)
    limit = jnp.broadcast_to(jnp.minimum(total, valid[...].astype(F32)), square)
    total = jnp.broadcast_to(total, square)
    start = jnp.sum(jnp.where(lane < sub, total, 0.0), axis=1, keepdims=True)
    stop = start + jnp.sum(jnp.where(lane == sub, limit, 0.0), axis=1, keepdims=True)
    at = lax.broadcasted_iota(jnp.int32, (utts, rows), 1).astype(F32)
    for slot, ref in enumerate((own_ref, pair_ref)):
        origin = meta[2 + slot].astype(F32)
        lo = start - origin
        hi = stop - origin
        inside = (at >= lo) & (at < hi)
        low = jnp.sum(jnp.where(inside, lo, 0.0), axis=0, keepdims=True)
        high = jnp.sum(jnp.where(inside, hi, 0.0), axis=0, keepdims=True)
        both = jnp.concatenate([low, high, jnp.zeros((126, rows), F32)], axis=0)
        ref[...] = both.T.astype(jnp.int32)


def bounds(meta, counts, valid, rows):
    vmem = pl.BlockSpec(memory_space=pltpu.VMEM)
    return pl.pallas_call(
        bounds_kernel,
        in_specs=[pl.BlockSpec(memory_space=pltpu.SMEM), vmem, vmem],
        out_specs=[vmem] * 2,
        out_shape=[jax.ShapeDtypeStruct((rows, 128), jnp.int32)] * 2,
        compiler_params=pltpu.CompilerParams(vmem_limit_bytes=VMEM_LIMIT),
        name="bounds",
    )(meta, counts, valid.reshape(1, -1))


def attend_kernel(a_high, query, center, side_a, side_b, run_ref, out_ref):
    rows = center.shape[0]
    width = center.shape[1] // 2 if query.shape[1] < center.shape[1] else center.shape[1] // 3
    q_cols = slice(query.shape[1] - width, query.shape[1])
    tile = rows // 2
    lane = lax.broadcasted_iota(jnp.int32, (tile, width), 1)

    def run(low_ref, high_ref):
        for block in range(2):
            at = block * tile
            pieces = (
                ((low_ref, 0, rows, -rows), (center, 0, rows, 0), (high_ref, 0, tile, rows))
                if block == 0
                else ((low_ref, tile, tile, -rows), (center, 0, rows, 0), (high_ref, 0, rows, rows))
            )
            position = lax.broadcasted_iota(jnp.int32, (tile, 1), 0) + at
            lo = run_ref[at : at + tile, 0:1]
            hi = run_ref[at : at + tile, 1:2]
            near_lo = jnp.maximum(lo, position - WIN)
            near_hi = jnp.minimum(hi, position + (WIN + 1))
            biases = []
            for _, first, size, origin in pieces:
                u = lax.broadcasted_iota(jnp.int32, (tile, size), 1) + (origin + first)
                biases.append(jnp.where((u >= near_lo) & (u < near_hi), 0.0, NEG))
            q = query[at : at + tile, q_cols]
            outs = []
            for sub in range(2):
                q_sub = jnp.where((lane >= HEAD_DIM) == (sub == 1), q, jnp.zeros_like(q))
                scores = []
                for (ref, first, size, _), bias in zip(pieces, biases):
                    s = lax.dot_general(
                        q_sub, ref[first : first + size, :width], (((1,), (1,)), ((), ())),
                        preferred_element_type=F32,
                    )
                    scores.append(s + bias)
                peak = functools.reduce(
                    jnp.maximum, [jnp.max(s, axis=1, keepdims=True) for s in scores]
                )
                total = jnp.zeros((tile, 1), F32)
                context = jnp.zeros((tile, width), F32)
                for (ref, first, size, _), s in zip(pieces, scores):
                    expw = jnp.exp2((s - peak) * EXP_SCALE)
                    total = total + jnp.sum(expw, axis=1, keepdims=True)
                    context = context + dot(
                        expw.astype(BF16), ref[first : first + size, width : 2 * width]
                    )
                outs.append(context / jnp.maximum(total, 1.0))
            joined = jnp.where(lane >= HEAD_DIM, outs[1], outs[0])
            out_ref[at : at + tile, :] = jnp.where(hi > lo, joined, 0.0).astype(BF16)

    @pl.when(a_high[0] == 1)
    def _():
        run(side_b, side_a)

    @pl.when(a_high[0] == 0)
    def _():
        run(side_a, side_b)


def attend(a_high, query, center, side_a, side_b, runs):
    rows, width = side_b.shape[0], side_b.shape[1] // 2
    vmem = pl.BlockSpec(memory_space=pltpu.VMEM)
    return pl.pallas_call(
        attend_kernel,
        in_specs=[pl.BlockSpec(memory_space=pltpu.SMEM)] + [vmem] * 5,
        out_specs=vmem,
        out_shape=jax.ShapeDtypeStruct((rows, width), BF16),
        compiler_params=pltpu.CompilerParams(vmem_limit_bytes=VMEM_LIMIT),
        name="attend",
    )(a_high, query, center, side_a, side_b, runs)


def gate_kernel(
    meta,
    mine_own, pair_own, mine_other, pair_other,
    x_own, x_other,
    out_own, out_other,
    gain_ref,
    in_own, in_other,
    run_ref,
    glu_ref, edge_ref, mid_keep, mid_send,
):
    h = meta[0]
    first = meta[1] == 0
    half = x_own.shape[1]
    rows = glu_ref.shape[0]
    here = pl.ds(pl.multiple_of(h * (rows - 2 * EDGE), EDGE), rows)

    def joined(mine, pair):
        mine = mine[here, :]
        pair = pair[here, :]
        return jnp.concatenate(
            [jnp.where(first, mine, pair), jnp.where(first, pair, mine)], axis=1
        )

    c_own = joined(mine_own, pair_own)
    c_other = joined(mine_other, pair_other)
    own_cols = pl.ds(pl.multiple_of(h * half, half), half)
    other_cols = pl.ds(pl.multiple_of((1 - h) * half, half), half)

    def mid(cols, x_ref):
        first = dot(c_own, out_own[:, cols]).astype(BF16).astype(F32)
        second = dot(c_other, out_other[:, cols]).astype(BF16).astype(F32)
        return (x_ref[here, :].astype(F32) + (first + second)).astype(BF16)

    m_own = mid(own_cols, x_own)
    m_other = mid(other_cols, x_other)
    keep = rows - EDGE

    @pl.when(h == 0)
    def _():
        mid_keep[...] = m_own[:keep]
        mid_send[...] = m_other[:keep]

    @pl.when(h == 1)
    def _():
        mid_keep[...] = m_own[EDGE:]
        mid_send[...] = m_other[EDGE:]

    n_own, n_other = normalize_halves(
        m_own.astype(F32), m_other.astype(F32), gain_ref[h], gain_ref[1 - h]
    )
    run = run_ref[here, :]
    valid = run[:, 1:2] > run[:, 0:1]
    glus = []
    for w_ref in (in_own, in_other):
        value = dot(n_own, w_ref[0, own_cols, :]) + dot(n_other, w_ref[0, other_cols, :])
        gate = dot(n_own, w_ref[1, own_cols, :]) + dot(n_other, w_ref[1, other_cols, :])
        glu = value / (1.0 + jnp.exp(-gate))
        glus.append(jnp.where(valid, glu, 0.0).astype(BF16))
    chan = glus[0].shape[1]
    glu_ref[:, :chan] = glus[0]
    glu_ref[:, chan:] = glus[1]

    @pl.when(h == 0)
    def _():
        edge_ref[:, :chan] = glus[1][:EDGE]
        edge_ref[:, chan:] = glus[0][:EDGE]

    @pl.when(h == 1)
    def _():
        edge_ref[:, :chan] = glus[1][rows - EDGE :]
        edge_ref[:, chan:] = glus[0][rows - EDGE :]


def gated(meta, contexts, x_own, x_other, out_own, out_other, gain, in_own, in_other, runs):
    rows = x_own.shape[0] // 2 + EDGE
    half = x_own.shape[1]
    chan = in_own.shape[2]
    vmem = pl.BlockSpec(memory_space=pltpu.VMEM)
    return pl.pallas_call(
        gate_kernel,
        in_specs=[pl.BlockSpec(memory_space=pltpu.SMEM)] + [vmem] * 12,
        out_specs=[vmem] * 4,
        out_shape=[
            jax.ShapeDtypeStruct((rows, 2 * chan), BF16),
            jax.ShapeDtypeStruct((EDGE, 2 * chan), BF16),
            jax.ShapeDtypeStruct((rows - EDGE, half), BF16),
            jax.ShapeDtypeStruct((rows - EDGE, half), BF16),
        ],
        compiler_params=pltpu.CompilerParams(vmem_limit_bytes=VMEM_LIMIT),
        name="gated",
    )(meta, *contexts, x_own, x_other, out_own, out_other,
      gain.reshape(2, 1, half), in_own, in_other, runs)


def conv_kernel(meta, glu_ref, edge_ref, run_ref, dw_own, dw_other, act_ref, ext):
    h = meta[0]
    rows, width = act_ref.shape
    chan = width // 2
    got = glu_ref.shape[0]
    ext[pl.ds(pl.multiple_of((1 - h) * EDGE, EDGE), got), :] = glu_ref[...].astype(F32)
    ext[pl.ds(pl.multiple_of(h * got, EDGE), EDGE), :] = edge_ref[...].astype(F32)
    first = pl.multiple_of(h * rows, rows)
    at = lax.broadcasted_iota(jnp.int32, (rows, 128), 0) + first
    run = run_ref[pl.ds(first, rows), :]
    low = jnp.broadcast_to(run[:, 0:1], (rows, 128)) - at
    high = jnp.broadcast_to(run[:, 1:2], (rows, 128)) - at
    reach = KERNEL // 2
    step = 64
    for base in range(0, rows, step):
        low_b = low[base : base + step]
        high_b = high[base : base + step]
        sums = jnp.zeros((step, 128), F32)
        squares = jnp.zeros((step, 128), F32)
        results = []
        for col in range(0, width, 128):
            dw_ref, c = (dw_own, col) if col < chan else (dw_other, col - chan)
            total = jnp.zeros((step, 128), F32)
            for tap in range(KERNEL):
                shift = tap - reach
                row = base + EDGE + shift
                piece = ext[row : row + step, col : col + 128]
                same = (low_b <= shift) & (high_b > shift)
                total = total + jnp.where(same, piece, 0.0) * dw_ref[tap : tap + 1, c : c + 128]
            sums = sums + total
            squares = squares + total * total
            results.append(total)
        mean = jnp.sum(sums, axis=1, keepdims=True) / CONV_CH
        square = jnp.sum(squares, axis=1, keepdims=True) / CONV_CH
        scale = lax.rsqrt(square - mean * mean + 1e-05)
        for col, total in zip(range(0, width, 128), results):
            dw_ref, c = (dw_own, col) if col < chan else (dw_other, col - chan)
            y = (total - mean) * scale * dw_ref[KERNEL : KERNEL + 1, c : c + 128]
            act_ref[base : base + step, col : col + 128] = (y / (1.0 + jnp.exp(-y))).astype(BF16)


def convolve(meta, glu, edge, runs, taps_own, taps_other):
    rows = glu.shape[0] - EDGE
    width = glu.shape[1]
    vmem = pl.BlockSpec(memory_space=pltpu.VMEM)
    return pl.pallas_call(
        conv_kernel,
        in_specs=[pl.BlockSpec(memory_space=pltpu.SMEM)] + [vmem] * 5,
        out_specs=vmem,
        out_shape=jax.ShapeDtypeStruct((rows, width), BF16),
        scratch_shapes=[pltpu.VMEM((rows + 2 * EDGE, width), F32)],
        compiler_params=pltpu.CompilerParams(vmem_limit_bytes=VMEM_LIMIT),
        name="convolve",
    )(meta, glu, edge, runs, taps_own, taps_other)


def finish_kernel(meta, act_own, act_other, mid_own, mid_other, w_own, w_other, out_ref):
    h = meta[0]
    rows, chan2 = act_own.shape
    chan = chan2 // 2
    half = out_ref.shape[1]
    cols = pl.ds(pl.multiple_of(h * half, half), half)
    w_a = w_own[:, cols]
    w_b = w_other[:, cols]

    def rows_of(act, mid, flip):
        first = dot(act[:, :chan], w_b if flip else w_a).astype(BF16).astype(F32)
        second = dot(act[:, chan:], w_a if flip else w_b).astype(BF16).astype(F32)
        return (mid[...].astype(F32) + (first + second)).astype(BF16)

    out_ref[pl.ds(pl.multiple_of(h * rows, rows), rows), :] = rows_of(act_own, mid_own, False)
    out_ref[pl.ds(pl.multiple_of((1 - h) * rows, rows), rows), :] = rows_of(
        act_other, mid_other, True
    )


def finish(meta, act_own, act_other, mid_own, mid_other, w_own, w_other):
    rows, half = mid_own.shape
    vmem = pl.BlockSpec(memory_space=pltpu.VMEM)
    return pl.pallas_call(
        finish_kernel,
        in_specs=[pl.BlockSpec(memory_space=pltpu.SMEM)] + [vmem] * 6,
        out_specs=vmem,
        out_shape=jax.ShapeDtypeStruct((2 * rows, half), BF16),
        compiler_params=pltpu.CompilerParams(vmem_limit_bytes=VMEM_LIMIT),
        name="finish",
    )(meta, act_own, act_other, mid_own, mid_other, w_own, w_other)


def local(
    blocks,
    frames,
    segment_ids,
    utt_valid,
    attn_gain,
    qkv_weight,
    out_weight,
    conv_gain,
    pointwise_in,
    depthwise,
    mid_gain,
    pointwise_out,
):
    rows = frames.shape[0]

    def swap(value):
        return lax.ppermute(value, "head", [(0, 1), (1, 0)])

    def shift(value, step):
        pairs = [(i, i - step if i % 2 == 0 else i + step) for i in range(blocks)]
        return lax.ppermute(value, "tm", [p for p in pairs if 0 <= p[1] < blocks])

    def exchange(value):
        return lax.ppermute(value, "tm", [(i, i ^ 1) for i in range(blocks)])

    block = lax.axis_index("tm").astype(jnp.int32)
    column = block % 2
    meta = jnp.stack([
        lax.axis_index("head").astype(jnp.int32),
        column,
        block * rows,
        (block + 1 - 2 * column) * rows,
    ])
    other = swap(frames)
    keep, query, send, passed = project(meta, frames, other, attn_gain, qkv_weight)
    far_own = shift(passed, 1)
    pair = exchange(send)
    far_pair = shift(keep, 2)

    segment_ids, _ = lax.optimization_barrier((segment_ids, passed))
    ids = jnp.arange(utt_valid.shape[0], dtype=jnp.int32)
    counts = jnp.sum((segment_ids[None, :] == ids[:, None]).astype(jnp.int32), axis=1)
    counts = lax.all_to_all(
        jnp.broadcast_to(counts[None, :], (blocks, counts.shape[0])), "tm", 0, 0
    )
    pointwise = pointwise_in.transpose(1, 0, 2)
    taps = jnp.concatenate([depthwise, mid_gain[None, :]], axis=0)
    out_weight, pointwise, taps, pointwise_out, _ = lax.optimization_barrier(
        (out_weight, pointwise, taps, pointwise_out, keep)
    )
    pointwise_other = swap(pointwise)
    out_other = swap(out_weight)
    pointwise_out_other = swap(pointwise_out)
    taps_other = swap(taps)
    runs, pair_runs = bounds(meta, counts, utt_valid, rows)

    pair_context = attend(column.reshape(1), pair, pair, keep, far_pair, pair_runs)
    pair_context = exchange(pair_context)
    context = attend((1 - column).reshape(1), query, keep, pair, far_own, runs)
    contexts = (context, pair_context, swap(context), swap(pair_context))
    glu, edge, mid_keep, mid_send = gated(
        meta, contexts, frames, other, out_weight, out_other, conv_gain,
        pointwise, pointwise_other, runs,
    )
    edges = [(2 * i, 2 * (i - 1) + 1) for i in range(1, blocks)]
    edges += [(2 * i + 1, 2 * (i + 1)) for i in range(blocks - 1)]
    edge = lax.ppermute(edge, ("tm", "head"), edges)
    mid_other = swap(mid_send)
    act = convolve(meta, glu, edge, runs, taps, taps_other)
    act_other = swap(act)
    return finish(
        meta, act, act_other, mid_keep, mid_other, pointwise_out, pointwise_out_other
    )


def solution(mesh):
    in_specs = (
        P(("grp", "tm"), "head"),
        P(("grp", "tm")),
        P("grp"),
        P(),
        P(None, None, "head"),
        P("head", None),
        P(),
        P(None, None, "head"),
        P(None, "head"),
        P("head"),
        P("head", None),
    )
    out_specs = P(("grp", "tm"), "head")
    return jax.shard_map(
        functools.partial(local, mesh.shape["tm"]),
        mesh=mesh,
        in_specs=in_specs,
        out_specs=out_specs,
        check_vma=False,
    )
```

```python
import functools
import math

import jax
import jax.numpy as jnp
from jax import lax
from jax.experimental import pallas as pl
from jax.experimental.pallas import tpu as pltpu
from jax.sharding import PartitionSpec as P

HEAD_DIM = 64
CONV_CH = 512
KERNEL = 31
WIN = 512
EDGE = 16
SENT = 64
NEG = -1e30
EXP_SCALE = HEAD_DIM ** (-0.5) * math.log2(math.e)
F32 = jnp.float32
BF16 = jnp.bfloat16
VMEM_LIMIT = 16 * 1024 * 1024


def weight(microseconds):
    return pl.CostEstimate(
        flops=int(microseconds * 1.15e9), bytes_accessed=0, transcendentals=0
    )


def dot(a, b):
    return jnp.dot(a, b, preferred_element_type=F32)


def normalize_halves(own, other, gain_own, gain_other):
    width = own.shape[1] + other.shape[1]
    mean = (
        jnp.sum(own, axis=1, keepdims=True) + jnp.sum(other, axis=1, keepdims=True)
    ) / width
    own = own - mean
    other = other - mean
    spread = (
        jnp.sum(own * own, axis=1, keepdims=True) + jnp.sum(other * other, axis=1, keepdims=True)
    ) / width
    scale = lax.rsqrt(spread + 1e-05)
    return (own * scale * gain_own).astype(BF16), (other * scale * gain_other).astype(BF16)


def qkv_kernel(
    meta, own_ref, other_ref, gain_ref, w_ref, keep_ref, query_ref, send_ref, pass_ref
):
    h = meta[0]
    first = meta[1] == 0
    rows = own_ref.shape[0]
    tile = 256
    for at in range(0, rows, tile):
        here = slice(at, at + tile)
        n_own, n_other = normalize_halves(
            own_ref[here, :].astype(F32), other_ref[here, :].astype(F32),
            gain_ref[h], gain_ref[1 - h],
        )
        for slot, part in enumerate((1, 2, 0)):
            value = (dot(n_own, w_ref[part, h]) + dot(n_other, w_ref[part, 1 - h])).astype(BF16)
            sub = value.shape[1] // 2
            cols = slice(slot * sub, slot * sub + sub)
            keep = jnp.where(first, value[:, :sub], value[:, sub:])
            send = jnp.where(first, value[:, sub:], value[:, :sub])
            send_ref[here, cols] = send
            if slot < 2:
                keep_ref[here, cols] = keep
                pass_ref[here, cols] = send
            else:
                query_ref[here, :] = keep


def project(meta, frames, other, gain, qkv):
    rows, half = frames.shape
    width = qkv.shape[2]
    vmem = pl.BlockSpec(memory_space=pltpu.VMEM)
    return pl.pallas_call(
        qkv_kernel,
        in_specs=[pl.BlockSpec(memory_space=pltpu.SMEM)] + [vmem] * 4,
        out_specs=[vmem] * 4,
        out_shape=[
            jax.ShapeDtypeStruct((rows, width), BF16),
            jax.ShapeDtypeStruct((rows, width // 2), BF16),
            jax.ShapeDtypeStruct((rows, 3 * width // 2), BF16),
            jax.ShapeDtypeStruct((rows, width), BF16),
        ],
        compiler_params=pltpu.CompilerParams(vmem_limit_bytes=VMEM_LIMIT),
        cost_estimate=weight(3),
        name="project",
    )(meta, frames, other, gain.reshape(2, 1, half),
      qkv.transpose(1, 0, 2).reshape(3, 2, half, width))


def bounds_kernel(meta, counts, valid, own_ref, pair_ref):
    utts = valid.shape[1]
    rows = own_ref.shape[0]
    square = (utts, utts)
    sub = lax.broadcasted_iota(jnp.int32, square, 0)
    lane = lax.broadcasted_iota(jnp.int32, square, 1)
    total = jnp.sum(counts[...].astype(F32), axis=0, keepdims=True)
    limit = jnp.broadcast_to(jnp.minimum(total, valid[...].astype(F32)), square)
    total = jnp.broadcast_to(total, square)
    start = jnp.sum(jnp.where(lane < sub, total, 0.0), axis=1, keepdims=True)
    stop = start + jnp.sum(jnp.where(lane == sub, limit, 0.0), axis=1, keepdims=True)
    at = lax.broadcasted_iota(jnp.int32, (utts, rows), 1).astype(F32)
    for slot, ref in enumerate((own_ref, pair_ref)):
        origin = meta[2 + slot].astype(F32)
        lo = start - origin
        hi = stop - origin
        inside = (at >= lo) & (at < hi)
        low = jnp.sum(jnp.where(inside, lo, 0.0), axis=0, keepdims=True)
        high = jnp.sum(jnp.where(inside, hi, 0.0), axis=0, keepdims=True)
        both = jnp.concatenate([low, high, jnp.zeros((126, rows), F32)], axis=0)
        ref[...] = both.T.astype(jnp.int32)


def bounds(meta, counts, valid, rows):
    vmem = pl.BlockSpec(memory_space=pltpu.VMEM)
    return pl.pallas_call(
        bounds_kernel,
        in_specs=[pl.BlockSpec(memory_space=pltpu.SMEM), vmem, vmem],
        out_specs=[vmem] * 2,
        out_shape=[jax.ShapeDtypeStruct((rows, 128), jnp.int32)] * 2,
        compiler_params=pltpu.CompilerParams(vmem_limit_bytes=VMEM_LIMIT),
        cost_estimate=weight(1),
        name="bounds",
    )(meta, counts, valid.reshape(1, -1))


def attend_kernel(a_high, query, center, side_a, side_b, run_ref, out_ref):
    rows = center.shape[0]
    width = center.shape[1] // 2 if query.shape[1] < center.shape[1] else center.shape[1] // 3
    q_cols = slice(query.shape[1] - width, query.shape[1])
    tile = rows // 2
    lane = lax.broadcasted_iota(jnp.int32, (tile, width), 1)

    def run(low_ref, high_ref):
        for block in range(2):
            at = block * tile
            pieces = (
                ((low_ref, 0, rows, -rows), (center, 0, rows, 0), (high_ref, 0, tile, rows))
                if block == 0
                else ((low_ref, tile, tile, -rows), (center, 0, rows, 0), (high_ref, 0, rows, rows))
            )
            position = lax.broadcasted_iota(jnp.int32, (tile, 1), 0) + at
            lo = run_ref[at : at + tile, 0:1]
            hi = run_ref[at : at + tile, 1:2]
            near_lo = jnp.maximum(lo, position - WIN)
            near_hi = jnp.minimum(hi, position + (WIN + 1))
            biases = []
            for _, first, size, origin in pieces:
                u = lax.broadcasted_iota(jnp.int32, (tile, size), 1) + (origin + first)
                biases.append(jnp.where((u >= near_lo) & (u < near_hi), 0.0, NEG))
            q = query[at : at + tile, q_cols]
            outs = []
            for sub in range(2):
                q_sub = jnp.where((lane >= HEAD_DIM) == (sub == 1), q, jnp.zeros_like(q))
                scores = []
                for (ref, first, size, _), bias in zip(pieces, biases):
                    s = lax.dot_general(
                        q_sub, ref[first : first + size, :width], (((1,), (1,)), ((), ())),
                        preferred_element_type=F32,
                    )
                    scores.append(s + bias)
                peak = functools.reduce(
                    jnp.maximum, [jnp.max(s, axis=1, keepdims=True) for s in scores]
                )
                total = jnp.zeros((tile, 1), F32)
                context = jnp.zeros((tile, width), F32)
                for (ref, first, size, _), s in zip(pieces, scores):
                    expw = jnp.exp2((s - peak) * EXP_SCALE)
                    total = total + jnp.sum(expw, axis=1, keepdims=True)
                    context = context + dot(
                        expw.astype(BF16), ref[first : first + size, width : 2 * width]
                    )
                outs.append(context / jnp.maximum(total, 1.0))
            joined = jnp.where(lane >= HEAD_DIM, outs[1], outs[0])
            out_ref[at : at + tile, :] = jnp.where(hi > lo, joined, 0.0).astype(BF16)

    @pl.when(a_high[0] == 1)
    def _():
        run(side_b, side_a)

    @pl.when(a_high[0] == 0)
    def _():
        run(side_a, side_b)


def attend(a_high, query, center, side_a, side_b, runs):
    rows, width = side_b.shape[0], side_b.shape[1] // 2
    vmem = pl.BlockSpec(memory_space=pltpu.VMEM)
    return pl.pallas_call(
        attend_kernel,
        in_specs=[pl.BlockSpec(memory_space=pltpu.SMEM)] + [vmem] * 5,
        out_specs=vmem,
        out_shape=jax.ShapeDtypeStruct((rows, width), BF16),
        compiler_params=pltpu.CompilerParams(vmem_limit_bytes=VMEM_LIMIT),
        cost_estimate=weight(3),
        name="attend",
    )(a_high, query, center, side_a, side_b, runs)


def gate_kernel(
    meta,
    mine_own, pair_own, mine_other, pair_other,
    x_own, x_other,
    out_own, out_other,
    gain_ref,
    in_own, in_other,
    run_ref,
    glu_ref, edge_ref, mid_keep, mid_send,
):
    h = meta[0]
    first = meta[1] == 0
    half = x_own.shape[1]
    rows = glu_ref.shape[0]
    here = pl.ds(pl.multiple_of(h * (rows - 2 * EDGE), EDGE), rows)

    def joined(mine, pair):
        mine = mine[here, :]
        pair = pair[here, :]
        return jnp.concatenate(
            [jnp.where(first, mine, pair), jnp.where(first, pair, mine)], axis=1
        )

    c_own = joined(mine_own, pair_own)
    c_other = joined(mine_other, pair_other)
    own_cols = pl.ds(pl.multiple_of(h * half, half), half)
    other_cols = pl.ds(pl.multiple_of((1 - h) * half, half), half)

    def mid(cols, x_ref):
        first = dot(c_own, out_own[:, cols]).astype(BF16).astype(F32)
        second = dot(c_other, out_other[:, cols]).astype(BF16).astype(F32)
        return (x_ref[here, :].astype(F32) + (first + second)).astype(BF16)

    m_own = mid(own_cols, x_own)
    m_other = mid(other_cols, x_other)
    keep = rows - EDGE

    @pl.when(h == 0)
    def _():
        mid_keep[...] = m_own[:keep]
        mid_send[...] = m_other[:keep]

    @pl.when(h == 1)
    def _():
        mid_keep[...] = m_own[EDGE:]
        mid_send[...] = m_other[EDGE:]

    n_own, n_other = normalize_halves(
        m_own.astype(F32), m_other.astype(F32), gain_ref[h], gain_ref[1 - h]
    )
    run = run_ref[here, :]
    valid = run[:, 1:2] > run[:, 0:1]
    glus = []
    for w_ref in (in_own, in_other):
        value = dot(n_own, w_ref[0, own_cols, :]) + dot(n_other, w_ref[0, other_cols, :])
        gate = dot(n_own, w_ref[1, own_cols, :]) + dot(n_other, w_ref[1, other_cols, :])
        glu = value / (1.0 + jnp.exp(-gate))
        glus.append(jnp.where(valid, glu, 0.0).astype(BF16))
    chan = glus[0].shape[1]
    glu_ref[:, :chan] = glus[0]
    glu_ref[:, chan:] = glus[1]

    @pl.when(h == 0)
    def _():
        edge_ref[:, :chan] = glus[1][:SENT]
        edge_ref[:, chan:] = glus[0][:SENT]

    @pl.when(h == 1)
    def _():
        edge_ref[:, :chan] = glus[1][rows - SENT :]
        edge_ref[:, chan:] = glus[0][rows - SENT :]


def gated(meta, contexts, x_own, x_other, out_own, out_other, gain, in_own, in_other, runs):
    rows = x_own.shape[0] // 2 + EDGE
    half = x_own.shape[1]
    chan = in_own.shape[2]
    vmem = pl.BlockSpec(memory_space=pltpu.VMEM)
    return pl.pallas_call(
        gate_kernel,
        in_specs=[pl.BlockSpec(memory_space=pltpu.SMEM)] + [vmem] * 12,
        out_specs=[vmem] * 4,
        out_shape=[
            jax.ShapeDtypeStruct((rows, 2 * chan), BF16),
            jax.ShapeDtypeStruct((SENT, 2 * chan), BF16),
            jax.ShapeDtypeStruct((rows - EDGE, half), BF16),
            jax.ShapeDtypeStruct((rows - EDGE, half), BF16),
        ],
        compiler_params=pltpu.CompilerParams(vmem_limit_bytes=VMEM_LIMIT),
        cost_estimate=weight(3),
        name="gated",
    )(meta, *contexts, x_own, x_other, out_own, out_other,
      gain.reshape(2, 1, half), in_own, in_other, runs)


def conv_rows(shifted, low, high, taps, out_ref, rows):
    width = out_ref.shape[1]
    chan = width // 2
    reach = KERNEL // 2
    step = min(32, rows)
    cols = range(0, width, 128)
    weights = [
        [
            (taps[0] if col < chan else taps[1])[tap : tap + 1, col % chan : col % chan + 128]
            for col in cols
        ]
        for tap in range(KERNEL + 1)
    ]
    for base in range(0, rows, step):
        totals = [jnp.zeros((step, 128), F32) for _ in cols]
        for tap in range(KERNEL):
            shift = tap - reach
            same = (low[base : base + step] <= shift) & (high[base : base + step] > shift)
            row = base + EDGE + shift
            first = row - row % 8
            for index, col in enumerate(cols):
                piece = shifted[row % 8, first : first + step, col : col + 128]
                totals[index] = totals[index] + jnp.where(same, piece, 0.0) * weights[tap][index]
        mean = jnp.sum(sum(totals), axis=1, keepdims=True) / CONV_CH
        square = jnp.sum(sum(t * t for t in totals), axis=1, keepdims=True) / CONV_CH
        scale = lax.rsqrt(square - mean * mean + 1e-05)
        for index, col in enumerate(cols):
            y = (totals[index] - mean) * scale * weights[KERNEL][index]
            out_ref[base : base + step, col : col + 128] = (y / (1.0 + jnp.exp(-y))).astype(BF16)


def run_offsets(run_ref, first, rows):
    run = run_ref[pl.ds(first, rows), :]
    at = lax.broadcasted_iota(jnp.int32, (rows, 128), 0) + first
    low = jnp.broadcast_to(run[:, 0:1], (rows, 128)) - at
    high = jnp.broadcast_to(run[:, 1:2], (rows, 128)) - at
    return low, high


def conv_kernel(meta, glu_ref, run_ref, taps_own, taps_other, act_ref, ext, shifted):
    h = meta[0]
    rows, width = act_ref.shape
    got = glu_ref.shape[0]
    ext[pl.ds(pl.multiple_of(h * got, EDGE), EDGE), :] = jnp.zeros((EDGE, width), F32)
    ext[pl.ds(pl.multiple_of((1 - h) * EDGE, EDGE), got), :] = glu_ref[...].astype(F32)
    size = shifted.shape[1]
    for s in range(8):
        shifted[s] = ext[s : s + size, :]
    low, high = run_offsets(run_ref, pl.multiple_of(h * rows, rows), rows)
    conv_rows(shifted, low, high, (taps_own, taps_other), act_ref, rows)


def convolve(meta, glu, runs, taps_own, taps_other):
    rows = glu.shape[0] - EDGE
    width = glu.shape[1]
    vmem = pl.BlockSpec(memory_space=pltpu.VMEM)
    return pl.pallas_call(
        conv_kernel,
        in_specs=[pl.BlockSpec(memory_space=pltpu.SMEM)] + [vmem] * 4,
        out_specs=vmem,
        out_shape=jax.ShapeDtypeStruct((rows, width), BF16),
        scratch_shapes=[
            pltpu.VMEM((rows + 2 * EDGE, width), F32),
            pltpu.VMEM((8, rows + 2 * EDGE - 8, width), F32),
        ],
        compiler_params=pltpu.CompilerParams(vmem_limit_bytes=VMEM_LIMIT),
        cost_estimate=weight(3),
        name="convolve",
    )(meta, glu, runs, taps_own, taps_other)


def rim_kernel(meta, glu_ref, edge_ref, run_ref, taps_own, taps_other, act_ref, ext, shifted):
    h = meta[0]
    got = glu_ref.shape[0]
    near = 2 * EDGE
    ext[pl.ds(pl.multiple_of(h * near, EDGE), EDGE), :] = edge_ref[
        pl.ds(pl.multiple_of((1 - h) * (SENT - EDGE), EDGE), EDGE), :
    ].astype(F32)
    ext[pl.ds(pl.multiple_of((1 - h) * EDGE, EDGE), near), :] = glu_ref[
        pl.ds(pl.multiple_of(h * (got - near), EDGE), near), :
    ].astype(F32)
    size = shifted.shape[1]
    for s in range(8):
        shifted[s] = ext[s : s + size, :]
    first = pl.multiple_of(h * (run_ref.shape[0] - EDGE), EDGE)
    low, high = run_offsets(run_ref, first, EDGE)
    conv_rows(shifted, low, high, (taps_own, taps_other), act_ref, EDGE)


def rim(meta, glu, edge, runs, taps_own, taps_other):
    width = glu.shape[1]
    vmem = pl.BlockSpec(memory_space=pltpu.VMEM)
    return pl.pallas_call(
        rim_kernel,
        in_specs=[pl.BlockSpec(memory_space=pltpu.SMEM)] + [vmem] * 5,
        out_specs=vmem,
        out_shape=jax.ShapeDtypeStruct((EDGE, width), BF16),
        scratch_shapes=[
            pltpu.VMEM((3 * EDGE, width), F32),
            pltpu.VMEM((8, 3 * EDGE - 8, width), F32),
        ],
        compiler_params=pltpu.CompilerParams(vmem_limit_bytes=VMEM_LIMIT),
        cost_estimate=weight(1),
        name="rim",
    )(meta, glu, edge, runs, taps_own, taps_other)


def last_product(act_ref, rim_ref, rim_at, mid_ref, w_first, w_second, cols, act):
    chan = act_ref.shape[1] // 2
    act[...] = act_ref[...]
    act[pl.ds(rim_at, EDGE), :] = rim_ref[...]
    first = dot(act[:, :chan], w_first[:, cols]).astype(BF16).astype(F32)
    second = dot(act[:, chan:], w_second[:, cols]).astype(BF16).astype(F32)
    return (mid_ref[...].astype(F32) + (first + second)).astype(BF16)


def finish_own_kernel(meta, act_ref, rim_ref, mid_ref, w_own, w_other, out_ref, act):
    h = meta[0]
    rows, half = out_ref.shape
    out_ref[...] = last_product(
        act_ref, rim_ref, pl.multiple_of(h * (rows - EDGE), EDGE), mid_ref, w_own, w_other,
        pl.ds(pl.multiple_of(h * half, half), half), act,
    )


def finish_kernel(meta, act_ref, rim_ref, mid_ref, w_own, w_other, done_ref, out_ref, act):
    h = meta[0]
    rows, half = done_ref.shape
    out_ref[pl.ds(pl.multiple_of(h * rows, rows), rows), :] = done_ref[...]
    out_ref[pl.ds(pl.multiple_of((1 - h) * rows, rows), rows), :] = last_product(
        act_ref, rim_ref, pl.multiple_of((1 - h) * (rows - EDGE), EDGE), mid_ref, w_other, w_own,
        pl.ds(pl.multiple_of(h * half, half), half), act,
    )


def finish(meta, act, rim_act, mid, w_own, w_other, done=None):
    rows, half = mid.shape
    vmem = pl.BlockSpec(memory_space=pltpu.VMEM)
    args = (act, rim_act, mid, w_own, w_other) + (() if done is None else (done,))
    return pl.pallas_call(
        finish_own_kernel if done is None else finish_kernel,
        in_specs=[pl.BlockSpec(memory_space=pltpu.SMEM)] + [vmem] * len(args),
        out_specs=vmem,
        out_shape=jax.ShapeDtypeStruct((rows if done is None else 2 * rows, half), BF16),
        scratch_shapes=[pltpu.VMEM(act.shape, BF16)],
        compiler_params=pltpu.CompilerParams(vmem_limit_bytes=VMEM_LIMIT),
        cost_estimate=weight(1.2),
        name="finish_own" if done is None else "finish",
    )(meta, *args)


def local(
    blocks,
    frames,
    segment_ids,
    utt_valid,
    attn_gain,
    qkv_weight,
    out_weight,
    conv_gain,
    pointwise_in,
    depthwise,
    mid_gain,
    pointwise_out,
):
    rows = frames.shape[0]

    def swap(value):
        return lax.ppermute(value, "head", [(0, 1), (1, 0)])

    def shift(value, step):
        pairs = [(i, i - step if i % 2 == 0 else i + step) for i in range(blocks)]
        return lax.ppermute(value, "tm", [p for p in pairs if 0 <= p[1] < blocks])

    def exchange(value):
        return lax.ppermute(value, "tm", [(i, i ^ 1) for i in range(blocks)])

    block = lax.axis_index("tm").astype(jnp.int32)
    column = block % 2
    meta = jnp.stack([
        lax.axis_index("head").astype(jnp.int32),
        column,
        block * rows,
        (block + 1 - 2 * column) * rows,
    ])
    other = swap(frames)
    keep, query, send, passed = project(meta, frames, other, attn_gain, qkv_weight)
    far_own = shift(passed, 1)
    pair = exchange(send)
    far_pair = shift(keep, 2)

    segment_ids, _ = lax.optimization_barrier((segment_ids, passed))
    ids = jnp.arange(utt_valid.shape[0], dtype=jnp.int32)
    counts = jnp.sum((segment_ids[None, :] == ids[:, None]).astype(jnp.int32), axis=1)
    counts = lax.all_to_all(
        jnp.broadcast_to(counts[None, :], (blocks, counts.shape[0])), "tm", 0, 0
    )
    pointwise = pointwise_in.transpose(1, 0, 2)
    out_weight, pointwise, depthwise, mid_gain, pointwise_out, _ = lax.optimization_barrier(
        (out_weight, pointwise, depthwise, mid_gain, pointwise_out, keep)
    )
    taps = jnp.concatenate([depthwise, mid_gain[None, :]], axis=0)
    pointwise_other = swap(pointwise)
    out_other = swap(out_weight)
    pointwise_out_other = swap(pointwise_out)
    taps_other = swap(taps)
    runs, pair_runs = bounds(meta, counts, utt_valid, rows)

    pair_context = attend(column.reshape(1), pair, pair, keep, far_pair, pair_runs)
    pair_context = exchange(pair_context)
    context = attend((1 - column).reshape(1), query, keep, pair, far_own, runs)
    contexts = (context, pair_context, swap(context), swap(pair_context))
    contexts, pointwise_out_other, taps_other = lax.optimization_barrier(
        (contexts, pointwise_out_other, taps_other)
    )
    glu, edge, mid_keep, mid_send = gated(
        meta, contexts, frames, other, out_weight, out_other, conv_gain,
        pointwise, pointwise_other, runs,
    )
    edges = [(2 * i, 2 * (i - 1) + 1) for i in range(1, blocks)]
    edges += [(2 * i + 1, 2 * (i + 1)) for i in range(blocks - 1)]
    edge = lax.ppermute(edge, ("tm", "head"), edges)
    mid_other = swap(mid_send)
    act = convolve(meta, glu, runs, taps, taps_other)
    act_other = swap(act)
    rim_act = rim(meta, glu, edge, runs, taps, taps_other)
    rim_other = swap(rim_act)
    done = finish(meta, act, rim_act, mid_keep, pointwise_out, pointwise_out_other)
    return finish(
        meta, act_other, rim_other, mid_other, pointwise_out, pointwise_out_other, done
    )


def solution(mesh):
    in_specs = (
        P(("grp", "tm"), "head"),
        P(("grp", "tm")),
        P("grp"),
        P(),
        P(None, None, "head"),
        P("head", None),
        P(),
        P(None, None, "head"),
        P(None, "head"),
        P("head"),
        P("head", None),
    )
    out_specs = P(("grp", "tm"), "head")
    return jax.shard_map(
        functools.partial(local, mesh.shape["tm"]),
        mesh=mesh,
        in_specs=in_specs,
        out_specs=out_specs,
        check_vma=False,
    )
```

```python
import functools
import math

import jax
import jax.numpy as jnp
from jax import lax
from jax.experimental import pallas as pl
from jax.experimental.pallas import tpu as pltpu
from jax.sharding import PartitionSpec as P

HEAD_DIM = 64
CONV_CH = 512
KERNEL = 31
WIN = 512
EDGE = 16
SENT = 64
NEG = -1e30
EXP_SCALE = HEAD_DIM ** (-0.5) * math.log2(math.e)
F32 = jnp.float32
BF16 = jnp.bfloat16
VMEM_LIMIT = 16 * 1024 * 1024


def weight(microseconds):
    return pl.CostEstimate(
        flops=int(microseconds * 1.15e9), bytes_accessed=0, transcendentals=0
    )


def dot(a, b):
    return jnp.dot(a, b, preferred_element_type=F32)


def normalize_halves(own, other, gain_own, gain_other):
    width = own.shape[1] + other.shape[1]
    mean = (
        jnp.sum(own, axis=1, keepdims=True) + jnp.sum(other, axis=1, keepdims=True)
    ) / width
    own = own - mean
    other = other - mean
    spread = (
        jnp.sum(own * own, axis=1, keepdims=True) + jnp.sum(other * other, axis=1, keepdims=True)
    ) / width
    scale = lax.rsqrt(spread + 1e-05)
    return (own * scale * gain_own).astype(BF16), (other * scale * gain_other).astype(BF16)


def qkv_kernel(
    meta, own_ref, other_ref, gain_ref, w_ref, keep_ref, query_ref, send_ref, pass_ref
):
    h = meta[0]
    first = meta[1] == 0
    rows = own_ref.shape[0]
    tile = 256
    for at in range(0, rows, tile):
        here = slice(at, at + tile)
        n_own, n_other = normalize_halves(
            own_ref[here, :].astype(F32), other_ref[here, :].astype(F32),
            gain_ref[h], gain_ref[1 - h],
        )
        for slot, part in enumerate((1, 2, 0)):
            value = (dot(n_own, w_ref[part, h]) + dot(n_other, w_ref[part, 1 - h])).astype(BF16)
            sub = value.shape[1] // 2
            cols = slice(slot * sub, slot * sub + sub)
            keep = jnp.where(first, value[:, :sub], value[:, sub:])
            send = jnp.where(first, value[:, sub:], value[:, :sub])
            send_ref[here, cols] = send
            if slot < 2:
                keep_ref[here, cols] = keep
                pass_ref[here, cols] = send
            else:
                query_ref[here, :] = keep


def project(meta, frames, other, gain, qkv):
    rows, half = frames.shape
    width = qkv.shape[2]
    vmem = pl.BlockSpec(memory_space=pltpu.VMEM)
    return pl.pallas_call(
        qkv_kernel,
        in_specs=[pl.BlockSpec(memory_space=pltpu.SMEM)] + [vmem] * 4,
        out_specs=[vmem] * 4,
        out_shape=[
            jax.ShapeDtypeStruct((rows, width), BF16),
            jax.ShapeDtypeStruct((rows, width // 2), BF16),
            jax.ShapeDtypeStruct((rows, 3 * width // 2), BF16),
            jax.ShapeDtypeStruct((rows, width), BF16),
        ],
        compiler_params=pltpu.CompilerParams(vmem_limit_bytes=VMEM_LIMIT),
        name="project",
    )(meta, frames, other, gain.reshape(2, 1, half),
      qkv.transpose(1, 0, 2).reshape(3, 2, half, width))


def bounds_kernel(meta, counts, valid, own_ref, pair_ref):
    utts = valid.shape[1]
    rows = own_ref.shape[0]
    square = (utts, utts)
    sub = lax.broadcasted_iota(jnp.int32, square, 0)
    lane = lax.broadcasted_iota(jnp.int32, square, 1)
    total = jnp.sum(counts[...].astype(F32), axis=0, keepdims=True)
    limit = jnp.broadcast_to(jnp.minimum(total, valid[...].astype(F32)), square)
    total = jnp.broadcast_to(total, square)
    start = jnp.sum(jnp.where(lane < sub, total, 0.0), axis=1, keepdims=True)
    stop = start + jnp.sum(jnp.where(lane == sub, limit, 0.0), axis=1, keepdims=True)
    at = lax.broadcasted_iota(jnp.int32, (utts, rows), 1).astype(F32)
    for slot, ref in enumerate((own_ref, pair_ref)):
        origin = meta[2 + slot].astype(F32)
        lo = start - origin
        hi = stop - origin
        inside = (at >= lo) & (at < hi)
        low = jnp.sum(jnp.where(inside, lo, 0.0), axis=0, keepdims=True)
        high = jnp.sum(jnp.where(inside, hi, 0.0), axis=0, keepdims=True)
        both = jnp.concatenate([low, high, jnp.zeros((126, rows), F32)], axis=0)
        ref[...] = both.T.astype(jnp.int32)


def bounds(meta, counts, valid, rows):
    vmem = pl.BlockSpec(memory_space=pltpu.VMEM)
    return pl.pallas_call(
        bounds_kernel,
        in_specs=[pl.BlockSpec(memory_space=pltpu.SMEM), vmem, vmem],
        out_specs=[vmem] * 2,
        out_shape=[jax.ShapeDtypeStruct((rows, 128), jnp.int32)] * 2,
        compiler_params=pltpu.CompilerParams(vmem_limit_bytes=VMEM_LIMIT),
        name="bounds",
    )(meta, counts, valid.reshape(1, -1))


def attend_kernel(a_high, query, center, side_a, side_b, run_ref, out_ref):
    rows = center.shape[0]
    width = center.shape[1] // 2 if query.shape[1] < center.shape[1] else center.shape[1] // 3
    q_cols = slice(query.shape[1] - width, query.shape[1])
    tile = rows // 2
    lane = lax.broadcasted_iota(jnp.int32, (tile, width), 1)

    def run(low_ref, high_ref):
        for block in range(2):
            at = block * tile
            pieces = (
                ((low_ref, 0, rows, -rows), (center, 0, rows, 0), (high_ref, 0, tile, rows))
                if block == 0
                else ((low_ref, tile, tile, -rows), (center, 0, rows, 0), (high_ref, 0, rows, rows))
            )
            position = lax.broadcasted_iota(jnp.int32, (tile, 1), 0) + at
            lo = run_ref[at : at + tile, 0:1]
            hi = run_ref[at : at + tile, 1:2]
            near_lo = jnp.maximum(lo, position - WIN)
            near_hi = jnp.minimum(hi, position + (WIN + 1))
            biases = []
            for _, first, size, origin in pieces:
                u = lax.broadcasted_iota(jnp.int32, (tile, size), 1) + (origin + first)
                biases.append(jnp.where((u >= near_lo) & (u < near_hi), 0.0, NEG))
            q = query[at : at + tile, q_cols]
            outs = []
            for sub in range(2):
                q_sub = jnp.where((lane >= HEAD_DIM) == (sub == 1), q, jnp.zeros_like(q))
                scores = []
                for (ref, first, size, _), bias in zip(pieces, biases):
                    s = lax.dot_general(
                        q_sub, ref[first : first + size, :width], (((1,), (1,)), ((), ())),
                        preferred_element_type=F32,
                    )
                    scores.append(s + bias)
                peak = functools.reduce(
                    jnp.maximum, [jnp.max(s, axis=1, keepdims=True) for s in scores]
                )
                total = jnp.zeros((tile, 1), F32)
                context = jnp.zeros((tile, width), F32)
                for (ref, first, size, _), s in zip(pieces, scores):
                    expw = jnp.exp2((s - peak) * EXP_SCALE)
                    total = total + jnp.sum(expw, axis=1, keepdims=True)
                    context = context + dot(
                        expw.astype(BF16), ref[first : first + size, width : 2 * width]
                    )
                outs.append(context / jnp.maximum(total, 1.0))
            joined = jnp.where(lane >= HEAD_DIM, outs[1], outs[0])
            out_ref[at : at + tile, :] = jnp.where(hi > lo, joined, 0.0).astype(BF16)

    @pl.when(a_high[0] == 1)
    def _():
        run(side_b, side_a)

    @pl.when(a_high[0] == 0)
    def _():
        run(side_a, side_b)


def attend(a_high, query, center, side_a, side_b, runs):
    rows, width = side_b.shape[0], side_b.shape[1] // 2
    vmem = pl.BlockSpec(memory_space=pltpu.VMEM)
    return pl.pallas_call(
        attend_kernel,
        in_specs=[pl.BlockSpec(memory_space=pltpu.SMEM)] + [vmem] * 5,
        out_specs=vmem,
        out_shape=jax.ShapeDtypeStruct((rows, width), BF16),
        compiler_params=pltpu.CompilerParams(vmem_limit_bytes=VMEM_LIMIT),
        name="attend",
    )(a_high, query, center, side_a, side_b, runs)


def gate_kernel(
    meta,
    mine_own, pair_own, mine_other, pair_other,
    x_own, x_other,
    out_own, out_other,
    gain_ref,
    in_own, in_other,
    run_ref,
    glu_ref, edge_ref, mid_keep, mid_send,
):
    h = meta[0]
    first = meta[1] == 0
    half = x_own.shape[1]
    rows = glu_ref.shape[0]
    here = pl.ds(pl.multiple_of(h * (rows - 2 * EDGE), EDGE), rows)

    def joined(mine, pair):
        mine = mine[here, :]
        pair = pair[here, :]
        return jnp.concatenate(
            [jnp.where(first, mine, pair), jnp.where(first, pair, mine)], axis=1
        )

    c_own = joined(mine_own, pair_own)
    c_other = joined(mine_other, pair_other)
    own_cols = pl.ds(pl.multiple_of(h * half, half), half)
    other_cols = pl.ds(pl.multiple_of((1 - h) * half, half), half)

    def mid(cols, x_ref):
        first = dot(c_own, out_own[:, cols]).astype(BF16).astype(F32)
        second = dot(c_other, out_other[:, cols]).astype(BF16).astype(F32)
        return (x_ref[here, :].astype(F32) + (first + second)).astype(BF16)

    m_own = mid(own_cols, x_own)
    m_other = mid(other_cols, x_other)
    keep = rows - EDGE

    @pl.when(h == 0)
    def _():
        mid_keep[...] = m_own[:keep]
        mid_send[...] = m_other[:keep]

    @pl.when(h == 1)
    def _():
        mid_keep[...] = m_own[EDGE:]
        mid_send[...] = m_other[EDGE:]

    n_own, n_other = normalize_halves(
        m_own.astype(F32), m_other.astype(F32), gain_ref[h], gain_ref[1 - h]
    )
    run = run_ref[here, :]
    valid = run[:, 1:2] > run[:, 0:1]
    glus = []
    for w_ref in (in_own, in_other):
        value = dot(n_own, w_ref[0, own_cols, :]) + dot(n_other, w_ref[0, other_cols, :])
        gate = dot(n_own, w_ref[1, own_cols, :]) + dot(n_other, w_ref[1, other_cols, :])
        glu = value / (1.0 + jnp.exp(-gate))
        glus.append(jnp.where(valid, glu, 0.0).astype(BF16))
    chan = glus[0].shape[1]
    glu_ref[:, :chan] = glus[0]
    glu_ref[:, chan:] = glus[1]

    @pl.when(h == 0)
    def _():
        edge_ref[:, :chan] = glus[1][:SENT]
        edge_ref[:, chan:] = glus[0][:SENT]

    @pl.when(h == 1)
    def _():
        edge_ref[:, :chan] = glus[1][rows - SENT :]
        edge_ref[:, chan:] = glus[0][rows - SENT :]


def gated(meta, contexts, x_own, x_other, out_own, out_other, gain, in_own, in_other, runs):
    rows = x_own.shape[0] // 2 + EDGE
    half = x_own.shape[1]
    chan = in_own.shape[2]
    vmem = pl.BlockSpec(memory_space=pltpu.VMEM)
    return pl.pallas_call(
        gate_kernel,
        in_specs=[pl.BlockSpec(memory_space=pltpu.SMEM)] + [vmem] * 12,
        out_specs=[vmem] * 4,
        out_shape=[
            jax.ShapeDtypeStruct((rows, 2 * chan), BF16),
            jax.ShapeDtypeStruct((SENT, 2 * chan), BF16),
            jax.ShapeDtypeStruct((rows - EDGE, half), BF16),
            jax.ShapeDtypeStruct((rows - EDGE, half), BF16),
        ],
        compiler_params=pltpu.CompilerParams(vmem_limit_bytes=VMEM_LIMIT),
        name="gated",
    )(meta, *contexts, x_own, x_other, out_own, out_other,
      gain.reshape(2, 1, half), in_own, in_other, runs)


def conv_rows(shifted, low, high, taps, out_ref, rows):
    width = out_ref.shape[1]
    chan = width // 2
    reach = KERNEL // 2
    step = min(32, rows)
    cols = range(0, width, 128)
    weights = [
        [
            (taps[0] if col < chan else taps[1])[tap : tap + 1, col % chan : col % chan + 128]
            for col in cols
        ]
        for tap in range(KERNEL + 1)
    ]
    for base in range(0, rows, step):
        totals = [jnp.zeros((step, 128), F32) for _ in cols]
        for tap in range(KERNEL):
            shift = tap - reach
            same = (low[base : base + step] <= shift) & (high[base : base + step] > shift)
            row = base + EDGE + shift
            first = row - row % 8
            for index, col in enumerate(cols):
                piece = shifted[row % 8, first : first + step, col : col + 128]
                totals[index] = totals[index] + jnp.where(same, piece, 0.0) * weights[tap][index]
        mean = jnp.sum(sum(totals), axis=1, keepdims=True) / CONV_CH
        square = jnp.sum(sum(t * t for t in totals), axis=1, keepdims=True) / CONV_CH
        scale = lax.rsqrt(square - mean * mean + 1e-05)
        for index, col in enumerate(cols):
            y = (totals[index] - mean) * scale * weights[KERNEL][index]
            out_ref[base : base + step, col : col + 128] = (y / (1.0 + jnp.exp(-y))).astype(BF16)


def run_offsets(run_ref, first, rows):
    run = run_ref[pl.ds(first, rows), :]
    at = lax.broadcasted_iota(jnp.int32, (rows, 128), 0) + first
    low = jnp.broadcast_to(run[:, 0:1], (rows, 128)) - at
    high = jnp.broadcast_to(run[:, 1:2], (rows, 128)) - at
    return low, high


def conv_kernel(meta, glu_ref, run_ref, taps_own, taps_other, act_ref, ext, shifted):
    h = meta[0]
    rows, width = act_ref.shape
    got = glu_ref.shape[0]
    ext[pl.ds(pl.multiple_of(h * got, EDGE), EDGE), :] = jnp.zeros((EDGE, width), F32)
    ext[pl.ds(pl.multiple_of((1 - h) * EDGE, EDGE), got), :] = glu_ref[...].astype(F32)
    size = shifted.shape[1]
    for s in range(8):
        shifted[s] = ext[s : s + size, :]
    low, high = run_offsets(run_ref, pl.multiple_of(h * rows, rows), rows)
    conv_rows(shifted, low, high, (taps_own, taps_other), act_ref, rows)


def convolve(meta, glu, runs, taps_own, taps_other):
    rows = glu.shape[0] - EDGE
    width = glu.shape[1]
    vmem = pl.BlockSpec(memory_space=pltpu.VMEM)
    return pl.pallas_call(
        conv_kernel,
        in_specs=[pl.BlockSpec(memory_space=pltpu.SMEM)] + [vmem] * 4,
        out_specs=vmem,
        out_shape=jax.ShapeDtypeStruct((rows, width), BF16),
        scratch_shapes=[
            pltpu.VMEM((rows + 2 * EDGE, width), F32),
            pltpu.VMEM((8, rows + 2 * EDGE - 8, width), F32),
        ],
        compiler_params=pltpu.CompilerParams(vmem_limit_bytes=VMEM_LIMIT),
        cost_estimate=weight(3),
        name="convolve",
    )(meta, glu, runs, taps_own, taps_other)


def rim_kernel(meta, glu_ref, edge_ref, run_ref, taps_own, taps_other, act_ref, ext, shifted):
    h = meta[0]
    got = glu_ref.shape[0]
    near = 2 * EDGE
    ext[pl.ds(pl.multiple_of(h * near, EDGE), EDGE), :] = edge_ref[
        pl.ds(pl.multiple_of((1 - h) * (SENT - EDGE), EDGE), EDGE), :
    ].astype(F32)
    ext[pl.ds(pl.multiple_of((1 - h) * EDGE, EDGE), near), :] = glu_ref[
        pl.ds(pl.multiple_of(h * (got - near), EDGE), near), :
    ].astype(F32)
    size = shifted.shape[1]
    for s in range(8):
        shifted[s] = ext[s : s + size, :]
    first = pl.multiple_of(h * (run_ref.shape[0] - EDGE), EDGE)
    low, high = run_offsets(run_ref, first, EDGE)
    conv_rows(shifted, low, high, (taps_own, taps_other), act_ref, EDGE)


def rim(meta, glu, edge, runs, taps_own, taps_other):
    width = glu.shape[1]
    vmem = pl.BlockSpec(memory_space=pltpu.VMEM)
    return pl.pallas_call(
        rim_kernel,
        in_specs=[pl.BlockSpec(memory_space=pltpu.SMEM)] + [vmem] * 5,
        out_specs=vmem,
        out_shape=jax.ShapeDtypeStruct((EDGE, width), BF16),
        scratch_shapes=[
            pltpu.VMEM((3 * EDGE, width), F32),
            pltpu.VMEM((8, 3 * EDGE - 8, width), F32),
        ],
        compiler_params=pltpu.CompilerParams(vmem_limit_bytes=VMEM_LIMIT),
        cost_estimate=weight(1),
        name="rim",
    )(meta, glu, edge, runs, taps_own, taps_other)


def last_product(act_ref, rim_ref, rim_at, mid_ref, w_first, w_second, cols, act):
    chan = act_ref.shape[1] // 2
    act[...] = act_ref[...]
    act[pl.ds(rim_at, EDGE), :] = rim_ref[...]
    first = dot(act[:, :chan], w_first[:, cols]).astype(BF16).astype(F32)
    second = dot(act[:, chan:], w_second[:, cols]).astype(BF16).astype(F32)
    return (mid_ref[...].astype(F32) + (first + second)).astype(BF16)


def finish_own_kernel(meta, act_ref, rim_ref, mid_ref, w_own, w_other, out_ref, act):
    h = meta[0]
    rows, half = out_ref.shape
    out_ref[...] = last_product(
        act_ref, rim_ref, pl.multiple_of(h * (rows - EDGE), EDGE), mid_ref, w_own, w_other,
        pl.ds(pl.multiple_of(h * half, half), half), act,
    )


def finish_kernel(meta, act_ref, rim_ref, mid_ref, w_own, w_other, done_ref, out_ref, act):
    h = meta[0]
    rows, half = done_ref.shape
    out_ref[pl.ds(pl.multiple_of(h * rows, rows), rows), :] = done_ref[...]
    out_ref[pl.ds(pl.multiple_of((1 - h) * rows, rows), rows), :] = last_product(
        act_ref, rim_ref, pl.multiple_of((1 - h) * (rows - EDGE), EDGE), mid_ref, w_other, w_own,
        pl.ds(pl.multiple_of(h * half, half), half), act,
    )


def finish(meta, act, rim_act, mid, w_own, w_other, done=None):
    rows, half = mid.shape
    vmem = pl.BlockSpec(memory_space=pltpu.VMEM)
    args = (act, rim_act, mid, w_own, w_other) + (() if done is None else (done,))
    return pl.pallas_call(
        finish_own_kernel if done is None else finish_kernel,
        in_specs=[pl.BlockSpec(memory_space=pltpu.SMEM)] + [vmem] * len(args),
        out_specs=vmem,
        out_shape=jax.ShapeDtypeStruct((rows if done is None else 2 * rows, half), BF16),
        scratch_shapes=[pltpu.VMEM(act.shape, BF16)],
        compiler_params=pltpu.CompilerParams(vmem_limit_bytes=VMEM_LIMIT),
        cost_estimate=weight(1.2),
        name="finish_own" if done is None else "finish",
    )(meta, *args)


def local(
    blocks,
    frames,
    segment_ids,
    utt_valid,
    attn_gain,
    qkv_weight,
    out_weight,
    conv_gain,
    pointwise_in,
    depthwise,
    mid_gain,
    pointwise_out,
):
    rows = frames.shape[0]

    def swap(value):
        return lax.ppermute(value, "head", [(0, 1), (1, 0)])

    def shift(value, step):
        pairs = [(i, i - step if i % 2 == 0 else i + step) for i in range(blocks)]
        return lax.ppermute(value, "tm", [p for p in pairs if 0 <= p[1] < blocks])

    def exchange(value):
        return lax.ppermute(value, "tm", [(i, i ^ 1) for i in range(blocks)])

    block = lax.axis_index("tm").astype(jnp.int32)
    column = block % 2
    meta = jnp.stack([
        lax.axis_index("head").astype(jnp.int32),
        column,
        block * rows,
        (block + 1 - 2 * column) * rows,
    ])
    other = swap(frames)
    keep, query, send, passed = project(meta, frames, other, attn_gain, qkv_weight)
    far_own = shift(passed, 1)
    pair = exchange(send)
    far_pair = shift(keep, 2)

    segment_ids, _ = lax.optimization_barrier((segment_ids, passed))
    ids = jnp.arange(utt_valid.shape[0], dtype=jnp.int32)
    counts = jnp.sum((segment_ids[None, :] == ids[:, None]).astype(jnp.int32), axis=1)
    counts = lax.all_to_all(
        jnp.broadcast_to(counts[None, :], (blocks, counts.shape[0])), "tm", 0, 0
    )
    pointwise = pointwise_in.transpose(1, 0, 2)
    out_weight, pointwise, _ = lax.optimization_barrier((out_weight, pointwise, keep))
    pointwise_other = swap(pointwise)
    out_other = swap(out_weight)
    runs, pair_runs = bounds(meta, counts, utt_valid, rows)
    pair, far_pair, far_own, runs, pair_runs = lax.optimization_barrier(
        (pair, far_pair, far_own, runs, pair_runs)
    )
    pair_context = attend(column.reshape(1), pair, pair, keep, far_pair, pair_runs)
    depthwise, mid_gain, pointwise_out, pair_context = lax.optimization_barrier(
        (depthwise, mid_gain, pointwise_out, pair_context)
    )
    pair_context = exchange(pair_context)
    taps = jnp.concatenate([depthwise, mid_gain[None, :]], axis=0)
    pointwise_out_other = swap(pointwise_out)
    taps_other = swap(taps)
    context = attend((1 - column).reshape(1), query, keep, pair, far_own, runs)
    contexts = (context, pair_context, swap(context), swap(pair_context))
    contexts, pointwise_out_other, taps_other = lax.optimization_barrier(
        (contexts, pointwise_out_other, taps_other)
    )
    glu, edge, mid_keep, mid_send = gated(
        meta, contexts, frames, other, out_weight, out_other, conv_gain,
        pointwise, pointwise_other, runs,
    )
    edges = [(2 * i, 2 * (i - 1) + 1) for i in range(1, blocks)]
    edges += [(2 * i + 1, 2 * (i + 1)) for i in range(blocks - 1)]
    edge = lax.ppermute(edge, ("tm", "head"), edges)
    mid_other = swap(mid_send)
    act = convolve(meta, glu, runs, taps, taps_other)
    act_other = swap(act)
    rim_act = rim(meta, glu, edge, runs, taps, taps_other)
    rim_other = swap(rim_act)
    done = finish(meta, act, rim_act, mid_keep, pointwise_out, pointwise_out_other)
    return finish(
        meta, act_other, rim_other, mid_other, pointwise_out, pointwise_out_other, done
    )


def solution(mesh):
    in_specs = (
        P(("grp", "tm"), "head"),
        P(("grp", "tm")),
        P("grp"),
        P(),
        P(None, None, "head"),
        P("head", None),
        P(),
        P(None, None, "head"),
        P(None, "head"),
        P("head"),
        P("head", None),
    )
    out_specs = P(("grp", "tm"), "head")
    return jax.shard_map(
        functools.partial(local, mesh.shape["tm"]),
        mesh=mesh,
        in_specs=in_specs,
        out_specs=out_specs,
        check_vma=False,
    )
```

```python
import functools
import math

import jax
import jax.numpy as jnp
from jax import lax
from jax.experimental import pallas as pl
from jax.experimental.pallas import tpu as pltpu
from jax.sharding import PartitionSpec as P

HEAD_DIM = 64
CONV_CH = 512
KERNEL = 31
WIN = 512
EDGE = 16
SENT = 64
NEG = -1e30
EXP_SCALE = HEAD_DIM ** (-0.5) * math.log2(math.e)
F32 = jnp.float32
BF16 = jnp.bfloat16
VMEM_LIMIT = 16 * 1024 * 1024


def weight(microseconds):
    return pl.CostEstimate(
        flops=int(microseconds * 1.15e9), bytes_accessed=0, transcendentals=0
    )


def dot(a, b):
    return jnp.dot(a, b, preferred_element_type=F32)


def normalize_halves(own, other, gain_own, gain_other):
    width = own.shape[1] + other.shape[1]
    mean = (
        jnp.sum(own, axis=1, keepdims=True) + jnp.sum(other, axis=1, keepdims=True)
    ) / width
    own = own - mean
    other = other - mean
    spread = (
        jnp.sum(own * own, axis=1, keepdims=True) + jnp.sum(other * other, axis=1, keepdims=True)
    ) / width
    scale = lax.rsqrt(spread + 1e-05)
    return (own * scale * gain_own).astype(BF16), (other * scale * gain_other).astype(BF16)


def qkv_kernel(
    meta, own_hbm, other_hbm, gain_ref, w_hbm, _, keep_ref, query_ref, send_ref, pass_ref,
    own_ref, other_ref, w_ref, sems,
):
    h = meta[0]
    first = meta[1] == 0
    order = (1, 2, 0)
    frames_in = [
        pltpu.make_async_copy(own_hbm, own_ref, sems.at[0]),
        pltpu.make_async_copy(other_hbm, other_ref, sems.at[1]),
    ]
    weights_in = [
        pltpu.make_async_copy(w_hbm.at[part], w_ref.at[part], sems.at[2 + slot])
        for slot, part in enumerate(order)
    ]
    for copy in frames_in + weights_in:
        copy.start()
    for copy in frames_in:
        copy.wait()
    rows = own_ref.shape[0]
    tile = 256
    for at in range(0, rows, tile):
        here = slice(at, at + tile)
        n_own, n_other = normalize_halves(
            own_ref[here, :].astype(F32), other_ref[here, :].astype(F32),
            gain_ref[h], gain_ref[1 - h],
        )
        for slot, part in enumerate(order):
            if at == 0:
                weights_in[slot].wait()
            value = (dot(n_own, w_ref[part, h]) + dot(n_other, w_ref[part, 1 - h])).astype(BF16)
            sub = value.shape[1] // 2
            cols = slice(slot * sub, slot * sub + sub)
            keep = jnp.where(first, value[:, :sub], value[:, sub:])
            send = jnp.where(first, value[:, sub:], value[:, :sub])
            send_ref[here, cols] = send
            if slot < 2:
                keep_ref[here, cols] = keep
                pass_ref[here, cols] = send
            else:
                query_ref[here, :] = keep


def project(meta, frames, other, gain, qkv, early):
    rows, half = frames.shape
    width = qkv.shape[2]
    vmem = pl.BlockSpec(memory_space=pltpu.VMEM)
    hbm = pl.BlockSpec(memory_space=pltpu.HBM)
    return pl.pallas_call(
        qkv_kernel,
        in_specs=[pl.BlockSpec(memory_space=pltpu.SMEM), hbm, hbm, vmem, hbm]
        + [pl.BlockSpec(memory_space=pl.ANY)],
        out_specs=[vmem] * 4,
        out_shape=[
            jax.ShapeDtypeStruct((rows, width), BF16),
            jax.ShapeDtypeStruct((rows, width // 2), BF16),
            jax.ShapeDtypeStruct((rows, 3 * width // 2), BF16),
            jax.ShapeDtypeStruct((rows, width), BF16),
        ],
        scratch_shapes=[
            pltpu.VMEM((rows, half), BF16),
            pltpu.VMEM((rows, half), BF16),
            pltpu.VMEM((3, 2, half, width), BF16),
            pltpu.SemaphoreType.DMA((5,)),
        ],
        compiler_params=pltpu.CompilerParams(vmem_limit_bytes=VMEM_LIMIT),
        name="project",
    )(meta, frames, other, gain.reshape(2, 1, half),
      qkv.transpose(1, 0, 2).reshape(3, 2, half, width), early)


def bounds_kernel(meta, counts, valid, own_ref, pair_ref):
    utts = valid.shape[1]
    rows = own_ref.shape[0]
    square = (utts, utts)
    sub = lax.broadcasted_iota(jnp.int32, square, 0)
    lane = lax.broadcasted_iota(jnp.int32, square, 1)
    total = jnp.sum(counts[...].astype(F32), axis=0, keepdims=True)
    limit = jnp.broadcast_to(jnp.minimum(total, valid[...].astype(F32)), square)
    total = jnp.broadcast_to(total, square)
    start = jnp.sum(jnp.where(lane < sub, total, 0.0), axis=1, keepdims=True)
    stop = start + jnp.sum(jnp.where(lane == sub, limit, 0.0), axis=1, keepdims=True)
    at = lax.broadcasted_iota(jnp.int32, (utts, rows), 1).astype(F32)
    for slot, ref in enumerate((own_ref, pair_ref)):
        origin = meta[2 + slot].astype(F32)
        lo = start - origin
        hi = stop - origin
        inside = (at >= lo) & (at < hi)
        low = jnp.sum(jnp.where(inside, lo, 0.0), axis=0, keepdims=True)
        high = jnp.sum(jnp.where(inside, hi, 0.0), axis=0, keepdims=True)
        both = jnp.concatenate([low, high, jnp.zeros((126, rows), F32)], axis=0)
        ref[...] = both.T.astype(jnp.int32)


def bounds(meta, counts, valid, rows):
    vmem = pl.BlockSpec(memory_space=pltpu.VMEM)
    return pl.pallas_call(
        bounds_kernel,
        in_specs=[pl.BlockSpec(memory_space=pltpu.SMEM), vmem, vmem],
        out_specs=[vmem] * 2,
        out_shape=[jax.ShapeDtypeStruct((rows, 128), jnp.int32)] * 2,
        compiler_params=pltpu.CompilerParams(vmem_limit_bytes=VMEM_LIMIT),
        name="bounds",
    )(meta, counts, valid.reshape(1, -1))


def attend_kernel(a_high, query, center, side_a, side_b, run_ref, out_ref):
    rows = center.shape[0]
    width = center.shape[1] // 2 if query.shape[1] < center.shape[1] else center.shape[1] // 3
    q_cols = slice(query.shape[1] - width, query.shape[1])
    tile = rows // 2
    lane = lax.broadcasted_iota(jnp.int32, (tile, width), 1)

    def run(low_ref, high_ref):
        for block in range(2):
            at = block * tile
            pieces = (
                ((low_ref, 0, rows, -rows), (center, 0, rows, 0), (high_ref, 0, tile, rows))
                if block == 0
                else ((low_ref, tile, tile, -rows), (center, 0, rows, 0), (high_ref, 0, rows, rows))
            )
            position = lax.broadcasted_iota(jnp.int32, (tile, 1), 0) + at
            lo = run_ref[at : at + tile, 0:1]
            hi = run_ref[at : at + tile, 1:2]
            near_lo = jnp.maximum(lo, position - WIN)
            near_hi = jnp.minimum(hi, position + (WIN + 1))
            biases = []
            for _, first, size, origin in pieces:
                u = lax.broadcasted_iota(jnp.int32, (tile, size), 1) + (origin + first)
                biases.append(jnp.where((u >= near_lo) & (u < near_hi), 0.0, NEG))
            q = query[at : at + tile, q_cols]
            outs = []
            for sub in range(2):
                q_sub = jnp.where((lane >= HEAD_DIM) == (sub == 1), q, jnp.zeros_like(q))
                scores = []
                for (ref, first, size, _), bias in zip(pieces, biases):
                    s = lax.dot_general(
                        q_sub, ref[first : first + size, :width], (((1,), (1,)), ((), ())),
                        preferred_element_type=F32,
                    )
                    scores.append(s + bias)
                peak = functools.reduce(
                    jnp.maximum, [jnp.max(s, axis=1, keepdims=True) for s in scores]
                )
                total = jnp.zeros((tile, 1), F32)
                context = jnp.zeros((tile, width), F32)
                for (ref, first, size, _), s in zip(pieces, scores):
                    expw = jnp.exp2((s - peak) * EXP_SCALE)
                    total = total + jnp.sum(expw, axis=1, keepdims=True)
                    context = context + dot(
                        expw.astype(BF16), ref[first : first + size, width : 2 * width]
                    )
                outs.append(context / jnp.maximum(total, 1.0))
            joined = jnp.where(lane >= HEAD_DIM, outs[1], outs[0])
            out_ref[at : at + tile, :] = jnp.where(hi > lo, joined, 0.0).astype(BF16)

    @pl.when(a_high[0] == 1)
    def _():
        run(side_b, side_a)

    @pl.when(a_high[0] == 0)
    def _():
        run(side_a, side_b)


def attend(a_high, query, center, side_a, side_b, runs):
    rows, width = side_b.shape[0], side_b.shape[1] // 2
    vmem = pl.BlockSpec(memory_space=pltpu.VMEM)
    return pl.pallas_call(
        attend_kernel,
        in_specs=[pl.BlockSpec(memory_space=pltpu.SMEM)] + [vmem] * 5,
        out_specs=vmem,
        out_shape=jax.ShapeDtypeStruct((rows, width), BF16),
        compiler_params=pltpu.CompilerParams(vmem_limit_bytes=VMEM_LIMIT),
        cost_estimate=weight(3),
        name="attend",
    )(a_high, query, center, side_a, side_b, runs)


def gate_kernel(
    meta,
    mine_own, pair_own, mine_other, pair_other,
    x_own, x_other,
    out_own, out_other,
    gain_ref,
    in_own, in_other,
    run_ref,
    glu_ref, edge_ref, mid_keep, mid_send,
):
    h = meta[0]
    first = meta[1] == 0
    half = x_own.shape[1]
    rows = glu_ref.shape[0]
    here = pl.ds(pl.multiple_of(h * (rows - 2 * EDGE), EDGE), rows)

    def joined(mine, pair):
        mine = mine[here, :]
        pair = pair[here, :]
        return jnp.concatenate(
            [jnp.where(first, mine, pair), jnp.where(first, pair, mine)], axis=1
        )

    depth = 2 * mine_own.shape[1]
    c_own = joined(mine_own, pair_own)
    c_other = joined(mine_other, pair_other)
    own_cols = pl.ds(pl.multiple_of(h * half, half), half)
    other_cols = pl.ds(pl.multiple_of((1 - h) * half, half), half)

    def mid(cols, x_ref):
        first = dot(c_own, out_own[:depth, cols]).astype(BF16).astype(F32)
        second = dot(c_other, out_other[:depth, cols]).astype(BF16).astype(F32)
        return (x_ref[here, :].astype(F32) + (first + second)).astype(BF16)

    m_own = mid(own_cols, x_own)
    m_other = mid(other_cols, x_other)
    keep = rows - EDGE

    @pl.when(h == 0)
    def _():
        mid_keep[...] = m_own[:keep]
        mid_send[...] = m_other[:keep]

    @pl.when(h == 1)
    def _():
        mid_keep[...] = m_own[EDGE:]
        mid_send[...] = m_other[EDGE:]

    n_own, n_other = normalize_halves(
        m_own.astype(F32), m_other.astype(F32), gain_ref[h], gain_ref[1 - h]
    )
    run = run_ref[here, :]
    valid = run[:, 1:2] > run[:, 0:1]
    glus = []
    for w_ref in (in_own, in_other):
        value = dot(n_own, w_ref[0, own_cols, :]) + dot(n_other, w_ref[0, other_cols, :])
        gate = dot(n_own, w_ref[1, own_cols, :]) + dot(n_other, w_ref[1, other_cols, :])
        glu = value / (1.0 + jnp.exp(-gate))
        glus.append(jnp.where(valid, glu, 0.0).astype(BF16))
    chan = glus[0].shape[1]
    glu_ref[:, :chan] = glus[0]
    glu_ref[:, chan:] = glus[1]

    @pl.when(h == 0)
    def _():
        edge_ref[:, :chan] = glus[1][:SENT]
        edge_ref[:, chan:] = glus[0][:SENT]

    @pl.when(h == 1)
    def _():
        edge_ref[:, :chan] = glus[1][rows - SENT :]
        edge_ref[:, chan:] = glus[0][rows - SENT :]


def gated(meta, contexts, x_own, x_other, out_own, out_other, gain, in_own, in_other, runs):
    rows = x_own.shape[0] // 2 + EDGE
    half = x_own.shape[1]
    chan = in_own.shape[2]
    vmem = pl.BlockSpec(memory_space=pltpu.VMEM)
    return pl.pallas_call(
        gate_kernel,
        in_specs=[pl.BlockSpec(memory_space=pltpu.SMEM)] + [vmem] * 12,
        out_specs=[vmem] * 4,
        out_shape=[
            jax.ShapeDtypeStruct((rows, 2 * chan), BF16),
            jax.ShapeDtypeStruct((SENT, 2 * chan), BF16),
            jax.ShapeDtypeStruct((rows - EDGE, half), BF16),
            jax.ShapeDtypeStruct((rows - EDGE, half), BF16),
        ],
        compiler_params=pltpu.CompilerParams(vmem_limit_bytes=VMEM_LIMIT),
        cost_estimate=weight(3),
        name="gated",
    )(meta, *contexts, x_own, x_other, out_own, out_other,
      gain.reshape(2, 1, half), in_own, in_other, runs)


def conv_rows(shifted, low, high, taps, out_ref, rows):
    width = out_ref.shape[1]
    chan = width // 2
    reach = KERNEL // 2
    step = min(32, rows)
    cols = range(0, width, 128)
    weights = [
        [
            (taps[0] if col < chan else taps[1])[tap : tap + 1, col % chan : col % chan + 128]
            for col in cols
        ]
        for tap in range(KERNEL + 1)
    ]
    for base in range(0, rows, step):
        totals = [jnp.zeros((step, 128), F32) for _ in cols]
        for tap in range(KERNEL):
            shift = tap - reach
            same = (low[base : base + step] <= shift) & (high[base : base + step] > shift)
            row = base + EDGE + shift
            first = row - row % 8
            for index, col in enumerate(cols):
                piece = shifted[row % 8, first : first + step, col : col + 128]
                totals[index] = totals[index] + jnp.where(same, piece, 0.0) * weights[tap][index]
        mean = jnp.sum(sum(totals), axis=1, keepdims=True) / CONV_CH
        square = jnp.sum(sum(t * t for t in totals), axis=1, keepdims=True) / CONV_CH
        scale = lax.rsqrt(square - mean * mean + 1e-05)
        for index, col in enumerate(cols):
            y = (totals[index] - mean) * scale * weights[KERNEL][index]
            out_ref[base : base + step, col : col + 128] = (y / (1.0 + jnp.exp(-y))).astype(BF16)


def run_offsets(run_ref, first, rows):
    run = run_ref[pl.ds(first, rows), :]
    at = lax.broadcasted_iota(jnp.int32, (rows, 128), 0) + first
    low = jnp.broadcast_to(run[:, 0:1], (rows, 128)) - at
    high = jnp.broadcast_to(run[:, 1:2], (rows, 128)) - at
    return low, high


def conv_kernel(meta, glu_ref, run_ref, taps_own, taps_other, act_ref, ext, shifted):
    h = meta[0]
    rows, width = act_ref.shape
    got = glu_ref.shape[0]
    ext[pl.ds(pl.multiple_of(h * got, EDGE), EDGE), :] = jnp.zeros((EDGE, width), F32)
    ext[pl.ds(pl.multiple_of((1 - h) * EDGE, EDGE), got), :] = glu_ref[...].astype(F32)
    size = shifted.shape[1]
    for s in range(8):
        shifted[s] = ext[s : s + size, :]
    low, high = run_offsets(run_ref, pl.multiple_of(h * rows, rows), rows)
    conv_rows(shifted, low, high, (taps_own, taps_other), act_ref, rows)


def convolve(meta, glu, runs, taps_own, taps_other):
    rows = glu.shape[0] - EDGE
    width = glu.shape[1]
    vmem = pl.BlockSpec(memory_space=pltpu.VMEM)
    return pl.pallas_call(
        conv_kernel,
        in_specs=[pl.BlockSpec(memory_space=pltpu.SMEM)] + [vmem] * 4,
        out_specs=vmem,
        out_shape=jax.ShapeDtypeStruct((rows, width), BF16),
        scratch_shapes=[
            pltpu.VMEM((rows + 2 * EDGE, width), F32),
            pltpu.VMEM((8, rows + 2 * EDGE - 8, width), F32),
        ],
        compiler_params=pltpu.CompilerParams(vmem_limit_bytes=VMEM_LIMIT),
        cost_estimate=weight(3),
        name="convolve",
    )(meta, glu, runs, taps_own, taps_other)


def rim_kernel(meta, glu_ref, edge_ref, run_ref, taps_own, taps_other, act_ref, ext, shifted):
    h = meta[0]
    got = glu_ref.shape[0]
    near = 2 * EDGE
    ext[pl.ds(pl.multiple_of(h * near, EDGE), EDGE), :] = edge_ref[
        pl.ds(pl.multiple_of((1 - h) * (SENT - EDGE), EDGE), EDGE), :
    ].astype(F32)
    ext[pl.ds(pl.multiple_of((1 - h) * EDGE, EDGE), near), :] = glu_ref[
        pl.ds(pl.multiple_of(h * (got - near), EDGE), near), :
    ].astype(F32)
    size = shifted.shape[1]
    for s in range(8):
        shifted[s] = ext[s : s + size, :]
    first = pl.multiple_of(h * (run_ref.shape[0] - EDGE), EDGE)
    low, high = run_offsets(run_ref, first, EDGE)
    conv_rows(shifted, low, high, (taps_own, taps_other), act_ref, EDGE)


def rim(meta, glu, edge, runs, taps_own, taps_other):
    width = glu.shape[1]
    vmem = pl.BlockSpec(memory_space=pltpu.VMEM)
    return pl.pallas_call(
        rim_kernel,
        in_specs=[pl.BlockSpec(memory_space=pltpu.SMEM)] + [vmem] * 5,
        out_specs=vmem,
        out_shape=jax.ShapeDtypeStruct((EDGE, width), BF16),
        scratch_shapes=[
            pltpu.VMEM((3 * EDGE, width), F32),
            pltpu.VMEM((8, 3 * EDGE - 8, width), F32),
        ],
        compiler_params=pltpu.CompilerParams(vmem_limit_bytes=VMEM_LIMIT),
        cost_estimate=weight(1),
        name="rim",
    )(meta, glu, edge, runs, taps_own, taps_other)


def last_product(act_ref, rim_ref, rim_at, mid_ref, w_first, w_second, cols, act):
    chan = act_ref.shape[1] // 2
    act[...] = act_ref[...]
    act[pl.ds(rim_at, EDGE), :] = rim_ref[...]
    below = w_first.shape[0] - chan
    first = dot(act[:, :chan], w_first[below:, cols]).astype(BF16).astype(F32)
    second = dot(act[:, chan:], w_second[below:, cols]).astype(BF16).astype(F32)
    return (mid_ref[...].astype(F32) + (first + second)).astype(BF16)


def finish_own_kernel(meta, act_ref, rim_ref, mid_ref, w_own, w_other, out_ref, act):
    h = meta[0]
    rows, half = out_ref.shape
    out_ref[...] = last_product(
        act_ref, rim_ref, pl.multiple_of(h * (rows - EDGE), EDGE), mid_ref, w_own, w_other,
        pl.ds(pl.multiple_of(h * half, half), half), act,
    )


def finish_kernel(meta, act_ref, rim_ref, mid_ref, w_own, w_other, done_ref, out_ref, act):
    h = meta[0]
    rows, half = done_ref.shape
    out_ref[pl.ds(pl.multiple_of(h * rows, rows), rows), :] = done_ref[...]
    out_ref[pl.ds(pl.multiple_of((1 - h) * rows, rows), rows), :] = last_product(
        act_ref, rim_ref, pl.multiple_of((1 - h) * (rows - EDGE), EDGE), mid_ref, w_other, w_own,
        pl.ds(pl.multiple_of(h * half, half), half), act,
    )


def finish(meta, act, rim_act, mid, w_own, w_other, done=None):
    rows, half = mid.shape
    vmem = pl.BlockSpec(memory_space=pltpu.VMEM)
    args = (act, rim_act, mid, w_own, w_other) + (() if done is None else (done,))
    return pl.pallas_call(
        finish_own_kernel if done is None else finish_kernel,
        in_specs=[pl.BlockSpec(memory_space=pltpu.SMEM)] + [vmem] * len(args),
        out_specs=vmem,
        out_shape=jax.ShapeDtypeStruct((rows if done is None else 2 * rows, half), BF16),
        scratch_shapes=[pltpu.VMEM(act.shape, BF16)],
        compiler_params=pltpu.CompilerParams(vmem_limit_bytes=VMEM_LIMIT),
        cost_estimate=weight(1.2),
        name="finish_own" if done is None else "finish",
    )(meta, *args)


def local(
    blocks,
    frames,
    segment_ids,
    utt_valid,
    attn_gain,
    qkv_weight,
    out_weight,
    conv_gain,
    pointwise_in,
    depthwise,
    mid_gain,
    pointwise_out,
):
    rows = frames.shape[0]

    def swap(value):
        return lax.ppermute(value, "head", [(0, 1), (1, 0)])

    def shift(value, step):
        pairs = [(i, i - step if i % 2 == 0 else i + step) for i in range(blocks)]
        return lax.ppermute(value, "tm", [p for p in pairs if 0 <= p[1] < blocks])

    def exchange(value):
        return lax.ppermute(value, "tm", [(i, i ^ 1) for i in range(blocks)])

    block = lax.axis_index("tm").astype(jnp.int32)
    column = block % 2
    meta = jnp.stack([
        lax.axis_index("head").astype(jnp.int32),
        column,
        block * rows,
        (block + 1 - 2 * column) * rows,
    ])
    other = swap(frames)
    pointwise = pointwise_in.transpose(1, 0, 2)
    keep, query, send, passed = project(
        meta, frames, other, attn_gain, qkv_weight, pointwise
    )
    far_own = shift(passed, 1)
    pair = exchange(send)
    far_pair = shift(keep, 2)

    segment_ids, _ = lax.optimization_barrier((segment_ids, passed))
    ids = jnp.arange(utt_valid.shape[0], dtype=jnp.int32)
    counts = jnp.sum((segment_ids[None, :] == ids[:, None]).astype(jnp.int32), axis=1)
    counts = lax.all_to_all(
        jnp.broadcast_to(counts[None, :], (blocks, counts.shape[0])), "tm", 0, 0
    )
    taps = jnp.concatenate([depthwise, mid_gain[None, :]], axis=0)
    out_weight, pointwise, taps, keep = lax.optimization_barrier(
        (out_weight, pointwise, taps, keep)
    )
    pointwise_other = swap(pointwise)
    out_other = swap(out_weight)
    runs, pair_runs = bounds(meta, counts, utt_valid, rows)
    taps, pointwise_out, runs = lax.optimization_barrier((taps, pointwise_out, runs))
    taps_other = swap(taps)
    pointwise_out_other = swap(pointwise_out)
    pair, far_pair, far_own, runs, pair_runs = lax.optimization_barrier(
        (pair, far_pair, far_own, runs, pair_runs)
    )
    pair_context = attend(column.reshape(1), pair, pair, keep, far_pair, pair_runs)
    pair_context = exchange(pair_context)
    context = attend((1 - column).reshape(1), query, keep, pair, far_own, runs)
    contexts = (context, pair_context, swap(context), swap(pair_context))
    glu, edge, mid_keep, mid_send = gated(
        meta, contexts, frames, other, out_weight, out_other, conv_gain,
        pointwise, pointwise_other, runs,
    )
    edges = [(2 * i, 2 * (i - 1) + 1) for i in range(1, blocks)]
    edges += [(2 * i + 1, 2 * (i + 1)) for i in range(blocks - 1)]
    edge = lax.ppermute(edge, ("tm", "head"), edges)
    mid_other = swap(mid_send)
    act = convolve(meta, glu, runs, taps, taps_other)
    act_other = swap(act)
    rim_act = rim(meta, glu, edge, runs, taps, taps_other)
    rim_other = swap(rim_act)
    done = finish(meta, act, rim_act, mid_keep, pointwise_out, pointwise_out_other)
    return finish(
        meta, act_other, rim_other, mid_other, pointwise_out, pointwise_out_other, done
    )


def solution(mesh):
    in_specs = (
        P(("grp", "tm"), "head"),
        P(("grp", "tm")),
        P("grp"),
        P(),
        P(None, None, "head"),
        P("head", None),
        P(),
        P(None, None, "head"),
        P(None, "head"),
        P("head"),
        P("head", None),
    )
    out_specs = P(("grp", "tm"), "head")
    return jax.shard_map(
        functools.partial(local, mesh.shape["tm"]),
        mesh=mesh,
        in_specs=in_specs,
        out_specs=out_specs,
        check_vma=False,
    )
```

```python
import functools
import math

import jax
import jax.numpy as jnp
from jax import lax
from jax.experimental import pallas as pl
from jax.experimental.pallas import tpu as pltpu
from jax.sharding import PartitionSpec as P

HEAD_DIM = 64
CONV_CH = 512
KERNEL = 31
WIN = 512
EDGE = 16
SENT = 64
NEG = -1e30
EXP_SCALE = HEAD_DIM ** (-0.5) * math.log2(math.e)
F32 = jnp.float32
BF16 = jnp.bfloat16
VMEM_LIMIT = 16 * 1024 * 1024


def weight(microseconds):
    return pl.CostEstimate(
        flops=int(microseconds * 1.15e9), bytes_accessed=0, transcendentals=0
    )


def traffic(microseconds):
    return pl.CostEstimate(
        flops=0, bytes_accessed=int(microseconds * 3.69e6), transcendentals=0
    )


def dot(a, b):
    return jnp.dot(a, b, preferred_element_type=F32)


def normalize_halves(own, other, gain_own, gain_other):
    width = own.shape[1] + other.shape[1]
    mean = (
        jnp.sum(own, axis=1, keepdims=True) + jnp.sum(other, axis=1, keepdims=True)
    ) / width
    own = own - mean
    other = other - mean
    spread = (
        jnp.sum(own * own, axis=1, keepdims=True) + jnp.sum(other * other, axis=1, keepdims=True)
    ) / width
    scale = lax.rsqrt(spread + 1e-05)
    return (own * scale * gain_own).astype(BF16), (other * scale * gain_other).astype(BF16)


def qkv_kernel(
    meta, own_ref, other_ref, gain_ref, w_ref, _, keep_ref, query_ref, send_ref, pass_ref
):
    h = meta[0]
    first = meta[1] == 0
    rows = own_ref.shape[0]
    tile = 256
    for at in range(0, rows, tile):
        here = slice(at, at + tile)
        n_own, n_other = normalize_halves(
            own_ref[here, :].astype(F32), other_ref[here, :].astype(F32),
            gain_ref[h], gain_ref[1 - h],
        )
        for slot, part in enumerate((1, 2, 0)):
            value = (dot(n_own, w_ref[part, h]) + dot(n_other, w_ref[part, 1 - h])).astype(BF16)
            sub = value.shape[1] // 2
            cols = slice(slot * sub, slot * sub + sub)
            keep = jnp.where(first, value[:, :sub], value[:, sub:])
            send = jnp.where(first, value[:, sub:], value[:, :sub])
            send_ref[here, cols] = send
            if slot < 2:
                keep_ref[here, cols] = keep
                pass_ref[here, cols] = send
            else:
                query_ref[here, :] = keep


def project(meta, frames, other, gain, qkv, early):
    rows, half = frames.shape
    width = qkv.shape[2]
    vmem = pl.BlockSpec(memory_space=pltpu.VMEM)
    return pl.pallas_call(
        qkv_kernel,
        in_specs=[pl.BlockSpec(memory_space=pltpu.SMEM)]
        + [vmem] * 4
        + [pl.BlockSpec(memory_space=pl.ANY)],
        out_specs=[vmem] * 4,
        out_shape=[
            jax.ShapeDtypeStruct((rows, width), BF16),
            jax.ShapeDtypeStruct((rows, width // 2), BF16),
            jax.ShapeDtypeStruct((rows, 3 * width // 2), BF16),
            jax.ShapeDtypeStruct((rows, width), BF16),
        ],
        compiler_params=pltpu.CompilerParams(vmem_limit_bytes=VMEM_LIMIT),
        name="project",
    )(meta, frames, other, gain.reshape(2, 1, half),
      qkv.transpose(1, 0, 2).reshape(3, 2, half, width), early)


def bounds_kernel(meta, counts, valid, own_ref, pair_ref):
    utts = valid.shape[1]
    rows = own_ref.shape[0]
    square = (utts, utts)
    sub = lax.broadcasted_iota(jnp.int32, square, 0)
    lane = lax.broadcasted_iota(jnp.int32, square, 1)
    total = jnp.sum(counts[...].astype(F32), axis=0, keepdims=True)
    limit = jnp.broadcast_to(jnp.minimum(total, valid[...].astype(F32)), square)
    total = jnp.broadcast_to(total, square)
    start = jnp.sum(jnp.where(lane < sub, total, 0.0), axis=1, keepdims=True)
    stop = start + jnp.sum(jnp.where(lane == sub, limit, 0.0), axis=1, keepdims=True)
    at = lax.broadcasted_iota(jnp.int32, (utts, rows), 1).astype(F32)
    for slot, ref in enumerate((own_ref, pair_ref)):
        origin = meta[2 + slot].astype(F32)
        lo = start - origin
        hi = stop - origin
        inside = (at >= lo) & (at < hi)
        low = jnp.sum(jnp.where(inside, lo, 0.0), axis=0, keepdims=True)
        high = jnp.sum(jnp.where(inside, hi, 0.0), axis=0, keepdims=True)
        both = jnp.concatenate([low, high, jnp.zeros((126, rows), F32)], axis=0)
        ref[...] = both.T.astype(jnp.int32)


def bounds(meta, counts, valid, rows):
    vmem = pl.BlockSpec(memory_space=pltpu.VMEM)
    return pl.pallas_call(
        bounds_kernel,
        in_specs=[pl.BlockSpec(memory_space=pltpu.SMEM), vmem, vmem],
        out_specs=[vmem] * 2,
        out_shape=[jax.ShapeDtypeStruct((rows, 128), jnp.int32)] * 2,
        compiler_params=pltpu.CompilerParams(vmem_limit_bytes=VMEM_LIMIT),
        name="bounds",
    )(meta, counts, valid.reshape(1, -1))


def attend_kernel(a_high, query, center, side_a, side_b, run_ref, out_ref):
    rows = center.shape[0]
    width = center.shape[1] // 2 if query.shape[1] < center.shape[1] else center.shape[1] // 3
    q_cols = slice(query.shape[1] - width, query.shape[1])
    tile = rows // 2
    lane = lax.broadcasted_iota(jnp.int32, (tile, width), 1)

    def run(low_ref, high_ref):
        for block in range(2):
            at = block * tile
            pieces = (
                ((low_ref, 0, rows, -rows), (center, 0, rows, 0), (high_ref, 0, tile, rows))
                if block == 0
                else ((low_ref, tile, tile, -rows), (center, 0, rows, 0), (high_ref, 0, rows, rows))
            )
            position = lax.broadcasted_iota(jnp.int32, (tile, 1), 0) + at
            lo = run_ref[at : at + tile, 0:1]
            hi = run_ref[at : at + tile, 1:2]
            near_lo = jnp.maximum(lo, position - WIN)
            near_hi = jnp.minimum(hi, position + (WIN + 1))
            biases = []
            for _, first, size, origin in pieces:
                u = lax.broadcasted_iota(jnp.int32, (tile, size), 1) + (origin + first)
                biases.append(jnp.where((u >= near_lo) & (u < near_hi), 0.0, NEG))
            q = query[at : at + tile, q_cols]
            outs = []
            for sub in range(2):
                q_sub = jnp.where((lane >= HEAD_DIM) == (sub == 1), q, jnp.zeros_like(q))
                scores = []
                for (ref, first, size, _), bias in zip(pieces, biases):
                    s = lax.dot_general(
                        q_sub, ref[first : first + size, :width], (((1,), (1,)), ((), ())),
                        preferred_element_type=F32,
                    )
                    scores.append(s + bias)
                peak = functools.reduce(
                    jnp.maximum, [jnp.max(s, axis=1, keepdims=True) for s in scores]
                )
                total = jnp.zeros((tile, 1), F32)
                context = jnp.zeros((tile, width), F32)
                for (ref, first, size, _), s in zip(pieces, scores):
                    expw = jnp.exp2((s - peak) * EXP_SCALE)
                    total = total + jnp.sum(expw, axis=1, keepdims=True)
                    context = context + dot(
                        expw.astype(BF16), ref[first : first + size, width : 2 * width]
                    )
                outs.append(context / jnp.maximum(total, 1.0))
            joined = jnp.where(lane >= HEAD_DIM, outs[1], outs[0])
            out_ref[at : at + tile, :] = jnp.where(hi > lo, joined, 0.0).astype(BF16)

    @pl.when(a_high[0] == 1)
    def _():
        run(side_b, side_a)

    @pl.when(a_high[0] == 0)
    def _():
        run(side_a, side_b)


def attend(a_high, query, center, side_a, side_b, runs):
    rows, width = side_b.shape[0], side_b.shape[1] // 2
    vmem = pl.BlockSpec(memory_space=pltpu.VMEM)
    return pl.pallas_call(
        attend_kernel,
        in_specs=[pl.BlockSpec(memory_space=pltpu.SMEM)] + [vmem] * 5,
        out_specs=vmem,
        out_shape=jax.ShapeDtypeStruct((rows, width), BF16),
        compiler_params=pltpu.CompilerParams(vmem_limit_bytes=VMEM_LIMIT),
        cost_estimate=traffic(3),
        name="attend",
    )(a_high, query, center, side_a, side_b, runs)


def gate_kernel(
    meta,
    mine_own, pair_own, mine_other, pair_other,
    x_own, x_other,
    out_own, out_other,
    gain_ref,
    in_own, in_other,
    run_ref,
    glu_ref, edge_ref, mid_keep, mid_send,
):
    h = meta[0]
    first = meta[1] == 0
    half = x_own.shape[1]
    rows = glu_ref.shape[0]
    here = pl.ds(pl.multiple_of(h * (rows - 2 * EDGE), EDGE), rows)

    def joined(mine, pair):
        mine = mine[here, :]
        pair = pair[here, :]
        return jnp.concatenate(
            [jnp.where(first, mine, pair), jnp.where(first, pair, mine)], axis=1
        )

    depth = 2 * mine_own.shape[1]
    c_own = joined(mine_own, pair_own)
    c_other = joined(mine_other, pair_other)
    own_cols = pl.ds(pl.multiple_of(h * half, half), half)
    other_cols = pl.ds(pl.multiple_of((1 - h) * half, half), half)

    def mid(cols, x_ref):
        first = dot(c_own, out_own[:depth, cols]).astype(BF16).astype(F32)
        second = dot(c_other, out_other[:depth, cols]).astype(BF16).astype(F32)
        return (x_ref[here, :].astype(F32) + (first + second)).astype(BF16)

    m_own = mid(own_cols, x_own)
    m_other = mid(other_cols, x_other)
    keep = rows - EDGE

    @pl.when(h == 0)
    def _():
        mid_keep[...] = m_own[:keep]
        mid_send[...] = m_other[:keep]

    @pl.when(h == 1)
    def _():
        mid_keep[...] = m_own[EDGE:]
        mid_send[...] = m_other[EDGE:]

    n_own, n_other = normalize_halves(
        m_own.astype(F32), m_other.astype(F32), gain_ref[h], gain_ref[1 - h]
    )
    run = run_ref[here, :]
    valid = run[:, 1:2] > run[:, 0:1]
    glus = []
    for w_ref in (in_own, in_other):
        value = dot(n_own, w_ref[0, own_cols, :]) + dot(n_other, w_ref[0, other_cols, :])
        gate = dot(n_own, w_ref[1, own_cols, :]) + dot(n_other, w_ref[1, other_cols, :])
        glu = value / (1.0 + jnp.exp(-gate))
        glus.append(jnp.where(valid, glu, 0.0).astype(BF16))
    chan = glus[0].shape[1]
    glu_ref[:, :chan] = glus[0]
    glu_ref[:, chan:] = glus[1]

    @pl.when(h == 0)
    def _():
        edge_ref[:, :chan] = glus[1][:SENT]
        edge_ref[:, chan:] = glus[0][:SENT]

    @pl.when(h == 1)
    def _():
        edge_ref[:, :chan] = glus[1][rows - SENT :]
        edge_ref[:, chan:] = glus[0][rows - SENT :]


def gated(meta, contexts, x_own, x_other, out_own, out_other, gain, in_own, in_other, runs):
    rows = x_own.shape[0] // 2 + EDGE
    half = x_own.shape[1]
    chan = in_own.shape[2]
    vmem = pl.BlockSpec(memory_space=pltpu.VMEM)
    return pl.pallas_call(
        gate_kernel,
        in_specs=[pl.BlockSpec(memory_space=pltpu.SMEM)] + [vmem] * 12,
        out_specs=[vmem] * 4,
        out_shape=[
            jax.ShapeDtypeStruct((rows, 2 * chan), BF16),
            jax.ShapeDtypeStruct((SENT, 2 * chan), BF16),
            jax.ShapeDtypeStruct((rows - EDGE, half), BF16),
            jax.ShapeDtypeStruct((rows - EDGE, half), BF16),
        ],
        compiler_params=pltpu.CompilerParams(vmem_limit_bytes=VMEM_LIMIT),
        cost_estimate=traffic(3),
        name="gated",
    )(meta, *contexts, x_own, x_other, out_own, out_other,
      gain.reshape(2, 1, half), in_own, in_other, runs)


def conv_rows(shifted, low, high, taps, out_ref, rows):
    width = out_ref.shape[1]
    chan = width // 2
    reach = KERNEL // 2
    step = min(32, rows)
    cols = range(0, width, 128)
    weights = [
        [
            (taps[0] if col < chan else taps[1])[tap : tap + 1, col % chan : col % chan + 128]
            for col in cols
        ]
        for tap in range(KERNEL + 1)
    ]
    for base in range(0, rows, step):
        totals = [jnp.zeros((step, 128), F32) for _ in cols]
        for tap in range(KERNEL):
            shift = tap - reach
            same = (low[base : base + step] <= shift) & (high[base : base + step] > shift)
            row = base + EDGE + shift
            first = row - row % 8
            for index, col in enumerate(cols):
                piece = shifted[row % 8, first : first + step, col : col + 128]
                totals[index] = totals[index] + jnp.where(same, piece, 0.0) * weights[tap][index]
        mean = jnp.sum(sum(totals), axis=1, keepdims=True) / CONV_CH
        square = jnp.sum(sum(t * t for t in totals), axis=1, keepdims=True) / CONV_CH
        scale = lax.rsqrt(square - mean * mean + 1e-05)
        for index, col in enumerate(cols):
            y = (totals[index] - mean) * scale * weights[KERNEL][index]
            out_ref[base : base + step, col : col + 128] = (y / (1.0 + jnp.exp(-y))).astype(BF16)


def run_offsets(run_ref, first, rows):
    run = run_ref[pl.ds(first, rows), :]
    at = lax.broadcasted_iota(jnp.int32, (rows, 128), 0) + first
    low = jnp.broadcast_to(run[:, 0:1], (rows, 128)) - at
    high = jnp.broadcast_to(run[:, 1:2], (rows, 128)) - at
    return low, high


def conv_kernel(meta, glu_ref, run_ref, taps_own, taps_other, act_ref, ext, shifted):
    h = meta[0]
    rows, width = act_ref.shape
    got = glu_ref.shape[0]
    ext[pl.ds(pl.multiple_of(h * got, EDGE), EDGE), :] = jnp.zeros((EDGE, width), F32)
    ext[pl.ds(pl.multiple_of((1 - h) * EDGE, EDGE), got), :] = glu_ref[...].astype(F32)
    size = shifted.shape[1]
    for s in range(8):
        shifted[s] = ext[s : s + size, :]
    low, high = run_offsets(run_ref, pl.multiple_of(h * rows, rows), rows)
    conv_rows(shifted, low, high, (taps_own, taps_other), act_ref, rows)


def convolve(meta, glu, runs, taps_own, taps_other):
    rows = glu.shape[0] - EDGE
    width = glu.shape[1]
    vmem = pl.BlockSpec(memory_space=pltpu.VMEM)
    return pl.pallas_call(
        conv_kernel,
        in_specs=[pl.BlockSpec(memory_space=pltpu.SMEM)] + [vmem] * 4,
        out_specs=vmem,
        out_shape=jax.ShapeDtypeStruct((rows, width), BF16),
        scratch_shapes=[
            pltpu.VMEM((rows + 2 * EDGE, width), F32),
            pltpu.VMEM((8, rows + 2 * EDGE - 8, width), F32),
        ],
        compiler_params=pltpu.CompilerParams(vmem_limit_bytes=VMEM_LIMIT),
        cost_estimate=weight(3),
        name="convolve",
    )(meta, glu, runs, taps_own, taps_other)


def rim_kernel(meta, glu_ref, edge_ref, run_ref, taps_own, taps_other, act_ref, ext, shifted):
    h = meta[0]
    got = glu_ref.shape[0]
    near = 2 * EDGE
    ext[pl.ds(pl.multiple_of(h * near, EDGE), EDGE), :] = edge_ref[
        pl.ds(pl.multiple_of((1 - h) * (SENT - EDGE), EDGE), EDGE), :
    ].astype(F32)
    ext[pl.ds(pl.multiple_of((1 - h) * EDGE, EDGE), near), :] = glu_ref[
        pl.ds(pl.multiple_of(h * (got - near), EDGE), near), :
    ].astype(F32)
    size = shifted.shape[1]
    for s in range(8):
        shifted[s] = ext[s : s + size, :]
    first = pl.multiple_of(h * (run_ref.shape[0] - EDGE), EDGE)
    low, high = run_offsets(run_ref, first, EDGE)
    conv_rows(shifted, low, high, (taps_own, taps_other), act_ref, EDGE)


def rim(meta, glu, edge, runs, taps_own, taps_other):
    width = glu.shape[1]
    vmem = pl.BlockSpec(memory_space=pltpu.VMEM)
    return pl.pallas_call(
        rim_kernel,
        in_specs=[pl.BlockSpec(memory_space=pltpu.SMEM)] + [vmem] * 5,
        out_specs=vmem,
        out_shape=jax.ShapeDtypeStruct((EDGE, width), BF16),
        scratch_shapes=[
            pltpu.VMEM((3 * EDGE, width), F32),
            pltpu.VMEM((8, 3 * EDGE - 8, width), F32),
        ],
        compiler_params=pltpu.CompilerParams(vmem_limit_bytes=VMEM_LIMIT),
        cost_estimate=weight(1),
        name="rim",
    )(meta, glu, edge, runs, taps_own, taps_other)


def last_product(act_ref, rim_ref, rim_at, mid_ref, w_first, w_second, cols, act):
    chan = act_ref.shape[1] // 2
    act[...] = act_ref[...]
    act[pl.ds(rim_at, EDGE), :] = rim_ref[...]
    below = w_first.shape[0] - chan
    first = dot(act[:, :chan], w_first[below:, cols]).astype(BF16).astype(F32)
    second = dot(act[:, chan:], w_second[below:, cols]).astype(BF16).astype(F32)
    return (mid_ref[...].astype(F32) + (first + second)).astype(BF16)


def finish_own_kernel(meta, act_ref, rim_ref, mid_ref, w_own, w_other, out_ref, act):
    h = meta[0]
    rows, half = out_ref.shape
    out_ref[...] = last_product(
        act_ref, rim_ref, pl.multiple_of(h * (rows - EDGE), EDGE), mid_ref, w_own, w_other,
        pl.ds(pl.multiple_of(h * half, half), half), act,
    )


def finish_kernel(meta, act_ref, rim_ref, mid_ref, w_own, w_other, done_ref, out_ref, act):
    h = meta[0]
    rows, half = done_ref.shape
    out_ref[pl.ds(pl.multiple_of(h * rows, rows), rows), :] = done_ref[...]
    out_ref[pl.ds(pl.multiple_of((1 - h) * rows, rows), rows), :] = last_product(
        act_ref, rim_ref, pl.multiple_of((1 - h) * (rows - EDGE), EDGE), mid_ref, w_other, w_own,
        pl.ds(pl.multiple_of(h * half, half), half), act,
    )


def finish(meta, act, rim_act, mid, w_own, w_other, done=None):
    rows, half = mid.shape
    vmem = pl.BlockSpec(memory_space=pltpu.VMEM)
    args = (act, rim_act, mid, w_own, w_other) + (() if done is None else (done,))
    return pl.pallas_call(
        finish_own_kernel if done is None else finish_kernel,
        in_specs=[pl.BlockSpec(memory_space=pltpu.SMEM)] + [vmem] * len(args),
        out_specs=vmem,
        out_shape=jax.ShapeDtypeStruct((rows if done is None else 2 * rows, half), BF16),
        scratch_shapes=[pltpu.VMEM(act.shape, BF16)],
        compiler_params=pltpu.CompilerParams(vmem_limit_bytes=VMEM_LIMIT),
        cost_estimate=weight(1.2),
        name="finish_own" if done is None else "finish",
    )(meta, *args)


def local(
    blocks,
    frames,
    segment_ids,
    utt_valid,
    attn_gain,
    qkv_weight,
    out_weight,
    conv_gain,
    pointwise_in,
    depthwise,
    mid_gain,
    pointwise_out,
):
    rows = frames.shape[0]

    def swap(value):
        return lax.ppermute(value, "head", [(0, 1), (1, 0)])

    def shift(value, step):
        pairs = [(i, i - step if i % 2 == 0 else i + step) for i in range(blocks)]
        return lax.ppermute(value, "tm", [p for p in pairs if 0 <= p[1] < blocks])

    def exchange(value):
        return lax.ppermute(value, "tm", [(i, i ^ 1) for i in range(blocks)])

    block = lax.axis_index("tm").astype(jnp.int32)
    column = block % 2
    meta = jnp.stack([
        lax.axis_index("head").astype(jnp.int32),
        column,
        block * rows,
        (block + 1 - 2 * column) * rows,
    ])
    other = swap(frames)
    pointwise = pointwise_in.transpose(1, 0, 2)
    keep, query, send, passed = project(
        meta, frames, other, attn_gain, qkv_weight, pointwise
    )
    far_own = shift(passed, 1)
    pair = exchange(send)
    far_pair = shift(keep, 2)

    segment_ids, _ = lax.optimization_barrier((segment_ids, passed))
    ids = jnp.arange(utt_valid.shape[0], dtype=jnp.int32)
    counts = jnp.sum((segment_ids[None, :] == ids[:, None]).astype(jnp.int32), axis=1)
    counts = lax.all_to_all(
        jnp.broadcast_to(counts[None, :], (blocks, counts.shape[0])), "tm", 0, 0
    )
    taps = jnp.concatenate([depthwise, mid_gain[None, :]], axis=0)
    out_weight, pointwise, taps, keep = lax.optimization_barrier(
        (out_weight, pointwise, taps, keep)
    )
    pointwise_other = swap(pointwise)
    out_other = swap(out_weight)
    runs, pair_runs = bounds(meta, counts, utt_valid, rows)
    taps, pointwise_out, runs = lax.optimization_barrier((taps, pointwise_out, runs))
    taps_other = swap(taps)
    pointwise_out_other = swap(pointwise_out)
    pair, far_pair, far_own, runs, pair_runs = lax.optimization_barrier(
        (pair, far_pair, far_own, runs, pair_runs)
    )
    pair_context = attend(column.reshape(1), pair, pair, keep, far_pair, pair_runs)
    pair_context = exchange(pair_context)
    context = attend((1 - column).reshape(1), query, keep, pair, far_own, runs)
    contexts = (context, pair_context, swap(context), swap(pair_context))
    glu, edge, mid_keep, mid_send = gated(
        meta, contexts, frames, other, out_weight, out_other, conv_gain,
        pointwise, pointwise_other, runs,
    )
    edges = [(2 * i, 2 * (i - 1) + 1) for i in range(1, blocks)]
    edges += [(2 * i + 1, 2 * (i + 1)) for i in range(blocks - 1)]
    edge = lax.ppermute(edge, ("tm", "head"), edges)
    mid_other = swap(mid_send)
    act = convolve(meta, glu, runs, taps, taps_other)
    act_other = swap(act)
    rim_act = rim(meta, glu, edge, runs, taps, taps_other)
    rim_other = swap(rim_act)
    done = finish(meta, act, rim_act, mid_keep, pointwise_out, pointwise_out_other)
    return finish(
        meta, act_other, rim_other, mid_other, pointwise_out, pointwise_out_other, done
    )


def solution(mesh):
    in_specs = (
        P(("grp", "tm"), "head"),
        P(("grp", "tm")),
        P("grp"),
        P(),
        P(None, None, "head"),
        P("head", None),
        P(),
        P(None, None, "head"),
        P(None, "head"),
        P("head"),
        P("head", None),
    )
    out_specs = P(("grp", "tm"), "head")
    return jax.shard_map(
        functools.partial(local, mesh.shape["tm"]),
        mesh=mesh,
        in_specs=in_specs,
        out_specs=out_specs,
        check_vma=False,
    )
```

```python
import functools
import math

import jax
import jax.numpy as jnp
from jax import lax
from jax.experimental import pallas as pl
from jax.experimental.pallas import tpu as pltpu
from jax.sharding import PartitionSpec as P

HEAD_DIM = 64
CONV_CH = 512
KERNEL = 31
WIN = 512
EDGE = 16
SENT = 64
NEG = -1e30
EXP_SCALE = HEAD_DIM ** (-0.5) * math.log2(math.e)
F32 = jnp.float32
BF16 = jnp.bfloat16
VMEM_LIMIT = 16 * 1024 * 1024


def weight(microseconds):
    return pl.CostEstimate(
        flops=int(microseconds * 1.15e9), bytes_accessed=0, transcendentals=0
    )


def traffic(microseconds):
    return pl.CostEstimate(
        flops=0, bytes_accessed=int(microseconds * 3.69e6), transcendentals=0
    )


def dot(a, b):
    return jnp.dot(a, b, preferred_element_type=F32)


def normalize_halves(own, other, gain_own, gain_other):
    width = own.shape[1] + other.shape[1]
    mean = (
        jnp.sum(own, axis=1, keepdims=True) + jnp.sum(other, axis=1, keepdims=True)
    ) / width
    own = own - mean
    other = other - mean
    spread = (
        jnp.sum(own * own, axis=1, keepdims=True) + jnp.sum(other * other, axis=1, keepdims=True)
    ) / width
    scale = lax.rsqrt(spread + 1e-05)
    return (own * scale * gain_own).astype(BF16), (other * scale * gain_other).astype(BF16)


def qkv_kernel(
    meta, own_ref, other_ref, gain_ref, w_ref, _, keep_ref, query_ref, send_ref, pass_ref
):
    h = meta[0]
    first = meta[1] == 0
    rows = own_ref.shape[0]
    tile = 256
    for at in range(0, rows, tile):
        here = slice(at, at + tile)
        n_own, n_other = normalize_halves(
            own_ref[here, :].astype(F32), other_ref[here, :].astype(F32),
            gain_ref[h], gain_ref[1 - h],
        )
        for slot, part in enumerate((1, 2, 0)):
            value = (dot(n_own, w_ref[part, h]) + dot(n_other, w_ref[part, 1 - h])).astype(BF16)
            sub = value.shape[1] // 2
            cols = slice(slot * sub, slot * sub + sub)
            keep = jnp.where(first, value[:, :sub], value[:, sub:])
            send = jnp.where(first, value[:, sub:], value[:, :sub])
            send_ref[here, cols] = send
            if slot < 2:
                keep_ref[here, cols] = keep
                pass_ref[here, cols] = send
            else:
                query_ref[here, :] = keep


def project(meta, frames, other, gain, qkv, early):
    rows, half = frames.shape
    width = qkv.shape[2]
    vmem = pl.BlockSpec(memory_space=pltpu.VMEM)
    return pl.pallas_call(
        qkv_kernel,
        in_specs=[pl.BlockSpec(memory_space=pltpu.SMEM)]
        + [vmem] * 4
        + [pl.BlockSpec(memory_space=pl.ANY)],
        out_specs=[vmem] * 4,
        out_shape=[
            jax.ShapeDtypeStruct((rows, width), BF16),
            jax.ShapeDtypeStruct((rows, width // 2), BF16),
            jax.ShapeDtypeStruct((rows, 3 * width // 2), BF16),
            jax.ShapeDtypeStruct((rows, width), BF16),
        ],
        compiler_params=pltpu.CompilerParams(vmem_limit_bytes=VMEM_LIMIT),
        name="project",
    )(meta, frames, other, gain.reshape(2, 1, half),
      qkv.transpose(1, 0, 2).reshape(3, 2, half, width), early)


def bounds_kernel(meta, counts, valid, *refs):
    own_ref, pair_ref = refs[-2:]
    utts = valid.shape[1]
    rows = own_ref.shape[0]
    square = (utts, utts)
    sub = lax.broadcasted_iota(jnp.int32, square, 0)
    lane = lax.broadcasted_iota(jnp.int32, square, 1)
    total = jnp.sum(counts[...].astype(F32), axis=0, keepdims=True)
    limit = jnp.broadcast_to(jnp.minimum(total, valid[...].astype(F32)), square)
    total = jnp.broadcast_to(total, square)
    start = jnp.sum(jnp.where(lane < sub, total, 0.0), axis=1, keepdims=True)
    stop = start + jnp.sum(jnp.where(lane == sub, limit, 0.0), axis=1, keepdims=True)
    at = lax.broadcasted_iota(jnp.int32, (utts, rows), 1).astype(F32)
    for slot, ref in enumerate((own_ref, pair_ref)):
        origin = meta[2 + slot].astype(F32)
        lo = start - origin
        hi = stop - origin
        inside = (at >= lo) & (at < hi)
        low = jnp.sum(jnp.where(inside, lo, 0.0), axis=0, keepdims=True)
        high = jnp.sum(jnp.where(inside, hi, 0.0), axis=0, keepdims=True)
        both = jnp.concatenate([low, high, jnp.zeros((126, rows), F32)], axis=0)
        ref[...] = both.T.astype(jnp.int32)


def bounds(meta, counts, valid, rows, held):
    vmem = pl.BlockSpec(memory_space=pltpu.VMEM)
    anywhere = [pl.BlockSpec(memory_space=pl.ANY)] * len(held)
    return pl.pallas_call(
        bounds_kernel,
        in_specs=[pl.BlockSpec(memory_space=pltpu.SMEM), vmem, vmem] + anywhere,
        out_specs=[vmem] * 2,
        out_shape=[jax.ShapeDtypeStruct((rows, 128), jnp.int32)] * 2,
        compiler_params=pltpu.CompilerParams(vmem_limit_bytes=VMEM_LIMIT),
        name="bounds",
    )(meta, counts, valid.reshape(1, -1), *held)


def attend_kernel(a_high, query, center, side_a, side_b, run_ref, *refs):
    out_ref = refs[-1]
    rows = center.shape[0]
    width = center.shape[1] // 2 if query.shape[1] < center.shape[1] else center.shape[1] // 3
    q_cols = slice(query.shape[1] - width, query.shape[1])
    tile = rows // 2
    lane = lax.broadcasted_iota(jnp.int32, (tile, width), 1)

    def run(low_ref, high_ref):
        for block in range(2):
            at = block * tile
            pieces = (
                ((low_ref, 0, rows, -rows), (center, 0, rows, 0), (high_ref, 0, tile, rows))
                if block == 0
                else ((low_ref, tile, tile, -rows), (center, 0, rows, 0), (high_ref, 0, rows, rows))
            )
            position = lax.broadcasted_iota(jnp.int32, (tile, 1), 0) + at
            lo = run_ref[at : at + tile, 0:1]
            hi = run_ref[at : at + tile, 1:2]
            near_lo = jnp.maximum(lo, position - WIN)
            near_hi = jnp.minimum(hi, position + (WIN + 1))
            biases = []
            for _, first, size, origin in pieces:
                u = lax.broadcasted_iota(jnp.int32, (tile, size), 1) + (origin + first)
                biases.append(jnp.where((u >= near_lo) & (u < near_hi), 0.0, NEG))
            q = query[at : at + tile, q_cols]
            outs = []
            for sub in range(2):
                q_sub = jnp.where((lane >= HEAD_DIM) == (sub == 1), q, jnp.zeros_like(q))
                scores = []
                for (ref, first, size, _), bias in zip(pieces, biases):
                    s = lax.dot_general(
                        q_sub, ref[first : first + size, :width], (((1,), (1,)), ((), ())),
                        preferred_element_type=F32,
                    )
                    scores.append(s + bias)
                peak = functools.reduce(
                    jnp.maximum, [jnp.max(s, axis=1, keepdims=True) for s in scores]
                )
                total = jnp.zeros((tile, 1), F32)
                context = jnp.zeros((tile, width), F32)
                for (ref, first, size, _), s in zip(pieces, scores):
                    expw = jnp.exp2((s - peak) * EXP_SCALE)
                    total = total + jnp.sum(expw, axis=1, keepdims=True)
                    context = context + dot(
                        expw.astype(BF16), ref[first : first + size, width : 2 * width]
                    )
                outs.append(context / jnp.maximum(total, 1.0))
            joined = jnp.where(lane >= HEAD_DIM, outs[1], outs[0])
            out_ref[at : at + tile, :] = jnp.where(hi > lo, joined, 0.0).astype(BF16)

    @pl.when(a_high[0] == 1)
    def _():
        run(side_b, side_a)

    @pl.when(a_high[0] == 0)
    def _():
        run(side_a, side_b)


def attend(a_high, query, center, side_a, side_b, runs, held):
    anywhere = [pl.BlockSpec(memory_space=pl.ANY)] * len(held)
    rows, width = side_b.shape[0], side_b.shape[1] // 2
    vmem = pl.BlockSpec(memory_space=pltpu.VMEM)
    return pl.pallas_call(
        attend_kernel,
        in_specs=[pl.BlockSpec(memory_space=pltpu.SMEM)] + [vmem] * 5 + anywhere,
        out_specs=vmem,
        out_shape=jax.ShapeDtypeStruct((rows, width), BF16),
        compiler_params=pltpu.CompilerParams(vmem_limit_bytes=VMEM_LIMIT),
        cost_estimate=traffic(3),
        name="attend",
    )(a_high, query, center, side_a, side_b, runs, *held)


def gate_kernel(
    meta,
    mine_own, pair_own, mine_other, pair_other,
    x_own, x_other,
    out_own, out_other,
    gain_ref,
    in_own, in_other,
    run_ref,
    glu_ref, edge_ref, mid_keep, mid_send,
):
    h = meta[0]
    first = meta[1] == 0
    half = x_own.shape[1]
    rows = glu_ref.shape[0]
    here = pl.ds(pl.multiple_of(h * (rows - 2 * EDGE), EDGE), rows)

    def joined(mine, pair):
        mine = mine[here, :]
        pair = pair[here, :]
        return jnp.concatenate(
            [jnp.where(first, mine, pair), jnp.where(first, pair, mine)], axis=1
        )

    depth = 2 * mine_own.shape[1]
    c_own = joined(mine_own, pair_own)
    c_other = joined(mine_other, pair_other)
    own_cols = pl.ds(pl.multiple_of(h * half, half), half)
    other_cols = pl.ds(pl.multiple_of((1 - h) * half, half), half)

    def mid(cols, x_ref):
        first = dot(c_own, out_own[:depth, cols]).astype(BF16).astype(F32)
        second = dot(c_other, out_other[:depth, cols]).astype(BF16).astype(F32)
        return (x_ref[here, :].astype(F32) + (first + second)).astype(BF16)

    m_own = mid(own_cols, x_own)
    m_other = mid(other_cols, x_other)
    keep = rows - EDGE

    @pl.when(h == 0)
    def _():
        mid_keep[...] = m_own[:keep]
        mid_send[...] = m_other[:keep]

    @pl.when(h == 1)
    def _():
        mid_keep[...] = m_own[EDGE:]
        mid_send[...] = m_other[EDGE:]

    n_own, n_other = normalize_halves(
        m_own.astype(F32), m_other.astype(F32), gain_ref[h], gain_ref[1 - h]
    )
    run = run_ref[here, :]
    valid = run[:, 1:2] > run[:, 0:1]
    glus = []
    for w_ref in (in_own, in_other):
        value = dot(n_own, w_ref[0, own_cols, :]) + dot(n_other, w_ref[0, other_cols, :])
        gate = dot(n_own, w_ref[1, own_cols, :]) + dot(n_other, w_ref[1, other_cols, :])
        glu = value / (1.0 + jnp.exp(-gate))
        glus.append(jnp.where(valid, glu, 0.0).astype(BF16))
    chan = glus[0].shape[1]
    glu_ref[:, :chan] = glus[0]
    glu_ref[:, chan:] = glus[1]

    @pl.when(h == 0)
    def _():
        edge_ref[:, :chan] = glus[1][:SENT]
        edge_ref[:, chan:] = glus[0][:SENT]

    @pl.when(h == 1)
    def _():
        edge_ref[:, :chan] = glus[1][rows - SENT :]
        edge_ref[:, chan:] = glus[0][rows - SENT :]


def gated(meta, contexts, x_own, x_other, out_own, out_other, gain, in_own, in_other, runs):
    rows = x_own.shape[0] // 2 + EDGE
    half = x_own.shape[1]
    chan = in_own.shape[2]
    vmem = pl.BlockSpec(memory_space=pltpu.VMEM)
    return pl.pallas_call(
        gate_kernel,
        in_specs=[pl.BlockSpec(memory_space=pltpu.SMEM)] + [vmem] * 12,
        out_specs=[vmem] * 4,
        out_shape=[
            jax.ShapeDtypeStruct((rows, 2 * chan), BF16),
            jax.ShapeDtypeStruct((SENT, 2 * chan), BF16),
            jax.ShapeDtypeStruct((rows - EDGE, half), BF16),
            jax.ShapeDtypeStruct((rows - EDGE, half), BF16),
        ],
        compiler_params=pltpu.CompilerParams(vmem_limit_bytes=VMEM_LIMIT),
        cost_estimate=traffic(3),
        name="gated",
    )(meta, *contexts, x_own, x_other, out_own, out_other,
      gain.reshape(2, 1, half), in_own, in_other, runs)


def conv_rows(shifted, low, high, taps, out_ref, rows):
    width = out_ref.shape[1]
    chan = width // 2
    reach = KERNEL // 2
    step = min(32, rows)
    cols = range(0, width, 128)
    weights = [
        [
            (taps[0] if col < chan else taps[1])[tap : tap + 1, col % chan : col % chan + 128]
            for col in cols
        ]
        for tap in range(KERNEL + 1)
    ]
    for base in range(0, rows, step):
        totals = [jnp.zeros((step, 128), F32) for _ in cols]
        for tap in range(KERNEL):
            shift = tap - reach
            same = (low[base : base + step] <= shift) & (high[base : base + step] > shift)
            row = base + EDGE + shift
            first = row - row % 8
            for index, col in enumerate(cols):
                piece = shifted[row % 8, first : first + step, col : col + 128]
                totals[index] = totals[index] + jnp.where(same, piece, 0.0) * weights[tap][index]
        mean = jnp.sum(sum(totals), axis=1, keepdims=True) / CONV_CH
        square = jnp.sum(sum(t * t for t in totals), axis=1, keepdims=True) / CONV_CH
        scale = lax.rsqrt(square - mean * mean + 1e-05)
        for index, col in enumerate(cols):
            y = (totals[index] - mean) * scale * weights[KERNEL][index]
            out_ref[base : base + step, col : col + 128] = (y / (1.0 + jnp.exp(-y))).astype(BF16)


def run_offsets(run_ref, first, rows):
    run = run_ref[pl.ds(first, rows), :]
    at = lax.broadcasted_iota(jnp.int32, (rows, 128), 0) + first
    low = jnp.broadcast_to(run[:, 0:1], (rows, 128)) - at
    high = jnp.broadcast_to(run[:, 1:2], (rows, 128)) - at
    return low, high


def conv_kernel(meta, glu_ref, run_ref, taps_own, taps_other, act_ref, ext, shifted):
    h = meta[0]
    rows, width = act_ref.shape
    got = glu_ref.shape[0]
    ext[pl.ds(pl.multiple_of(h * got, EDGE), EDGE), :] = jnp.zeros((EDGE, width), F32)
    ext[pl.ds(pl.multiple_of((1 - h) * EDGE, EDGE), got), :] = glu_ref[...].astype(F32)
    size = shifted.shape[1]
    for s in range(8):
        shifted[s] = ext[s : s + size, :]
    low, high = run_offsets(run_ref, pl.multiple_of(h * rows, rows), rows)
    conv_rows(shifted, low, high, (taps_own, taps_other), act_ref, rows)


def convolve(meta, glu, runs, taps_own, taps_other):
    rows = glu.shape[0] - EDGE
    width = glu.shape[1]
    vmem = pl.BlockSpec(memory_space=pltpu.VMEM)
    return pl.pallas_call(
        conv_kernel,
        in_specs=[pl.BlockSpec(memory_space=pltpu.SMEM)] + [vmem] * 4,
        out_specs=vmem,
        out_shape=jax.ShapeDtypeStruct((rows, width), BF16),
        scratch_shapes=[
            pltpu.VMEM((rows + 2 * EDGE, width), F32),
            pltpu.VMEM((8, rows + 2 * EDGE - 8, width), F32),
        ],
        compiler_params=pltpu.CompilerParams(vmem_limit_bytes=VMEM_LIMIT),
        cost_estimate=weight(3),
        name="convolve",
    )(meta, glu, runs, taps_own, taps_other)


def rim_kernel(meta, glu_ref, edge_ref, run_ref, taps_own, taps_other, act_ref, ext, shifted):
    h = meta[0]
    got = glu_ref.shape[0]
    near = 2 * EDGE
    ext[pl.ds(pl.multiple_of(h * near, EDGE), EDGE), :] = edge_ref[
        pl.ds(pl.multiple_of((1 - h) * (SENT - EDGE), EDGE), EDGE), :
    ].astype(F32)
    ext[pl.ds(pl.multiple_of((1 - h) * EDGE, EDGE), near), :] = glu_ref[
        pl.ds(pl.multiple_of(h * (got - near), EDGE), near), :
    ].astype(F32)
    size = shifted.shape[1]
    for s in range(8):
        shifted[s] = ext[s : s + size, :]
    first = pl.multiple_of(h * (run_ref.shape[0] - EDGE), EDGE)
    low, high = run_offsets(run_ref, first, EDGE)
    conv_rows(shifted, low, high, (taps_own, taps_other), act_ref, EDGE)


def rim(meta, glu, edge, runs, taps_own, taps_other):
    width = glu.shape[1]
    vmem = pl.BlockSpec(memory_space=pltpu.VMEM)
    return pl.pallas_call(
        rim_kernel,
        in_specs=[pl.BlockSpec(memory_space=pltpu.SMEM)] + [vmem] * 5,
        out_specs=vmem,
        out_shape=jax.ShapeDtypeStruct((EDGE, width), BF16),
        scratch_shapes=[
            pltpu.VMEM((3 * EDGE, width), F32),
            pltpu.VMEM((8, 3 * EDGE - 8, width), F32),
        ],
        compiler_params=pltpu.CompilerParams(vmem_limit_bytes=VMEM_LIMIT),
        cost_estimate=weight(1),
        name="rim",
    )(meta, glu, edge, runs, taps_own, taps_other)


def last_product(act_ref, rim_ref, rim_at, mid_ref, w_first, w_second, cols, act):
    chan = act_ref.shape[1] // 2
    act[...] = act_ref[...]
    act[pl.ds(rim_at, EDGE), :] = rim_ref[...]
    below = w_first.shape[0] - chan
    first = dot(act[:, :chan], w_first[below:, cols]).astype(BF16).astype(F32)
    second = dot(act[:, chan:], w_second[below:, cols]).astype(BF16).astype(F32)
    return (mid_ref[...].astype(F32) + (first + second)).astype(BF16)


def finish_own_kernel(meta, act_ref, rim_ref, mid_ref, w_own, w_other, out_ref, act):
    h = meta[0]
    rows, half = out_ref.shape
    out_ref[...] = last_product(
        act_ref, rim_ref, pl.multiple_of(h * (rows - EDGE), EDGE), mid_ref, w_own, w_other,
        pl.ds(pl.multiple_of(h * half, half), half), act,
    )


def finish_kernel(meta, act_ref, rim_ref, mid_ref, w_own, w_other, done_ref, out_ref, act):
    h = meta[0]
    rows, half = done_ref.shape
    out_ref[pl.ds(pl.multiple_of(h * rows, rows), rows), :] = done_ref[...]
    out_ref[pl.ds(pl.multiple_of((1 - h) * rows, rows), rows), :] = last_product(
        act_ref, rim_ref, pl.multiple_of((1 - h) * (rows - EDGE), EDGE), mid_ref, w_other, w_own,
        pl.ds(pl.multiple_of(h * half, half), half), act,
    )


def finish(meta, act, rim_act, mid, w_own, w_other, done=None):
    rows, half = mid.shape
    vmem = pl.BlockSpec(memory_space=pltpu.VMEM)
    args = (act, rim_act, mid, w_own, w_other) + (() if done is None else (done,))
    return pl.pallas_call(
        finish_own_kernel if done is None else finish_kernel,
        in_specs=[pl.BlockSpec(memory_space=pltpu.SMEM)] + [vmem] * len(args),
        out_specs=vmem,
        out_shape=jax.ShapeDtypeStruct((rows if done is None else 2 * rows, half), BF16),
        scratch_shapes=[pltpu.VMEM(act.shape, BF16)],
        compiler_params=pltpu.CompilerParams(vmem_limit_bytes=VMEM_LIMIT),
        cost_estimate=weight(1.2),
        name="finish_own" if done is None else "finish",
    )(meta, *args)


def local(
    blocks,
    frames,
    segment_ids,
    utt_valid,
    attn_gain,
    qkv_weight,
    out_weight,
    conv_gain,
    pointwise_in,
    depthwise,
    mid_gain,
    pointwise_out,
):
    rows = frames.shape[0]

    def swap(value):
        return lax.ppermute(value, "head", [(0, 1), (1, 0)])

    def shift(value, step):
        pairs = [(i, i - step if i % 2 == 0 else i + step) for i in range(blocks)]
        return lax.ppermute(value, "tm", [p for p in pairs if 0 <= p[1] < blocks])

    def exchange(value):
        return lax.ppermute(value, "tm", [(i, i ^ 1) for i in range(blocks)])

    block = lax.axis_index("tm").astype(jnp.int32)
    column = block % 2
    meta = jnp.stack([
        lax.axis_index("head").astype(jnp.int32),
        column,
        block * rows,
        (block + 1 - 2 * column) * rows,
    ])
    other = swap(frames)
    pointwise = pointwise_in.transpose(1, 0, 2)
    keep, query, send, passed = project(
        meta, frames, other, attn_gain, qkv_weight, pointwise
    )
    far_own = shift(passed, 1)
    pair = exchange(send)
    far_pair = shift(keep, 2)

    segment_ids, _ = lax.optimization_barrier((segment_ids, passed))
    ids = jnp.arange(utt_valid.shape[0], dtype=jnp.int32)
    counts = jnp.sum((segment_ids[None, :] == ids[:, None]).astype(jnp.int32), axis=1)
    counts = lax.all_to_all(
        jnp.broadcast_to(counts[None, :], (blocks, counts.shape[0])), "tm", 0, 0
    )
    taps = jnp.concatenate([depthwise, mid_gain[None, :]], axis=0)
    out_weight, pointwise, taps, keep = lax.optimization_barrier(
        (out_weight, pointwise, taps, keep)
    )
    pointwise_other = swap(pointwise)
    out_other = swap(out_weight)
    runs, pair_runs = bounds(meta, counts, utt_valid, rows, (query,))
    taps, pointwise_out, runs = lax.optimization_barrier((taps, pointwise_out, runs))
    taps_other = swap(taps)
    pointwise_out_other = swap(pointwise_out)
    pair, far_pair, far_own, runs, pair_runs = lax.optimization_barrier(
        (pair, far_pair, far_own, runs, pair_runs)
    )
    weights = (pointwise_other, out_other)
    pair_context = attend(
        column.reshape(1), pair, pair, keep, far_pair, pair_runs, (query, far_own, *weights)
    )
    pair_context = exchange(pair_context)
    context = attend((1 - column).reshape(1), query, keep, pair, far_own, runs, weights)
    contexts = (context, pair_context, swap(context), swap(pair_context))
    glu, edge, mid_keep, mid_send = gated(
        meta, contexts, frames, other, out_weight, out_other, conv_gain,
        pointwise, pointwise_other, runs,
    )
    edges = [(2 * i, 2 * (i - 1) + 1) for i in range(1, blocks)]
    edges += [(2 * i + 1, 2 * (i + 1)) for i in range(blocks - 1)]
    edge = lax.ppermute(edge, ("tm", "head"), edges)
    mid_other = swap(mid_send)
    act = convolve(meta, glu, runs, taps, taps_other)
    act_other = swap(act)
    rim_act = rim(meta, glu, edge, runs, taps, taps_other)
    rim_other = swap(rim_act)
    done = finish(meta, act, rim_act, mid_keep, pointwise_out, pointwise_out_other)
    return finish(
        meta, act_other, rim_other, mid_other, pointwise_out, pointwise_out_other, done
    )


def solution(mesh):
    in_specs = (
        P(("grp", "tm"), "head"),
        P(("grp", "tm")),
        P("grp"),
        P(),
        P(None, None, "head"),
        P("head", None),
        P(),
        P(None, None, "head"),
        P(None, "head"),
        P("head"),
        P("head", None),
    )
    out_specs = P(("grp", "tm"), "head")
    return jax.shard_map(
        functools.partial(local, mesh.shape["tm"]),
        mesh=mesh,
        in_specs=in_specs,
        out_specs=out_specs,
        check_vma=False,
    )
```

```python
import functools
import math

import jax
import jax.numpy as jnp
from jax import lax
from jax.experimental import pallas as pl
from jax.experimental.pallas import tpu as pltpu
from jax.sharding import PartitionSpec as P

HEAD_DIM = 64
CONV_CH = 512
KERNEL = 31
WIN = 512
EDGE = 16
SENT = 64
NEG = -1e30
EXP_SCALE = HEAD_DIM ** (-0.5) * math.log2(math.e)
F32 = jnp.float32
BF16 = jnp.bfloat16
VMEM_LIMIT = 8 * 1024 * 1024


def weight(microseconds):
    return pl.CostEstimate(
        flops=int(microseconds * 1.15e9), bytes_accessed=0, transcendentals=0
    )


def traffic(microseconds):
    return pl.CostEstimate(
        flops=0, bytes_accessed=int(microseconds * 3.69e6), transcendentals=0
    )


def dot(a, b):
    return jnp.dot(a, b, preferred_element_type=F32)


def normalize_halves(own, other, gain_own, gain_other):
    width = own.shape[1] + other.shape[1]
    mean = (
        jnp.sum(own, axis=1, keepdims=True) + jnp.sum(other, axis=1, keepdims=True)
    ) / width
    own = own - mean
    other = other - mean
    spread = (
        jnp.sum(own * own, axis=1, keepdims=True) + jnp.sum(other * other, axis=1, keepdims=True)
    ) / width
    scale = lax.rsqrt(spread + 1e-05)
    return (own * scale * gain_own).astype(BF16), (other * scale * gain_other).astype(BF16)


def qkv_kernel(
    meta, own_ref, other_ref, gain_ref, w_ref, _, keep_ref, query_ref, send_ref, pass_ref
):
    h = meta[0]
    first = meta[1] == 0
    rows = own_ref.shape[0]
    tile = 256
    for at in range(0, rows, tile):
        here = slice(at, at + tile)
        n_own, n_other = normalize_halves(
            own_ref[here, :].astype(F32), other_ref[here, :].astype(F32),
            gain_ref[h], gain_ref[1 - h],
        )
        for slot, part in enumerate((1, 2, 0)):
            value = (dot(n_own, w_ref[part, h]) + dot(n_other, w_ref[part, 1 - h])).astype(BF16)
            sub = value.shape[1] // 2
            cols = slice(slot * sub, slot * sub + sub)
            keep = jnp.where(first, value[:, :sub], value[:, sub:])
            send = jnp.where(first, value[:, sub:], value[:, :sub])
            send_ref[here, cols] = send
            if slot < 2:
                keep_ref[here, cols] = keep
                pass_ref[here, cols] = send
            else:
                query_ref[here, :] = keep


def project(meta, frames, other, gain, qkv, early):
    rows, half = frames.shape
    width = qkv.shape[2]
    vmem = pl.BlockSpec(memory_space=pltpu.VMEM)
    return pl.pallas_call(
        qkv_kernel,
        in_specs=[pl.BlockSpec(memory_space=pltpu.SMEM)]
        + [vmem] * 4
        + [pl.BlockSpec(memory_space=pl.ANY)],
        out_specs=[vmem] * 4,
        out_shape=[
            jax.ShapeDtypeStruct((rows, width), BF16),
            jax.ShapeDtypeStruct((rows, width // 2), BF16),
            jax.ShapeDtypeStruct((rows, 3 * width // 2), BF16),
            jax.ShapeDtypeStruct((rows, width), BF16),
        ],
        compiler_params=pltpu.CompilerParams(vmem_limit_bytes=VMEM_LIMIT),
        name="project",
    )(meta, frames, other, gain.reshape(2, 1, half),
      qkv.transpose(1, 0, 2).reshape(3, 2, half, width), early)


def bounds_kernel(meta, counts, valid, *refs):
    own_ref, pair_ref = refs[-2:]
    utts = valid.shape[1]
    rows = own_ref.shape[0]
    square = (utts, utts)
    sub = lax.broadcasted_iota(jnp.int32, square, 0)
    lane = lax.broadcasted_iota(jnp.int32, square, 1)
    total = jnp.sum(counts[...].astype(F32), axis=0, keepdims=True)
    limit = jnp.broadcast_to(jnp.minimum(total, valid[...].astype(F32)), square)
    total = jnp.broadcast_to(total, square)
    start = jnp.sum(jnp.where(lane < sub, total, 0.0), axis=1, keepdims=True)
    stop = start + jnp.sum(jnp.where(lane == sub, limit, 0.0), axis=1, keepdims=True)
    at = lax.broadcasted_iota(jnp.int32, (utts, rows), 1).astype(F32)
    for slot, ref in enumerate((own_ref, pair_ref)):
        origin = meta[2 + slot].astype(F32)
        lo = start - origin
        hi = stop - origin
        inside = (at >= lo) & (at < hi)
        low = jnp.sum(jnp.where(inside, lo, 0.0), axis=0, keepdims=True)
        high = jnp.sum(jnp.where(inside, hi, 0.0), axis=0, keepdims=True)
        both = jnp.concatenate([low, high, jnp.zeros((126, rows), F32)], axis=0)
        ref[...] = both.T.astype(jnp.int32)


def bounds(meta, counts, valid, rows, held):
    vmem = pl.BlockSpec(memory_space=pltpu.VMEM)
    anywhere = [pl.BlockSpec(memory_space=pl.ANY)] * len(held)
    return pl.pallas_call(
        bounds_kernel,
        in_specs=[pl.BlockSpec(memory_space=pltpu.SMEM), vmem, vmem] + anywhere,
        out_specs=[vmem] * 2,
        out_shape=[jax.ShapeDtypeStruct((rows, 128), jnp.int32)] * 2,
        compiler_params=pltpu.CompilerParams(vmem_limit_bytes=VMEM_LIMIT),
        name="bounds",
    )(meta, counts, valid.reshape(1, -1), *held)


def attend_kernel(a_high, query, center, side_a, side_b, run_ref, *refs):
    out_ref = refs[-1]
    rows = center.shape[0]
    width = center.shape[1] // 2 if query.shape[1] < center.shape[1] else center.shape[1] // 3
    q_cols = slice(query.shape[1] - width, query.shape[1])
    tile = rows // 2
    lane = lax.broadcasted_iota(jnp.int32, (tile, width), 1)

    def run(low_ref, high_ref):
        for block in range(2):
            at = block * tile
            pieces = (
                ((low_ref, 0, rows, -rows), (center, 0, rows, 0), (high_ref, 0, tile, rows))
                if block == 0
                else ((low_ref, tile, tile, -rows), (center, 0, rows, 0), (high_ref, 0, rows, rows))
            )
            position = lax.broadcasted_iota(jnp.int32, (tile, 1), 0) + at
            lo = run_ref[at : at + tile, 0:1]
            hi = run_ref[at : at + tile, 1:2]
            near_lo = jnp.maximum(lo, position - WIN)
            near_hi = jnp.minimum(hi, position + (WIN + 1))
            biases = []
            for _, first, size, origin in pieces:
                u = lax.broadcasted_iota(jnp.int32, (tile, size), 1) + (origin + first)
                biases.append(jnp.where((u >= near_lo) & (u < near_hi), 0.0, NEG))
            q = query[at : at + tile, q_cols]
            outs = []
            for sub in range(2):
                q_sub = jnp.where((lane >= HEAD_DIM) == (sub == 1), q, jnp.zeros_like(q))
                scores = []
                for (ref, first, size, _), bias in zip(pieces, biases):
                    s = lax.dot_general(
                        q_sub, ref[first : first + size, :width], (((1,), (1,)), ((), ())),
                        preferred_element_type=F32,
                    )
                    scores.append(s + bias)
                peak = functools.reduce(
                    jnp.maximum, [jnp.max(s, axis=1, keepdims=True) for s in scores]
                )
                total = jnp.zeros((tile, 1), F32)
                context = jnp.zeros((tile, width), F32)
                for (ref, first, size, _), s in zip(pieces, scores):
                    expw = jnp.exp2((s - peak) * EXP_SCALE)
                    total = total + jnp.sum(expw, axis=1, keepdims=True)
                    context = context + dot(
                        expw.astype(BF16), ref[first : first + size, width : 2 * width]
                    )
                outs.append(context / jnp.maximum(total, 1.0))
            joined = jnp.where(lane >= HEAD_DIM, outs[1], outs[0])
            out_ref[at : at + tile, :] = jnp.where(hi > lo, joined, 0.0).astype(BF16)

    @pl.when(a_high[0] == 1)
    def _():
        run(side_b, side_a)

    @pl.when(a_high[0] == 0)
    def _():
        run(side_a, side_b)


def attend(a_high, query, center, side_a, side_b, runs, held):
    anywhere = [pl.BlockSpec(memory_space=pl.ANY)] * len(held)
    rows, width = side_b.shape[0], side_b.shape[1] // 2
    vmem = pl.BlockSpec(memory_space=pltpu.VMEM)
    return pl.pallas_call(
        attend_kernel,
        in_specs=[pl.BlockSpec(memory_space=pltpu.SMEM)] + [vmem] * 5 + anywhere,
        out_specs=vmem,
        out_shape=jax.ShapeDtypeStruct((rows, width), BF16),
        compiler_params=pltpu.CompilerParams(vmem_limit_bytes=VMEM_LIMIT),
        cost_estimate=traffic(3),
        name="attend",
    )(a_high, query, center, side_a, side_b, runs, *held)


def gate_kernel(
    meta,
    mine_own, pair_own, mine_other, pair_other,
    x_own, x_other,
    out_own, out_other,
    gain_ref,
    in_own, in_other,
    run_ref,
    glu_ref, edge_ref, mid_keep, mid_send,
):
    h = meta[0]
    first = meta[1] == 0
    half = x_own.shape[1]
    rows = glu_ref.shape[0]
    here = pl.ds(pl.multiple_of(h * (rows - 2 * EDGE), EDGE), rows)

    def joined(mine, pair):
        mine = mine[here, :]
        pair = pair[here, :]
        return jnp.concatenate(
            [jnp.where(first, mine, pair), jnp.where(first, pair, mine)], axis=1
        )

    depth = 2 * mine_own.shape[1]
    c_own = joined(mine_own, pair_own)
    c_other = joined(mine_other, pair_other)
    own_cols = pl.ds(pl.multiple_of(h * half, half), half)
    other_cols = pl.ds(pl.multiple_of((1 - h) * half, half), half)

    def mid(cols, x_ref):
        first = dot(c_own, out_own[:depth, cols]).astype(BF16).astype(F32)
        second = dot(c_other, out_other[:depth, cols]).astype(BF16).astype(F32)
        return (x_ref[here, :].astype(F32) + (first + second)).astype(BF16)

    m_own = mid(own_cols, x_own)
    m_other = mid(other_cols, x_other)
    keep = rows - EDGE

    @pl.when(h == 0)
    def _():
        mid_keep[...] = m_own[:keep]
        mid_send[...] = m_other[:keep]

    @pl.when(h == 1)
    def _():
        mid_keep[...] = m_own[EDGE:]
        mid_send[...] = m_other[EDGE:]

    n_own, n_other = normalize_halves(
        m_own.astype(F32), m_other.astype(F32), gain_ref[h], gain_ref[1 - h]
    )
    run = run_ref[here, :]
    valid = run[:, 1:2] > run[:, 0:1]
    glus = []
    for w_ref in (in_own, in_other):
        value = dot(n_own, w_ref[0, own_cols, :]) + dot(n_other, w_ref[0, other_cols, :])
        gate = dot(n_own, w_ref[1, own_cols, :]) + dot(n_other, w_ref[1, other_cols, :])
        glu = value / (1.0 + jnp.exp(-gate))
        glus.append(jnp.where(valid, glu, 0.0).astype(BF16))
    chan = glus[0].shape[1]
    glu_ref[:, :chan] = glus[0]
    glu_ref[:, chan:] = glus[1]

    @pl.when(h == 0)
    def _():
        edge_ref[:, :chan] = glus[1][:SENT]
        edge_ref[:, chan:] = glus[0][:SENT]

    @pl.when(h == 1)
    def _():
        edge_ref[:, :chan] = glus[1][rows - SENT :]
        edge_ref[:, chan:] = glus[0][rows - SENT :]


def gated(meta, contexts, x_own, x_other, out_own, out_other, gain, in_own, in_other, runs):
    rows = x_own.shape[0] // 2 + EDGE
    half = x_own.shape[1]
    chan = in_own.shape[2]
    vmem = pl.BlockSpec(memory_space=pltpu.VMEM)
    return pl.pallas_call(
        gate_kernel,
        in_specs=[pl.BlockSpec(memory_space=pltpu.SMEM)] + [vmem] * 12,
        out_specs=[vmem] * 4,
        out_shape=[
            jax.ShapeDtypeStruct((rows, 2 * chan), BF16),
            jax.ShapeDtypeStruct((SENT, 2 * chan), BF16),
            jax.ShapeDtypeStruct((rows - EDGE, half), BF16),
            jax.ShapeDtypeStruct((rows - EDGE, half), BF16),
        ],
        compiler_params=pltpu.CompilerParams(vmem_limit_bytes=VMEM_LIMIT),
        cost_estimate=traffic(3),
        name="gated",
    )(meta, *contexts, x_own, x_other, out_own, out_other,
      gain.reshape(2, 1, half), in_own, in_other, runs)


def conv_rows(shifted, low, high, taps, out_ref, rows):
    width = out_ref.shape[1]
    chan = width // 2
    reach = KERNEL // 2
    step = min(32, rows)
    cols = range(0, width, 128)
    weights = [
        [
            (taps[0] if col < chan else taps[1])[tap : tap + 1, col % chan : col % chan + 128]
            for col in cols
        ]
        for tap in range(KERNEL + 1)
    ]
    for base in range(0, rows, step):
        totals = [jnp.zeros((step, 128), F32) for _ in cols]
        for tap in range(KERNEL):
            shift = tap - reach
            same = (low[base : base + step] <= shift) & (high[base : base + step] > shift)
            row = base + EDGE + shift
            first = row - row % 8
            for index, col in enumerate(cols):
                piece = shifted[row % 8, first : first + step, col : col + 128]
                totals[index] = totals[index] + jnp.where(same, piece, 0.0) * weights[tap][index]
        mean = jnp.sum(sum(totals), axis=1, keepdims=True) / CONV_CH
        square = jnp.sum(sum(t * t for t in totals), axis=1, keepdims=True) / CONV_CH
        scale = lax.rsqrt(square - mean * mean + 1e-05)
        for index, col in enumerate(cols):
            y = (totals[index] - mean) * scale * weights[KERNEL][index]
            out_ref[base : base + step, col : col + 128] = (y / (1.0 + jnp.exp(-y))).astype(BF16)


def run_offsets(run_ref, first, rows):
    run = run_ref[pl.ds(first, rows), :]
    at = lax.broadcasted_iota(jnp.int32, (rows, 128), 0) + first
    low = jnp.broadcast_to(run[:, 0:1], (rows, 128)) - at
    high = jnp.broadcast_to(run[:, 1:2], (rows, 128)) - at
    return low, high


def conv_kernel(meta, glu_ref, run_ref, taps_own, taps_other, act_ref, ext, shifted):
    h = meta[0]
    rows, width = act_ref.shape
    got = glu_ref.shape[0]
    ext[pl.ds(pl.multiple_of(h * got, EDGE), EDGE), :] = jnp.zeros((EDGE, width), F32)
    ext[pl.ds(pl.multiple_of((1 - h) * EDGE, EDGE), got), :] = glu_ref[...].astype(F32)
    size = shifted.shape[1]
    for s in range(8):
        shifted[s] = ext[s : s + size, :]
    low, high = run_offsets(run_ref, pl.multiple_of(h * rows, rows), rows)
    conv_rows(shifted, low, high, (taps_own, taps_other), act_ref, rows)


def convolve(meta, glu, runs, taps_own, taps_other):
    rows = glu.shape[0] - EDGE
    width = glu.shape[1]
    vmem = pl.BlockSpec(memory_space=pltpu.VMEM)
    return pl.pallas_call(
        conv_kernel,
        in_specs=[pl.BlockSpec(memory_space=pltpu.SMEM)] + [vmem] * 4,
        out_specs=vmem,
        out_shape=jax.ShapeDtypeStruct((rows, width), BF16),
        scratch_shapes=[
            pltpu.VMEM((rows + 2 * EDGE, width), F32),
            pltpu.VMEM((8, rows + 2 * EDGE - 8, width), F32),
        ],
        compiler_params=pltpu.CompilerParams(vmem_limit_bytes=VMEM_LIMIT),
        cost_estimate=weight(3),
        name="convolve",
    )(meta, glu, runs, taps_own, taps_other)


def rim_kernel(meta, glu_ref, edge_ref, run_ref, taps_own, taps_other, act_ref, ext, shifted):
    h = meta[0]
    got = glu_ref.shape[0]
    near = 2 * EDGE
    ext[pl.ds(pl.multiple_of(h * near, EDGE), EDGE), :] = edge_ref[
        pl.ds(pl.multiple_of((1 - h) * (SENT - EDGE), EDGE), EDGE), :
    ].astype(F32)
    ext[pl.ds(pl.multiple_of((1 - h) * EDGE, EDGE), near), :] = glu_ref[
        pl.ds(pl.multiple_of(h * (got - near), EDGE), near), :
    ].astype(F32)
    size = shifted.shape[1]
    for s in range(8):
        shifted[s] = ext[s : s + size, :]
    first = pl.multiple_of(h * (run_ref.shape[0] - EDGE), EDGE)
    low, high = run_offsets(run_ref, first, EDGE)
    conv_rows(shifted, low, high, (taps_own, taps_other), act_ref, EDGE)


def rim(meta, glu, edge, runs, taps_own, taps_other):
    width = glu.shape[1]
    vmem = pl.BlockSpec(memory_space=pltpu.VMEM)
    return pl.pallas_call(
        rim_kernel,
        in_specs=[pl.BlockSpec(memory_space=pltpu.SMEM)] + [vmem] * 5,
        out_specs=vmem,
        out_shape=jax.ShapeDtypeStruct((EDGE, width), BF16),
        scratch_shapes=[
            pltpu.VMEM((3 * EDGE, width), F32),
            pltpu.VMEM((8, 3 * EDGE - 8, width), F32),
        ],
        compiler_params=pltpu.CompilerParams(vmem_limit_bytes=VMEM_LIMIT),
        cost_estimate=weight(1),
        name="rim",
    )(meta, glu, edge, runs, taps_own, taps_other)


def last_product(act_ref, rim_ref, rim_at, mid_ref, w_first, w_second, cols, act):
    chan = act_ref.shape[1] // 2
    act[...] = act_ref[...]
    act[pl.ds(rim_at, EDGE), :] = rim_ref[...]
    below = w_first.shape[0] - chan
    first = dot(act[:, :chan], w_first[below:, cols]).astype(BF16).astype(F32)
    second = dot(act[:, chan:], w_second[below:, cols]).astype(BF16).astype(F32)
    return (mid_ref[...].astype(F32) + (first + second)).astype(BF16)


def finish_own_kernel(meta, act_ref, rim_ref, mid_ref, w_own, w_other, out_ref, act):
    h = meta[0]
    rows, half = out_ref.shape
    out_ref[...] = last_product(
        act_ref, rim_ref, pl.multiple_of(h * (rows - EDGE), EDGE), mid_ref, w_own, w_other,
        pl.ds(pl.multiple_of(h * half, half), half), act,
    )


def finish_kernel(meta, act_ref, rim_ref, mid_ref, w_own, w_other, done_ref, out_ref, act):
    h = meta[0]
    rows, half = done_ref.shape
    out_ref[pl.ds(pl.multiple_of(h * rows, rows), rows), :] = done_ref[...]
    out_ref[pl.ds(pl.multiple_of((1 - h) * rows, rows), rows), :] = last_product(
        act_ref, rim_ref, pl.multiple_of((1 - h) * (rows - EDGE), EDGE), mid_ref, w_other, w_own,
        pl.ds(pl.multiple_of(h * half, half), half), act,
    )


def finish(meta, act, rim_act, mid, w_own, w_other, done=None):
    rows, half = mid.shape
    vmem = pl.BlockSpec(memory_space=pltpu.VMEM)
    args = (act, rim_act, mid, w_own, w_other) + (() if done is None else (done,))
    return pl.pallas_call(
        finish_own_kernel if done is None else finish_kernel,
        in_specs=[pl.BlockSpec(memory_space=pltpu.SMEM)] + [vmem] * len(args),
        out_specs=vmem,
        out_shape=jax.ShapeDtypeStruct((rows if done is None else 2 * rows, half), BF16),
        scratch_shapes=[pltpu.VMEM(act.shape, BF16)],
        compiler_params=pltpu.CompilerParams(vmem_limit_bytes=VMEM_LIMIT),
        cost_estimate=weight(1.2),
        name="finish_own" if done is None else "finish",
    )(meta, *args)


def local(
    blocks,
    frames,
    segment_ids,
    utt_valid,
    attn_gain,
    qkv_weight,
    out_weight,
    conv_gain,
    pointwise_in,
    depthwise,
    mid_gain,
    pointwise_out,
):
    rows = frames.shape[0]

    def swap(value):
        return lax.ppermute(value, "head", [(0, 1), (1, 0)])

    def shift(value, step):
        pairs = [(i, i - step if i % 2 == 0 else i + step) for i in range(blocks)]
        return lax.ppermute(value, "tm", [p for p in pairs if 0 <= p[1] < blocks])

    def exchange(value):
        return lax.ppermute(value, "tm", [(i, i ^ 1) for i in range(blocks)])

    block = lax.axis_index("tm").astype(jnp.int32)
    column = block % 2
    meta = jnp.stack([
        lax.axis_index("head").astype(jnp.int32),
        column,
        block * rows,
        (block + 1 - 2 * column) * rows,
    ])
    other = swap(frames)
    pointwise = pointwise_in.transpose(1, 0, 2)
    keep, query, send, passed = project(
        meta, frames, other, attn_gain, qkv_weight, pointwise
    )
    far_own = shift(passed, 1)
    pair = exchange(send)
    far_pair = shift(keep, 2)

    segment_ids, _ = lax.optimization_barrier((segment_ids, passed))
    ids = jnp.arange(utt_valid.shape[0], dtype=jnp.int32)
    counts = jnp.sum((segment_ids[None, :] == ids[:, None]).astype(jnp.int32), axis=1)
    counts = lax.all_to_all(
        jnp.broadcast_to(counts[None, :], (blocks, counts.shape[0])), "tm", 0, 0
    )
    taps = jnp.concatenate([depthwise, mid_gain[None, :]], axis=0)
    out_weight, pointwise, taps, keep = lax.optimization_barrier(
        (out_weight, pointwise, taps, keep)
    )
    pointwise_other = swap(pointwise)
    out_other = swap(out_weight)
    runs, pair_runs = bounds(meta, counts, utt_valid, rows, (query,))
    taps, pointwise_out, runs = lax.optimization_barrier((taps, pointwise_out, runs))
    taps_other = swap(taps)
    pointwise_out_other = swap(pointwise_out)
    pair, far_pair, far_own, runs, pair_runs = lax.optimization_barrier(
        (pair, far_pair, far_own, runs, pair_runs)
    )
    weights = (pointwise_other, out_other)
    pair_context = attend(
        column.reshape(1), pair, pair, keep, far_pair, pair_runs, (query, far_own, *weights)
    )
    pair_context = exchange(pair_context)
    context = attend((1 - column).reshape(1), query, keep, pair, far_own, runs, weights)
    contexts = (context, pair_context, swap(context), swap(pair_context))
    glu, edge, mid_keep, mid_send = gated(
        meta, contexts, frames, other, out_weight, out_other, conv_gain,
        pointwise, pointwise_other, runs,
    )
    edges = [(2 * i, 2 * (i - 1) + 1) for i in range(1, blocks)]
    edges += [(2 * i + 1, 2 * (i + 1)) for i in range(blocks - 1)]
    edge = lax.ppermute(edge, ("tm", "head"), edges)
    mid_other = swap(mid_send)
    act = convolve(meta, glu, runs, taps, taps_other)
    act_other = swap(act)
    rim_act = rim(meta, glu, edge, runs, taps, taps_other)
    rim_other = swap(rim_act)
    done = finish(meta, act, rim_act, mid_keep, pointwise_out, pointwise_out_other)
    return finish(
        meta, act_other, rim_other, mid_other, pointwise_out, pointwise_out_other, done
    )


def solution(mesh):
    in_specs = (
        P(("grp", "tm"), "head"),
        P(("grp", "tm")),
        P("grp"),
        P(),
        P(None, None, "head"),
        P("head", None),
        P(),
        P(None, None, "head"),
        P(None, "head"),
        P("head"),
        P("head", None),
    )
    out_specs = P(("grp", "tm"), "head")
    return jax.shard_map(
        functools.partial(local, mesh.shape["tm"]),
        mesh=mesh,
        in_specs=in_specs,
        out_specs=out_specs,
        check_vma=False,
    )
```

```python
import functools
import math

import jax
import jax.numpy as jnp
from jax import lax
from jax.experimental import pallas as pl
from jax.experimental.pallas import tpu as pltpu
from jax.sharding import PartitionSpec as P

HEAD_DIM = 64
CONV_CH = 512
KERNEL = 31
WIN = 512
EDGE = 16
SENT = 64
NEG = -1e30
EXP_SCALE = HEAD_DIM ** (-0.5) * math.log2(math.e)
F32 = jnp.float32
BF16 = jnp.bfloat16
VMEM_LIMIT = 16 * 1024 * 1024


def weight(microseconds):
    return pl.CostEstimate(
        flops=int(microseconds * 1.15e9), bytes_accessed=0, transcendentals=0
    )


def traffic(microseconds):
    return pl.CostEstimate(
        flops=0, bytes_accessed=int(microseconds * 3.69e6), transcendentals=0
    )


def dot(a, b):
    return jnp.dot(a, b, preferred_element_type=F32)


def normalize_halves(own, other, gain_own, gain_other):
    width = own.shape[1] + other.shape[1]
    mean = (
        jnp.sum(own, axis=1, keepdims=True) + jnp.sum(other, axis=1, keepdims=True)
    ) / width
    own = own - mean
    other = other - mean
    spread = (
        jnp.sum(own * own, axis=1, keepdims=True) + jnp.sum(other * other, axis=1, keepdims=True)
    ) / width
    scale = lax.rsqrt(spread + 1e-05)
    return (own * scale * gain_own).astype(BF16), (other * scale * gain_other).astype(BF16)


def qkv_kernel(
    meta, own_ref, other_ref, gain_ref, w_ref, _, keep_ref, hold_ref, send_ref, pass_ref
):
    h = meta[0]
    first = meta[1] == 0
    rows = own_ref.shape[0]
    tile = 256
    for at in range(0, rows, tile):
        here = slice(at, at + tile)
        n_own, n_other = normalize_halves(
            own_ref[here, :].astype(F32), other_ref[here, :].astype(F32),
            gain_ref[h], gain_ref[1 - h],
        )
        for slot, part in enumerate((1, 2, 0)):
            value = (dot(n_own, w_ref[part, h]) + dot(n_other, w_ref[part, 1 - h])).astype(BF16)
            sub = value.shape[1] // 2
            cols = slice(slot * sub, slot * sub + sub)
            keep = jnp.where(first, value[:, :sub], value[:, sub:])
            send = jnp.where(first, value[:, sub:], value[:, :sub])
            send_ref[here, cols] = send
            hold_ref[here, cols] = keep
            if slot < 2:
                keep_ref[here, cols] = keep
                pass_ref[here, cols] = send


def project(meta, frames, other, gain, qkv, early):
    rows, half = frames.shape
    width = qkv.shape[2]
    vmem = pl.BlockSpec(memory_space=pltpu.VMEM)
    return pl.pallas_call(
        qkv_kernel,
        in_specs=[pl.BlockSpec(memory_space=pltpu.SMEM)]
        + [vmem] * 4
        + [pl.BlockSpec(memory_space=pl.ANY)],
        out_specs=[vmem] * 4,
        out_shape=[
            jax.ShapeDtypeStruct((rows, width), BF16),
            jax.ShapeDtypeStruct((rows, 3 * width // 2), BF16),
            jax.ShapeDtypeStruct((rows, 3 * width // 2), BF16),
            jax.ShapeDtypeStruct((rows, width), BF16),
        ],
        compiler_params=pltpu.CompilerParams(vmem_limit_bytes=VMEM_LIMIT),
        name="project",
    )(meta, frames, other, gain.reshape(2, 1, half),
      qkv.transpose(1, 0, 2).reshape(3, 2, half, width), early)


def bounds_kernel(meta, counts, valid, own_ref, pair_ref):
    utts = valid.shape[1]
    rows = own_ref.shape[0]
    square = (utts, utts)
    sub = lax.broadcasted_iota(jnp.int32, square, 0)
    lane = lax.broadcasted_iota(jnp.int32, square, 1)
    total = jnp.sum(counts[...].astype(F32), axis=0, keepdims=True)
    limit = jnp.broadcast_to(jnp.minimum(total, valid[...].astype(F32)), square)
    total = jnp.broadcast_to(total, square)
    start = jnp.sum(jnp.where(lane < sub, total, 0.0), axis=1, keepdims=True)
    stop = start + jnp.sum(jnp.where(lane == sub, limit, 0.0), axis=1, keepdims=True)
    at = lax.broadcasted_iota(jnp.int32, (utts, rows), 1).astype(F32)
    for slot, ref in enumerate((own_ref, pair_ref)):
        origin = meta[2 + slot].astype(F32)
        lo = start - origin
        hi = stop - origin
        inside = (at >= lo) & (at < hi)
        low = jnp.sum(jnp.where(inside, lo, 0.0), axis=0, keepdims=True)
        high = jnp.sum(jnp.where(inside, hi, 0.0), axis=0, keepdims=True)
        both = jnp.concatenate([low, high, jnp.zeros((126, rows), F32)], axis=0)
        ref[...] = both.T.astype(jnp.int32)


def bounds(meta, counts, valid, rows):
    vmem = pl.BlockSpec(memory_space=pltpu.VMEM)
    return pl.pallas_call(
        bounds_kernel,
        in_specs=[pl.BlockSpec(memory_space=pltpu.SMEM), vmem, vmem],
        out_specs=[vmem] * 2,
        out_shape=[jax.ShapeDtypeStruct((rows, 128), jnp.int32)] * 2,
        compiler_params=pltpu.CompilerParams(vmem_limit_bytes=VMEM_LIMIT),
        name="bounds",
    )(meta, counts, valid.reshape(1, -1))


def attend_kernel(a_high, query, center, side_a, side_b, run_ref, out_ref):
    rows = center.shape[0]
    width = center.shape[1] // 3
    q_cols = slice(query.shape[1] - width, query.shape[1])
    tile = rows // 2
    lane = lax.broadcasted_iota(jnp.int32, (tile, width), 1)

    def run(low_ref, high_ref):
        for block in range(2):
            at = block * tile
            pieces = (
                ((low_ref, 0, rows, -rows), (center, 0, rows, 0), (high_ref, 0, tile, rows))
                if block == 0
                else ((low_ref, tile, tile, -rows), (center, 0, rows, 0), (high_ref, 0, rows, rows))
            )
            position = lax.broadcasted_iota(jnp.int32, (tile, 1), 0) + at
            lo = run_ref[at : at + tile, 0:1]
            hi = run_ref[at : at + tile, 1:2]
            near_lo = jnp.maximum(lo, position - WIN)
            near_hi = jnp.minimum(hi, position + (WIN + 1))
            biases = []
            for _, first, size, origin in pieces:
                u = lax.broadcasted_iota(jnp.int32, (tile, size), 1) + (origin + first)
                biases.append(jnp.where((u >= near_lo) & (u < near_hi), 0.0, NEG))
            q = query[at : at + tile, q_cols]
            outs = []
            for sub in range(2):
                q_sub = jnp.where((lane >= HEAD_DIM) == (sub == 1), q, jnp.zeros_like(q))
                scores = []
                for (ref, first, size, _), bias in zip(pieces, biases):
                    s = lax.dot_general(
                        q_sub, ref[first : first + size, :width], (((1,), (1,)), ((), ())),
                        preferred_element_type=F32,
                    )
                    scores.append(s + bias)
                peak = functools.reduce(
                    jnp.maximum, [jnp.max(s, axis=1, keepdims=True) for s in scores]
                )
                total = jnp.zeros((tile, 1), F32)
                context = jnp.zeros((tile, width), F32)
                for (ref, first, size, _), s in zip(pieces, scores):
                    expw = jnp.exp2((s - peak) * EXP_SCALE)
                    total = total + jnp.sum(expw, axis=1, keepdims=True)
                    context = context + dot(
                        expw.astype(BF16), ref[first : first + size, width : 2 * width]
                    )
                outs.append(context / jnp.maximum(total, 1.0))
            joined = jnp.where(lane >= HEAD_DIM, outs[1], outs[0])
            out_ref[at : at + tile, :] = jnp.where(hi > lo, joined, 0.0).astype(BF16)

    @pl.when(a_high[0] == 1)
    def _():
        run(side_b, side_a)

    @pl.when(a_high[0] == 0)
    def _():
        run(side_a, side_b)


def attend(a_high, query, center, side_a, side_b, runs):
    rows, width = side_b.shape[0], side_b.shape[1] // 2
    vmem = pl.BlockSpec(memory_space=pltpu.VMEM)
    return pl.pallas_call(
        attend_kernel,
        in_specs=[pl.BlockSpec(memory_space=pltpu.SMEM)] + [vmem] * 5,
        out_specs=vmem,
        out_shape=jax.ShapeDtypeStruct((rows, width), BF16),
        compiler_params=pltpu.CompilerParams(vmem_limit_bytes=VMEM_LIMIT),
        cost_estimate=traffic(3),
        name="attend",
    )(a_high, query, center, side_a, side_b, runs)


def gate_kernel(
    meta,
    mine_own, pair_own, mine_other, pair_other,
    x_own, x_other,
    out_own, out_other,
    gain_ref,
    in_own, in_other,
    run_ref,
    glu_ref, edge_ref, mid_keep, mid_send,
):
    h = meta[0]
    first = meta[1] == 0
    half = x_own.shape[1]
    rows = glu_ref.shape[0]
    here = pl.ds(pl.multiple_of(h * (rows - 2 * EDGE), EDGE), rows)

    def joined(mine, pair):
        mine = mine[here, :]
        pair = pair[here, :]
        return jnp.concatenate(
            [jnp.where(first, mine, pair), jnp.where(first, pair, mine)], axis=1
        )

    depth = 2 * mine_own.shape[1]
    c_own = joined(mine_own, pair_own)
    c_other = joined(mine_other, pair_other)
    own_cols = pl.ds(pl.multiple_of(h * half, half), half)
    other_cols = pl.ds(pl.multiple_of((1 - h) * half, half), half)

    def mid(cols, x_ref):
        first = dot(c_own, out_own[:depth, cols]).astype(BF16).astype(F32)
        second = dot(c_other, out_other[:depth, cols]).astype(BF16).astype(F32)
        return (x_ref[here, :].astype(F32) + (first + second)).astype(BF16)

    m_own = mid(own_cols, x_own)
    m_other = mid(other_cols, x_other)
    keep = rows - EDGE

    @pl.when(h == 0)
    def _():
        mid_keep[...] = m_own[:keep]
        mid_send[...] = m_other[:keep]

    @pl.when(h == 1)
    def _():
        mid_keep[...] = m_own[EDGE:]
        mid_send[...] = m_other[EDGE:]

    n_own, n_other = normalize_halves(
        m_own.astype(F32), m_other.astype(F32), gain_ref[h], gain_ref[1 - h]
    )
    run = run_ref[here, :]
    valid = run[:, 1:2] > run[:, 0:1]
    glus = []
    for w_ref in (in_own, in_other):
        value = dot(n_own, w_ref[0, own_cols, :]) + dot(n_other, w_ref[0, other_cols, :])
        gate = dot(n_own, w_ref[1, own_cols, :]) + dot(n_other, w_ref[1, other_cols, :])
        glu = value / (1.0 + jnp.exp(-gate))
        glus.append(jnp.where(valid, glu, 0.0).astype(BF16))
    chan = glus[0].shape[1]
    glu_ref[:, :chan] = glus[0]
    glu_ref[:, chan:] = glus[1]

    @pl.when(h == 0)
    def _():
        edge_ref[:, :chan] = glus[1][:SENT]
        edge_ref[:, chan:] = glus[0][:SENT]

    @pl.when(h == 1)
    def _():
        edge_ref[:, :chan] = glus[1][rows - SENT :]
        edge_ref[:, chan:] = glus[0][rows - SENT :]


def gated(meta, contexts, x_own, x_other, out_own, out_other, gain, in_own, in_other, runs):
    rows = x_own.shape[0] // 2 + EDGE
    half = x_own.shape[1]
    chan = in_own.shape[2]
    vmem = pl.BlockSpec(memory_space=pltpu.VMEM)
    return pl.pallas_call(
        gate_kernel,
        in_specs=[pl.BlockSpec(memory_space=pltpu.SMEM)] + [vmem] * 12,
        out_specs=[vmem] * 4,
        out_shape=[
            jax.ShapeDtypeStruct((rows, 2 * chan), BF16),
            jax.ShapeDtypeStruct((SENT, 2 * chan), BF16),
            jax.ShapeDtypeStruct((rows - EDGE, half), BF16),
            jax.ShapeDtypeStruct((rows - EDGE, half), BF16),
        ],
        compiler_params=pltpu.CompilerParams(vmem_limit_bytes=VMEM_LIMIT),
        cost_estimate=traffic(3),
        name="gated",
    )(meta, *contexts, x_own, x_other, out_own, out_other,
      gain.reshape(2, 1, half), in_own, in_other, runs)


def conv_rows(shifted, low, high, taps, out_ref, rows):
    width = out_ref.shape[1]
    chan = width // 2
    reach = KERNEL // 2
    step = min(32, rows)
    cols = range(0, width, 128)
    weights = [
        [
            (taps[0] if col < chan else taps[1])[tap : tap + 1, col % chan : col % chan + 128]
            for col in cols
        ]
        for tap in range(KERNEL + 1)
    ]
    for base in range(0, rows, step):
        totals = [jnp.zeros((step, 128), F32) for _ in cols]
        for tap in range(KERNEL):
            shift = tap - reach
            same = (low[base : base + step] <= shift) & (high[base : base + step] > shift)
            row = base + EDGE + shift
            first = row - row % 8
            for index, col in enumerate(cols):
                piece = shifted[row % 8, first : first + step, col : col + 128]
                totals[index] = totals[index] + jnp.where(same, piece, 0.0) * weights[tap][index]
        mean = jnp.sum(sum(totals), axis=1, keepdims=True) / CONV_CH
        square = jnp.sum(sum(t * t for t in totals), axis=1, keepdims=True) / CONV_CH
        scale = lax.rsqrt(square - mean * mean + 1e-05)
        for index, col in enumerate(cols):
            y = (totals[index] - mean) * scale * weights[KERNEL][index]
            out_ref[base : base + step, col : col + 128] = (y / (1.0 + jnp.exp(-y))).astype(BF16)


def run_offsets(run_ref, first, rows):
    run = run_ref[pl.ds(first, rows), :]
    at = lax.broadcasted_iota(jnp.int32, (rows, 128), 0) + first
    low = jnp.broadcast_to(run[:, 0:1], (rows, 128)) - at
    high = jnp.broadcast_to(run[:, 1:2], (rows, 128)) - at
    return low, high


def conv_kernel(meta, glu_ref, run_ref, taps_own, taps_other, act_ref, ext, shifted):
    h = meta[0]
    rows, width = act_ref.shape
    got = glu_ref.shape[0]
    ext[pl.ds(pl.multiple_of(h * got, EDGE), EDGE), :] = jnp.zeros((EDGE, width), F32)
    ext[pl.ds(pl.multiple_of((1 - h) * EDGE, EDGE), got), :] = glu_ref[...].astype(F32)
    size = shifted.shape[1]
    for s in range(8):
        shifted[s] = ext[s : s + size, :]
    low, high = run_offsets(run_ref, pl.multiple_of(h * rows, rows), rows)
    conv_rows(shifted, low, high, (taps_own, taps_other), act_ref, rows)


def convolve(meta, glu, runs, taps_own, taps_other):
    rows = glu.shape[0] - EDGE
    width = glu.shape[1]
    vmem = pl.BlockSpec(memory_space=pltpu.VMEM)
    return pl.pallas_call(
        conv_kernel,
        in_specs=[pl.BlockSpec(memory_space=pltpu.SMEM)] + [vmem] * 4,
        out_specs=vmem,
        out_shape=jax.ShapeDtypeStruct((rows, width), BF16),
        scratch_shapes=[
            pltpu.VMEM((rows + 2 * EDGE, width), F32),
            pltpu.VMEM((8, rows + 2 * EDGE - 8, width), F32),
        ],
        compiler_params=pltpu.CompilerParams(vmem_limit_bytes=VMEM_LIMIT),
        cost_estimate=weight(3),
        name="convolve",
    )(meta, glu, runs, taps_own, taps_other)


def rim_kernel(meta, glu_ref, edge_ref, run_ref, taps_own, taps_other, act_ref, ext, shifted):
    h = meta[0]
    got = glu_ref.shape[0]
    near = 2 * EDGE
    ext[pl.ds(pl.multiple_of(h * near, EDGE), EDGE), :] = edge_ref[
        pl.ds(pl.multiple_of((1 - h) * (SENT - EDGE), EDGE), EDGE), :
    ].astype(F32)
    ext[pl.ds(pl.multiple_of((1 - h) * EDGE, EDGE), near), :] = glu_ref[
        pl.ds(pl.multiple_of(h * (got - near), EDGE), near), :
    ].astype(F32)
    size = shifted.shape[1]
    for s in range(8):
        shifted[s] = ext[s : s + size, :]
    first = pl.multiple_of(h * (run_ref.shape[0] - EDGE), EDGE)
    low, high = run_offsets(run_ref, first, EDGE)
    conv_rows(shifted, low, high, (taps_own, taps_other), act_ref, EDGE)


def rim(meta, glu, edge, runs, taps_own, taps_other):
    width = glu.shape[1]
    vmem = pl.BlockSpec(memory_space=pltpu.VMEM)
    return pl.pallas_call(
        rim_kernel,
        in_specs=[pl.BlockSpec(memory_space=pltpu.SMEM)] + [vmem] * 5,
        out_specs=vmem,
        out_shape=jax.ShapeDtypeStruct((EDGE, width), BF16),
        scratch_shapes=[
            pltpu.VMEM((3 * EDGE, width), F32),
            pltpu.VMEM((8, 3 * EDGE - 8, width), F32),
        ],
        compiler_params=pltpu.CompilerParams(vmem_limit_bytes=VMEM_LIMIT),
        cost_estimate=weight(1),
        name="rim",
    )(meta, glu, edge, runs, taps_own, taps_other)


def last_product(act_ref, rim_ref, rim_at, mid_ref, w_first, w_second, cols, act):
    chan = act_ref.shape[1] // 2
    act[...] = act_ref[...]
    act[pl.ds(rim_at, EDGE), :] = rim_ref[...]
    below = w_first.shape[0] - chan
    first = dot(act[:, :chan], w_first[below:, cols]).astype(BF16).astype(F32)
    second = dot(act[:, chan:], w_second[below:, cols]).astype(BF16).astype(F32)
    return (mid_ref[...].astype(F32) + (first + second)).astype(BF16)


def finish_own_kernel(meta, act_ref, rim_ref, mid_ref, w_own, w_other, out_ref, act):
    h = meta[0]
    rows, half = out_ref.shape
    out_ref[...] = last_product(
        act_ref, rim_ref, pl.multiple_of(h * (rows - EDGE), EDGE), mid_ref, w_own, w_other,
        pl.ds(pl.multiple_of(h * half, half), half), act,
    )


def finish_kernel(meta, act_ref, rim_ref, mid_ref, w_own, w_other, done_ref, out_ref, act):
    h = meta[0]
    rows, half = done_ref.shape
    out_ref[pl.ds(pl.multiple_of(h * rows, rows), rows), :] = done_ref[...]
    out_ref[pl.ds(pl.multiple_of((1 - h) * rows, rows), rows), :] = last_product(
        act_ref, rim_ref, pl.multiple_of((1 - h) * (rows - EDGE), EDGE), mid_ref, w_other, w_own,
        pl.ds(pl.multiple_of(h * half, half), half), act,
    )


def finish(meta, act, rim_act, mid, w_own, w_other, done=None):
    rows, half = mid.shape
    vmem = pl.BlockSpec(memory_space=pltpu.VMEM)
    args = (act, rim_act, mid, w_own, w_other) + (() if done is None else (done,))
    return pl.pallas_call(
        finish_own_kernel if done is None else finish_kernel,
        in_specs=[pl.BlockSpec(memory_space=pltpu.SMEM)] + [vmem] * len(args),
        out_specs=vmem,
        out_shape=jax.ShapeDtypeStruct((rows if done is None else 2 * rows, half), BF16),
        scratch_shapes=[pltpu.VMEM(act.shape, BF16)],
        compiler_params=pltpu.CompilerParams(vmem_limit_bytes=VMEM_LIMIT),
        cost_estimate=weight(1.2),
        name="finish_own" if done is None else "finish",
    )(meta, *args)


def local(
    blocks,
    frames,
    segment_ids,
    utt_valid,
    attn_gain,
    qkv_weight,
    out_weight,
    conv_gain,
    pointwise_in,
    depthwise,
    mid_gain,
    pointwise_out,
):
    rows = frames.shape[0]

    def swap(value):
        return lax.ppermute(value, "head", [(0, 1), (1, 0)])

    def shift(value, step):
        pairs = [(i, i - step if i % 2 == 0 else i + step) for i in range(blocks)]
        return lax.ppermute(value, "tm", [p for p in pairs if 0 <= p[1] < blocks])

    def exchange(value):
        return lax.ppermute(value, "tm", [(i, i ^ 1) for i in range(blocks)])

    block = lax.axis_index("tm").astype(jnp.int32)
    column = block % 2
    meta = jnp.stack([
        lax.axis_index("head").astype(jnp.int32),
        column,
        block * rows,
        (block + 1 - 2 * column) * rows,
    ])
    other = swap(frames)
    pointwise = pointwise_in.transpose(1, 0, 2)
    keep, held, send, passed = project(
        meta, frames, other, attn_gain, qkv_weight, pointwise
    )
    far_own = shift(passed, 1)
    pair = exchange(send)
    far_pair = shift(keep, 2)

    segment_ids, _ = lax.optimization_barrier((segment_ids, passed))
    ids = jnp.arange(utt_valid.shape[0], dtype=jnp.int32)
    counts = jnp.sum((segment_ids[None, :] == ids[:, None]).astype(jnp.int32), axis=1)
    counts = lax.all_to_all(
        jnp.broadcast_to(counts[None, :], (blocks, counts.shape[0])), "tm", 0, 0
    )
    taps = jnp.concatenate([depthwise, mid_gain[None, :]], axis=0)
    out_weight, pointwise, taps, keep = lax.optimization_barrier(
        (out_weight, pointwise, taps, keep)
    )
    pointwise_other = swap(pointwise)
    out_other = swap(out_weight)
    runs, pair_runs = bounds(meta, counts, utt_valid, rows)
    taps, pointwise_out, runs = lax.optimization_barrier((taps, pointwise_out, runs))
    taps_other = swap(taps)
    pointwise_out_other = swap(pointwise_out)
    pair, far_pair, runs, pair_runs = lax.optimization_barrier(
        (pair, far_pair, runs, pair_runs)
    )
    pair_context = attend(column.reshape(1), pair, pair, held, far_pair, pair_runs)
    pair_context = exchange(pair_context)
    context = attend((1 - column).reshape(1), held, held, pair, far_own, runs)
    contexts = (context, pair_context, swap(context), swap(pair_context))
    glu, edge, mid_keep, mid_send = gated(
        meta, contexts, frames, other, out_weight, out_other, conv_gain,
        pointwise, pointwise_other, runs,
    )
    edges = [(2 * i, 2 * (i - 1) + 1) for i in range(1, blocks)]
    edges += [(2 * i + 1, 2 * (i + 1)) for i in range(blocks - 1)]
    edge = lax.ppermute(edge, ("tm", "head"), edges)
    mid_other = swap(mid_send)
    act = convolve(meta, glu, runs, taps, taps_other)
    act_other = swap(act)
    rim_act = rim(meta, glu, edge, runs, taps, taps_other)
    rim_other = swap(rim_act)
    done = finish(meta, act, rim_act, mid_keep, pointwise_out, pointwise_out_other)
    return finish(
        meta, act_other, rim_other, mid_other, pointwise_out, pointwise_out_other, done
    )


def solution(mesh):
    in_specs = (
        P(("grp", "tm"), "head"),
        P(("grp", "tm")),
        P("grp"),
        P(),
        P(None, None, "head"),
        P("head", None),
        P(),
        P(None, None, "head"),
        P(None, "head"),
        P("head"),
        P("head", None),
    )
    out_specs = P(("grp", "tm"), "head")
    return jax.shard_map(
        functools.partial(local, mesh.shape["tm"]),
        mesh=mesh,
        in_specs=in_specs,
        out_specs=out_specs,
        check_vma=False,
    )
```

```python
import functools
import math

import jax
import jax.numpy as jnp
from jax import lax
from jax.experimental import pallas as pl
from jax.experimental.pallas import tpu as pltpu
from jax.sharding import PartitionSpec as P

HEAD_DIM = 64
CONV_CH = 512
KERNEL = 31
WIN = 512
EDGE = 16
SENT = 64
NEG = -1e30
EXP_SCALE = HEAD_DIM ** (-0.5) * math.log2(math.e)
F32 = jnp.float32
BF16 = jnp.bfloat16
VMEM_LIMIT = 16 * 1024 * 1024


def weight(microseconds):
    return pl.CostEstimate(
        flops=int(microseconds * 1.15e9), bytes_accessed=0, transcendentals=0
    )


def traffic(microseconds):
    return pl.CostEstimate(
        flops=0, bytes_accessed=int(microseconds * 3.69e6), transcendentals=0
    )


def dot(a, b):
    return jnp.dot(a, b, preferred_element_type=F32)


def normalize_halves(own, other, gain_own, gain_other):
    width = own.shape[1] + other.shape[1]
    mean = (
        jnp.sum(own, axis=1, keepdims=True) + jnp.sum(other, axis=1, keepdims=True)
    ) / width
    own = own - mean
    other = other - mean
    spread = (
        jnp.sum(own * own, axis=1, keepdims=True) + jnp.sum(other * other, axis=1, keepdims=True)
    ) / width
    scale = lax.rsqrt(spread + 1e-05)
    return (own * scale * gain_own).astype(BF16), (other * scale * gain_other).astype(BF16)


def qkv_kernel(
    meta, own_ref, other_ref, gain_ref, w_ref, _, keep_ref, hold_ref, send_ref, pass_ref
):
    h = meta[0]
    first = meta[1] == 0
    rows = own_ref.shape[0]
    tile = 256
    for at in range(0, rows, tile):
        here = slice(at, at + tile)
        n_own, n_other = normalize_halves(
            own_ref[here, :].astype(F32), other_ref[here, :].astype(F32),
            gain_ref[h], gain_ref[1 - h],
        )
        for slot, part in enumerate((1, 2, 0)):
            value = (dot(n_own, w_ref[part, h]) + dot(n_other, w_ref[part, 1 - h])).astype(BF16)
            sub = value.shape[1] // 2
            cols = slice(slot * sub, slot * sub + sub)
            keep = jnp.where(first, value[:, :sub], value[:, sub:])
            send = jnp.where(first, value[:, sub:], value[:, :sub])
            hold_ref[here, cols] = keep
            if slot < 2:
                keep_ref[here, cols] = keep
                pass_ref[here, cols] = send
            else:
                send_ref[here, :] = send


def project(meta, frames, other, gain, qkv, early):
    rows, half = frames.shape
    width = qkv.shape[2]
    vmem = pl.BlockSpec(memory_space=pltpu.VMEM)
    return pl.pallas_call(
        qkv_kernel,
        in_specs=[pl.BlockSpec(memory_space=pltpu.SMEM)]
        + [vmem] * 4
        + [pl.BlockSpec(memory_space=pl.ANY)],
        out_specs=[vmem] * 4,
        out_shape=[
            jax.ShapeDtypeStruct((rows, width), BF16),
            jax.ShapeDtypeStruct((rows, 3 * width // 2), BF16),
            jax.ShapeDtypeStruct((rows, width // 2), BF16),
            jax.ShapeDtypeStruct((rows, width), BF16),
        ],
        compiler_params=pltpu.CompilerParams(vmem_limit_bytes=VMEM_LIMIT),
        name="project",
    )(meta, frames, other, gain.reshape(2, 1, half),
      qkv.transpose(1, 0, 2).reshape(3, 2, half, width), early)


def bounds_kernel(meta, counts, valid, own_ref, pair_ref):
    utts = valid.shape[1]
    rows = own_ref.shape[0]
    square = (utts, utts)
    sub = lax.broadcasted_iota(jnp.int32, square, 0)
    lane = lax.broadcasted_iota(jnp.int32, square, 1)
    total = jnp.sum(counts[...].astype(F32), axis=0, keepdims=True)
    limit = jnp.broadcast_to(jnp.minimum(total, valid[...].astype(F32)), square)
    total = jnp.broadcast_to(total, square)
    start = jnp.sum(jnp.where(lane < sub, total, 0.0), axis=1, keepdims=True)
    stop = start + jnp.sum(jnp.where(lane == sub, limit, 0.0), axis=1, keepdims=True)
    at = lax.broadcasted_iota(jnp.int32, (utts, rows), 1).astype(F32)
    for slot, ref in enumerate((own_ref, pair_ref)):
        origin = meta[2 + slot].astype(F32)
        lo = start - origin
        hi = stop - origin
        inside = (at >= lo) & (at < hi)
        low = jnp.sum(jnp.where(inside, lo, 0.0), axis=0, keepdims=True)
        high = jnp.sum(jnp.where(inside, hi, 0.0), axis=0, keepdims=True)
        both = jnp.concatenate([low, high, jnp.zeros((126, rows), F32)], axis=0)
        ref[...] = both.T.astype(jnp.int32)


def bounds(meta, counts, valid, rows):
    vmem = pl.BlockSpec(memory_space=pltpu.VMEM)
    return pl.pallas_call(
        bounds_kernel,
        in_specs=[pl.BlockSpec(memory_space=pltpu.SMEM), vmem, vmem],
        out_specs=[vmem] * 2,
        out_shape=[jax.ShapeDtypeStruct((rows, 128), jnp.int32)] * 2,
        compiler_params=pltpu.CompilerParams(vmem_limit_bytes=VMEM_LIMIT),
        name="bounds",
    )(meta, counts, valid.reshape(1, -1))


def attend_kernel(a_high, query, center, side_a, side_b, run_ref, out_ref):
    rows = center.shape[0]
    width = side_b.shape[1] // 2
    q_cols = slice(query.shape[1] - width, query.shape[1])
    tile = rows // 2
    lane = lax.broadcasted_iota(jnp.int32, (tile, width), 1)

    def run(low_ref, high_ref):
        for block in range(2):
            at = block * tile
            pieces = (
                ((low_ref, 0, rows, -rows), (center, 0, rows, 0), (high_ref, 0, tile, rows))
                if block == 0
                else ((low_ref, tile, tile, -rows), (center, 0, rows, 0), (high_ref, 0, rows, rows))
            )
            position = lax.broadcasted_iota(jnp.int32, (tile, 1), 0) + at
            lo = run_ref[at : at + tile, 0:1]
            hi = run_ref[at : at + tile, 1:2]
            near_lo = jnp.maximum(lo, position - WIN)
            near_hi = jnp.minimum(hi, position + (WIN + 1))
            biases = []
            for _, first, size, origin in pieces:
                u = lax.broadcasted_iota(jnp.int32, (tile, size), 1) + (origin + first)
                biases.append(jnp.where((u >= near_lo) & (u < near_hi), 0.0, NEG))
            q = query[at : at + tile, q_cols]
            outs = []
            for sub in range(2):
                q_sub = jnp.where((lane >= HEAD_DIM) == (sub == 1), q, jnp.zeros_like(q))
                scores = []
                for (ref, first, size, _), bias in zip(pieces, biases):
                    s = lax.dot_general(
                        q_sub, ref[first : first + size, :width], (((1,), (1,)), ((), ())),
                        preferred_element_type=F32,
                    )
                    scores.append(s + bias)
                peak = functools.reduce(
                    jnp.maximum, [jnp.max(s, axis=1, keepdims=True) for s in scores]
                )
                total = jnp.zeros((tile, 1), F32)
                context = jnp.zeros((tile, width), F32)
                for (ref, first, size, _), s in zip(pieces, scores):
                    expw = jnp.exp2((s - peak) * EXP_SCALE)
                    total = total + jnp.sum(expw, axis=1, keepdims=True)
                    context = context + dot(
                        expw.astype(BF16), ref[first : first + size, width : 2 * width]
                    )
                outs.append(context / jnp.maximum(total, 1.0))
            joined = jnp.where(lane >= HEAD_DIM, outs[1], outs[0])
            out_ref[at : at + tile, :] = jnp.where(hi > lo, joined, 0.0).astype(BF16)

    @pl.when(a_high[0] == 1)
    def _():
        run(side_b, side_a)

    @pl.when(a_high[0] == 0)
    def _():
        run(side_a, side_b)


def attend(a_high, query, center, side_a, side_b, runs):
    rows, width = side_b.shape[0], side_b.shape[1] // 2
    vmem = pl.BlockSpec(memory_space=pltpu.VMEM)
    return pl.pallas_call(
        attend_kernel,
        in_specs=[pl.BlockSpec(memory_space=pltpu.SMEM)] + [vmem] * 5,
        out_specs=vmem,
        out_shape=jax.ShapeDtypeStruct((rows, width), BF16),
        compiler_params=pltpu.CompilerParams(vmem_limit_bytes=VMEM_LIMIT),
        cost_estimate=traffic(3),
        name="attend",
    )(a_high, query, center, side_a, side_b, runs)


def gate_kernel(
    meta,
    mine_own, pair_own, mine_other, pair_other,
    x_own, x_other,
    out_own, out_other,
    gain_ref,
    in_own, in_other,
    run_ref,
    glu_ref, edge_ref, mid_keep, mid_send,
):
    h = meta[0]
    first = meta[1] == 0
    half = x_own.shape[1]
    rows = glu_ref.shape[0]
    here = pl.ds(pl.multiple_of(h * (rows - 2 * EDGE), EDGE), rows)

    def joined(mine, pair):
        mine = mine[here, :]
        pair = pair[here, :]
        return jnp.concatenate(
            [jnp.where(first, mine, pair), jnp.where(first, pair, mine)], axis=1
        )

    depth = 2 * mine_own.shape[1]
    c_own = joined(mine_own, pair_own)
    c_other = joined(mine_other, pair_other)
    own_cols = pl.ds(pl.multiple_of(h * half, half), half)
    other_cols = pl.ds(pl.multiple_of((1 - h) * half, half), half)

    def mid(cols, x_ref):
        first = dot(c_own, out_own[:depth, cols]).astype(BF16).astype(F32)
        second = dot(c_other, out_other[:depth, cols]).astype(BF16).astype(F32)
        return (x_ref[here, :].astype(F32) + (first + second)).astype(BF16)

    m_own = mid(own_cols, x_own)
    m_other = mid(other_cols, x_other)
    keep = rows - EDGE

    @pl.when(h == 0)
    def _():
        mid_keep[...] = m_own[:keep]
        mid_send[...] = m_other[:keep]

    @pl.when(h == 1)
    def _():
        mid_keep[...] = m_own[EDGE:]
        mid_send[...] = m_other[EDGE:]

    n_own, n_other = normalize_halves(
        m_own.astype(F32), m_other.astype(F32), gain_ref[h], gain_ref[1 - h]
    )
    run = run_ref[here, :]
    valid = run[:, 1:2] > run[:, 0:1]
    glus = []
    for w_ref in (in_own, in_other):
        value = dot(n_own, w_ref[0, own_cols, :]) + dot(n_other, w_ref[0, other_cols, :])
        gate = dot(n_own, w_ref[1, own_cols, :]) + dot(n_other, w_ref[1, other_cols, :])
        glu = value / (1.0 + jnp.exp(-gate))
        glus.append(jnp.where(valid, glu, 0.0).astype(BF16))
    chan = glus[0].shape[1]
    glu_ref[:, :chan] = glus[0]
    glu_ref[:, chan:] = glus[1]

    @pl.when(h == 0)
    def _():
        edge_ref[:, :chan] = glus[1][:SENT]
        edge_ref[:, chan:] = glus[0][:SENT]

    @pl.when(h == 1)
    def _():
        edge_ref[:, :chan] = glus[1][rows - SENT :]
        edge_ref[:, chan:] = glus[0][rows - SENT :]


def gated(meta, contexts, x_own, x_other, out_own, out_other, gain, in_own, in_other, runs):
    rows = x_own.shape[0] // 2 + EDGE
    half = x_own.shape[1]
    chan = in_own.shape[2]
    vmem = pl.BlockSpec(memory_space=pltpu.VMEM)
    return pl.pallas_call(
        gate_kernel,
        in_specs=[pl.BlockSpec(memory_space=pltpu.SMEM)] + [vmem] * 12,
        out_specs=[vmem] * 4,
        out_shape=[
            jax.ShapeDtypeStruct((rows, 2 * chan), BF16),
            jax.ShapeDtypeStruct((SENT, 2 * chan), BF16),
            jax.ShapeDtypeStruct((rows - EDGE, half), BF16),
            jax.ShapeDtypeStruct((rows - EDGE, half), BF16),
        ],
        compiler_params=pltpu.CompilerParams(vmem_limit_bytes=VMEM_LIMIT),
        cost_estimate=traffic(3),
        name="gated",
    )(meta, *contexts, x_own, x_other, out_own, out_other,
      gain.reshape(2, 1, half), in_own, in_other, runs)


def conv_rows(shifted, low, high, taps, out_ref, rows):
    width = out_ref.shape[1]
    chan = width // 2
    reach = KERNEL // 2
    step = min(32, rows)
    cols = range(0, width, 128)
    weights = [
        [
            (taps[0] if col < chan else taps[1])[tap : tap + 1, col % chan : col % chan + 128]
            for col in cols
        ]
        for tap in range(KERNEL + 1)
    ]
    for base in range(0, rows, step):
        totals = [jnp.zeros((step, 128), F32) for _ in cols]
        for tap in range(KERNEL):
            shift = tap - reach
            same = (low[base : base + step] <= shift) & (high[base : base + step] > shift)
            row = base + EDGE + shift
            first = row - row % 8
            for index, col in enumerate(cols):
                piece = shifted[row % 8, first : first + step, col : col + 128]
                totals[index] = totals[index] + jnp.where(same, piece, 0.0) * weights[tap][index]
        mean = jnp.sum(sum(totals), axis=1, keepdims=True) / CONV_CH
        square = jnp.sum(sum(t * t for t in totals), axis=1, keepdims=True) / CONV_CH
        scale = lax.rsqrt(square - mean * mean + 1e-05)
        for index, col in enumerate(cols):
            y = (totals[index] - mean) * scale * weights[KERNEL][index]
            out_ref[base : base + step, col : col + 128] = (y / (1.0 + jnp.exp(-y))).astype(BF16)


def run_offsets(run_ref, first, rows):
    run = run_ref[pl.ds(first, rows), :]
    at = lax.broadcasted_iota(jnp.int32, (rows, 128), 0) + first
    low = jnp.broadcast_to(run[:, 0:1], (rows, 128)) - at
    high = jnp.broadcast_to(run[:, 1:2], (rows, 128)) - at
    return low, high


def conv_kernel(meta, glu_ref, run_ref, taps_own, taps_other, act_ref, ext, shifted):
    h = meta[0]
    rows, width = act_ref.shape
    got = glu_ref.shape[0]
    ext[pl.ds(pl.multiple_of(h * got, EDGE), EDGE), :] = jnp.zeros((EDGE, width), F32)
    ext[pl.ds(pl.multiple_of((1 - h) * EDGE, EDGE), got), :] = glu_ref[...].astype(F32)
    size = shifted.shape[1]
    for s in range(8):
        shifted[s] = ext[s : s + size, :]
    low, high = run_offsets(run_ref, pl.multiple_of(h * rows, rows), rows)
    conv_rows(shifted, low, high, (taps_own, taps_other), act_ref, rows)


def convolve(meta, glu, runs, taps_own, taps_other):
    rows = glu.shape[0] - EDGE
    width = glu.shape[1]
    vmem = pl.BlockSpec(memory_space=pltpu.VMEM)
    return pl.pallas_call(
        conv_kernel,
        in_specs=[pl.BlockSpec(memory_space=pltpu.SMEM)] + [vmem] * 4,
        out_specs=vmem,
        out_shape=jax.ShapeDtypeStruct((rows, width), BF16),
        scratch_shapes=[
            pltpu.VMEM((rows + 2 * EDGE, width), F32),
            pltpu.VMEM((8, rows + 2 * EDGE - 8, width), F32),
        ],
        compiler_params=pltpu.CompilerParams(vmem_limit_bytes=VMEM_LIMIT),
        cost_estimate=weight(3),
        name="convolve",
    )(meta, glu, runs, taps_own, taps_other)


def rim_kernel(meta, glu_ref, edge_ref, run_ref, taps_own, taps_other, act_ref, ext, shifted):
    h = meta[0]
    got = glu_ref.shape[0]
    near = 2 * EDGE
    ext[pl.ds(pl.multiple_of(h * near, EDGE), EDGE), :] = edge_ref[
        pl.ds(pl.multiple_of((1 - h) * (SENT - EDGE), EDGE), EDGE), :
    ].astype(F32)
    ext[pl.ds(pl.multiple_of((1 - h) * EDGE, EDGE), near), :] = glu_ref[
        pl.ds(pl.multiple_of(h * (got - near), EDGE), near), :
    ].astype(F32)
    size = shifted.shape[1]
    for s in range(8):
        shifted[s] = ext[s : s + size, :]
    first = pl.multiple_of(h * (run_ref.shape[0] - EDGE), EDGE)
    low, high = run_offsets(run_ref, first, EDGE)
    conv_rows(shifted, low, high, (taps_own, taps_other), act_ref, EDGE)


def rim(meta, glu, edge, runs, taps_own, taps_other):
    width = glu.shape[1]
    vmem = pl.BlockSpec(memory_space=pltpu.VMEM)
    return pl.pallas_call(
        rim_kernel,
        in_specs=[pl.BlockSpec(memory_space=pltpu.SMEM)] + [vmem] * 5,
        out_specs=vmem,
        out_shape=jax.ShapeDtypeStruct((EDGE, width), BF16),
        scratch_shapes=[
            pltpu.VMEM((3 * EDGE, width), F32),
            pltpu.VMEM((8, 3 * EDGE - 8, width), F32),
        ],
        compiler_params=pltpu.CompilerParams(vmem_limit_bytes=VMEM_LIMIT),
        cost_estimate=weight(1),
        name="rim",
    )(meta, glu, edge, runs, taps_own, taps_other)


def last_product(act_ref, rim_ref, rim_at, mid_ref, w_first, w_second, cols, act):
    chan = act_ref.shape[1] // 2
    act[...] = act_ref[...]
    act[pl.ds(rim_at, EDGE), :] = rim_ref[...]
    below = w_first.shape[0] - chan
    first = dot(act[:, :chan], w_first[below:, cols]).astype(BF16).astype(F32)
    second = dot(act[:, chan:], w_second[below:, cols]).astype(BF16).astype(F32)
    return (mid_ref[...].astype(F32) + (first + second)).astype(BF16)


def finish_own_kernel(meta, act_ref, rim_ref, mid_ref, w_own, w_other, out_ref, act):
    h = meta[0]
    rows, half = out_ref.shape
    out_ref[...] = last_product(
        act_ref, rim_ref, pl.multiple_of(h * (rows - EDGE), EDGE), mid_ref, w_own, w_other,
        pl.ds(pl.multiple_of(h * half, half), half), act,
    )


def finish_kernel(meta, act_ref, rim_ref, mid_ref, w_own, w_other, done_ref, out_ref, act):
    h = meta[0]
    rows, half = done_ref.shape
    out_ref[pl.ds(pl.multiple_of(h * rows, rows), rows), :] = done_ref[...]
    out_ref[pl.ds(pl.multiple_of((1 - h) * rows, rows), rows), :] = last_product(
        act_ref, rim_ref, pl.multiple_of((1 - h) * (rows - EDGE), EDGE), mid_ref, w_other, w_own,
        pl.ds(pl.multiple_of(h * half, half), half), act,
    )


def finish(meta, act, rim_act, mid, w_own, w_other, done=None):
    rows, half = mid.shape
    vmem = pl.BlockSpec(memory_space=pltpu.VMEM)
    args = (act, rim_act, mid, w_own, w_other) + (() if done is None else (done,))
    return pl.pallas_call(
        finish_own_kernel if done is None else finish_kernel,
        in_specs=[pl.BlockSpec(memory_space=pltpu.SMEM)] + [vmem] * len(args),
        out_specs=vmem,
        out_shape=jax.ShapeDtypeStruct((rows if done is None else 2 * rows, half), BF16),
        scratch_shapes=[pltpu.VMEM(act.shape, BF16)],
        compiler_params=pltpu.CompilerParams(vmem_limit_bytes=VMEM_LIMIT),
        cost_estimate=weight(1.2),
        name="finish_own" if done is None else "finish",
    )(meta, *args)


def local(
    blocks,
    frames,
    segment_ids,
    utt_valid,
    attn_gain,
    qkv_weight,
    out_weight,
    conv_gain,
    pointwise_in,
    depthwise,
    mid_gain,
    pointwise_out,
):
    rows = frames.shape[0]

    def swap(value):
        return lax.ppermute(value, "head", [(0, 1), (1, 0)])

    def shift(value, step):
        pairs = [(i, i - step if i % 2 == 0 else i + step) for i in range(blocks)]
        return lax.ppermute(value, "tm", [p for p in pairs if 0 <= p[1] < blocks])

    def exchange(value):
        return lax.ppermute(value, "tm", [(i, i ^ 1) for i in range(blocks)])

    block = lax.axis_index("tm").astype(jnp.int32)
    column = block % 2
    meta = jnp.stack([
        lax.axis_index("head").astype(jnp.int32),
        column,
        block * rows,
        (block + 1 - 2 * column) * rows,
    ])
    other = swap(frames)
    pointwise = pointwise_in.transpose(1, 0, 2)
    keep, held, send, passed = project(
        meta, frames, other, attn_gain, qkv_weight, pointwise
    )
    pair = exchange(passed)
    far_pair = shift(keep, 2)
    pair_query = exchange(send)
    far_own = shift(pair, -2)

    segment_ids, _ = lax.optimization_barrier((segment_ids, passed))
    ids = jnp.arange(utt_valid.shape[0], dtype=jnp.int32)
    counts = jnp.sum((segment_ids[None, :] == ids[:, None]).astype(jnp.int32), axis=1)
    counts = lax.all_to_all(
        jnp.broadcast_to(counts[None, :], (blocks, counts.shape[0])), "tm", 0, 0
    )
    taps = jnp.concatenate([depthwise, mid_gain[None, :]], axis=0)
    out_weight, pointwise, taps, keep = lax.optimization_barrier(
        (out_weight, pointwise, taps, keep)
    )
    pointwise_other = swap(pointwise)
    out_other = swap(out_weight)
    runs, pair_runs = bounds(meta, counts, utt_valid, rows)
    taps, pointwise_out, runs = lax.optimization_barrier((taps, pointwise_out, runs))
    taps_other = swap(taps)
    pointwise_out_other = swap(pointwise_out)
    pair, pair_query, far_pair, far_own, runs, pair_runs = lax.optimization_barrier(
        (pair, pair_query, far_pair, far_own, runs, pair_runs)
    )
    pair_context = attend(column.reshape(1), pair_query, pair, held, far_pair, pair_runs)
    pair_context = exchange(pair_context)
    context = attend((1 - column).reshape(1), held, held, pair, far_own, runs)
    contexts = (context, pair_context, swap(context), swap(pair_context))
    glu, edge, mid_keep, mid_send = gated(
        meta, contexts, frames, other, out_weight, out_other, conv_gain,
        pointwise, pointwise_other, runs,
    )
    edges = [(2 * i, 2 * (i - 1) + 1) for i in range(1, blocks)]
    edges += [(2 * i + 1, 2 * (i + 1)) for i in range(blocks - 1)]
    edge = lax.ppermute(edge, ("tm", "head"), edges)
    mid_other = swap(mid_send)
    act = convolve(meta, glu, runs, taps, taps_other)
    act_other = swap(act)
    rim_act = rim(meta, glu, edge, runs, taps, taps_other)
    rim_other = swap(rim_act)
    done = finish(meta, act, rim_act, mid_keep, pointwise_out, pointwise_out_other)
    return finish(
        meta, act_other, rim_other, mid_other, pointwise_out, pointwise_out_other, done
    )


def solution(mesh):
    in_specs = (
        P(("grp", "tm"), "head"),
        P(("grp", "tm")),
        P("grp"),
        P(),
        P(None, None, "head"),
        P("head", None),
        P(),
        P(None, None, "head"),
        P(None, "head"),
        P("head"),
        P("head", None),
    )
    out_specs = P(("grp", "tm"), "head")
    return jax.shard_map(
        functools.partial(local, mesh.shape["tm"]),
        mesh=mesh,
        in_specs=in_specs,
        out_specs=out_specs,
        check_vma=False,
    )
```

```python
import functools
import math

import jax
import jax.numpy as jnp
from jax import lax
from jax.experimental import pallas as pl
from jax.experimental.pallas import tpu as pltpu
from jax.sharding import PartitionSpec as P

HEAD_DIM = 64
CONV_CH = 512
KERNEL = 31
WIN = 512
EDGE = 16
SENT = 64
NEG = -1e30
EXP_SCALE = HEAD_DIM ** (-0.5) * math.log2(math.e)
F32 = jnp.float32
BF16 = jnp.bfloat16
VMEM_LIMIT = 16 * 1024 * 1024


def weight(microseconds):
    return pl.CostEstimate(
        flops=int(microseconds * 1.15e9), bytes_accessed=0, transcendentals=0
    )


def traffic(microseconds):
    return pl.CostEstimate(
        flops=0, bytes_accessed=int(microseconds * 3.69e6), transcendentals=0
    )


def dot(a, b):
    return jnp.dot(a, b, preferred_element_type=F32)


def normalize_halves(own, other, gain_own, gain_other):
    width = own.shape[1] + other.shape[1]
    mean = (
        jnp.sum(own, axis=1, keepdims=True) + jnp.sum(other, axis=1, keepdims=True)
    ) / width
    own = own - mean
    other = other - mean
    spread = (
        jnp.sum(own * own, axis=1, keepdims=True) + jnp.sum(other * other, axis=1, keepdims=True)
    ) / width
    scale = lax.rsqrt(spread + 1e-05)
    return (own * scale * gain_own).astype(BF16), (other * scale * gain_other).astype(BF16)


def qkv_kernel(
    meta, own_ref, other_ref, gain_ref, w_ref, _, keep_ref, hold_ref, send_ref, pass_ref
):
    h = meta[0]
    first = meta[1] == 0
    rows = own_ref.shape[0]
    tile = 256
    for at in range(0, rows, tile):
        here = slice(at, at + tile)
        n_own, n_other = normalize_halves(
            own_ref[here, :].astype(F32), other_ref[here, :].astype(F32),
            gain_ref[h], gain_ref[1 - h],
        )
        for slot, part in enumerate((1, 2, 0)):
            value = (dot(n_own, w_ref[part, h]) + dot(n_other, w_ref[part, 1 - h])).astype(BF16)
            sub = value.shape[1] // 2
            cols = slice(slot * sub, slot * sub + sub)
            keep = jnp.where(first, value[:, :sub], value[:, sub:])
            send = jnp.where(first, value[:, sub:], value[:, :sub])
            hold_ref[here, cols] = keep
            if slot < 2:
                keep_ref[here, cols] = keep
                pass_ref[here, cols] = send
            else:
                send_ref[here, :] = send


def project(meta, frames, other, gain, qkv, early):
    rows, half = frames.shape
    width = qkv.shape[2]
    vmem = pl.BlockSpec(memory_space=pltpu.VMEM)
    return pl.pallas_call(
        qkv_kernel,
        in_specs=[pl.BlockSpec(memory_space=pltpu.SMEM)]
        + [vmem] * 4
        + [pl.BlockSpec(memory_space=pl.ANY)],
        out_specs=[vmem] * 4,
        out_shape=[
            jax.ShapeDtypeStruct((rows, width), BF16),
            jax.ShapeDtypeStruct((rows, 3 * width // 2), BF16),
            jax.ShapeDtypeStruct((rows, width // 2), BF16),
            jax.ShapeDtypeStruct((rows, width), BF16),
        ],
        compiler_params=pltpu.CompilerParams(vmem_limit_bytes=VMEM_LIMIT),
        name="project",
    )(meta, frames, other, gain.reshape(2, 1, half),
      qkv.transpose(1, 0, 2).reshape(3, 2, half, width), early)


def bounds_kernel(meta, counts, valid, own_ref, pair_ref):
    utts = valid.shape[1]
    rows = own_ref.shape[0]
    square = (utts, utts)
    sub = lax.broadcasted_iota(jnp.int32, square, 0)
    lane = lax.broadcasted_iota(jnp.int32, square, 1)
    total = jnp.sum(counts[...].astype(F32), axis=0, keepdims=True)
    limit = jnp.broadcast_to(jnp.minimum(total, valid[...].astype(F32)), square)
    total = jnp.broadcast_to(total, square)
    start = jnp.sum(jnp.where(lane < sub, total, 0.0), axis=1, keepdims=True)
    stop = start + jnp.sum(jnp.where(lane == sub, limit, 0.0), axis=1, keepdims=True)
    at = lax.broadcasted_iota(jnp.int32, (utts, rows), 1).astype(F32)
    for slot, ref in enumerate((own_ref, pair_ref)):
        origin = meta[2 + slot].astype(F32)
        lo = start - origin
        hi = stop - origin
        inside = (at >= lo) & (at < hi)
        low = jnp.sum(jnp.where(inside, lo, 0.0), axis=0, keepdims=True)
        high = jnp.sum(jnp.where(inside, hi, 0.0), axis=0, keepdims=True)
        both = jnp.concatenate([low, high, jnp.zeros((126, rows), F32)], axis=0)
        ref[...] = both.T.astype(jnp.int32)


def bounds(meta, counts, valid, rows):
    vmem = pl.BlockSpec(memory_space=pltpu.VMEM)
    return pl.pallas_call(
        bounds_kernel,
        in_specs=[pl.BlockSpec(memory_space=pltpu.SMEM), vmem, vmem],
        out_specs=[vmem] * 2,
        out_shape=[jax.ShapeDtypeStruct((rows, 128), jnp.int32)] * 2,
        compiler_params=pltpu.CompilerParams(vmem_limit_bytes=VMEM_LIMIT),
        name="bounds",
    )(meta, counts, valid.reshape(1, -1))


def attend_kernel(a_high, query, center, side_a, side_b, run_ref, out_ref):
    rows = center.shape[0]
    width = side_b.shape[1] // 2
    q_cols = slice(query.shape[1] - width, query.shape[1])
    tile = rows // 2
    lane = lax.broadcasted_iota(jnp.int32, (tile, width), 1)

    def run(low_ref, high_ref):
        for block in range(2):
            at = block * tile
            pieces = (
                ((low_ref, 0, rows, -rows), (center, 0, rows, 0), (high_ref, 0, tile, rows))
                if block == 0
                else ((low_ref, tile, tile, -rows), (center, 0, rows, 0), (high_ref, 0, rows, rows))
            )
            position = lax.broadcasted_iota(jnp.int32, (tile, 1), 0) + at
            lo = run_ref[at : at + tile, 0:1]
            hi = run_ref[at : at + tile, 1:2]
            near_lo = jnp.maximum(lo, position - WIN)
            near_hi = jnp.minimum(hi, position + (WIN + 1))
            biases = []
            for _, first, size, origin in pieces:
                u = lax.broadcasted_iota(jnp.int32, (tile, size), 1) + (origin + first)
                biases.append(jnp.where((u >= near_lo) & (u < near_hi), 0.0, NEG))
            q = query[at : at + tile, q_cols]
            outs = []
            for sub in range(2):
                q_sub = jnp.where((lane >= HEAD_DIM) == (sub == 1), q, jnp.zeros_like(q))
                scores = []
                for (ref, first, size, _), bias in zip(pieces, biases):
                    s = lax.dot_general(
                        q_sub, ref[first : first + size, :width], (((1,), (1,)), ((), ())),
                        preferred_element_type=F32,
                    )
                    scores.append(s + bias)
                peak = functools.reduce(
                    jnp.maximum, [jnp.max(s, axis=1, keepdims=True) for s in scores]
                )
                total = jnp.zeros((tile, 1), F32)
                context = jnp.zeros((tile, width), F32)
                for (ref, first, size, _), s in zip(pieces, scores):
                    expw = jnp.exp2((s - peak) * EXP_SCALE)
                    total = total + jnp.sum(expw, axis=1, keepdims=True)
                    context = context + dot(
                        expw.astype(BF16), ref[first : first + size, width : 2 * width]
                    )
                outs.append(context / jnp.maximum(total, 1.0))
            joined = jnp.where(lane >= HEAD_DIM, outs[1], outs[0])
            out_ref[at : at + tile, :] = jnp.where(hi > lo, joined, 0.0).astype(BF16)

    @pl.when(a_high[0] == 1)
    def _():
        run(side_b, side_a)

    @pl.when(a_high[0] == 0)
    def _():
        run(side_a, side_b)


def attend(a_high, query, center, side_a, side_b, runs):
    rows, width = side_b.shape[0], side_b.shape[1] // 2
    vmem = pl.BlockSpec(memory_space=pltpu.VMEM)
    return pl.pallas_call(
        attend_kernel,
        in_specs=[pl.BlockSpec(memory_space=pltpu.SMEM)] + [vmem] * 5,
        out_specs=vmem,
        out_shape=jax.ShapeDtypeStruct((rows, width), BF16),
        compiler_params=pltpu.CompilerParams(vmem_limit_bytes=VMEM_LIMIT),
        cost_estimate=traffic(3),
        name="attend",
    )(a_high, query, center, side_a, side_b, runs)


def gate_kernel(
    meta,
    mine_own, pair_own, mine_other, pair_other,
    x_own, x_other,
    out_own, out_other,
    gain_ref,
    in_own, in_other,
    run_ref,
    glu_ref, edge_ref, mid_keep, mid_send,
):
    h = meta[0]
    first = meta[1] == 0
    half = x_own.shape[1]
    rows = glu_ref.shape[0]
    here = pl.ds(pl.multiple_of(h * (rows - 2 * EDGE), EDGE), rows)

    def joined(mine, pair):
        mine = mine[here, :]
        pair = pair[here, :]
        return jnp.concatenate(
            [jnp.where(first, mine, pair), jnp.where(first, pair, mine)], axis=1
        )

    depth = 2 * mine_own.shape[1]
    c_own = joined(mine_own, pair_own)
    c_other = joined(mine_other, pair_other)
    own_cols = pl.ds(pl.multiple_of(h * half, half), half)
    other_cols = pl.ds(pl.multiple_of((1 - h) * half, half), half)

    def mid(cols, x_ref):
        first = dot(c_own, out_own[:depth, cols]).astype(BF16).astype(F32)
        second = dot(c_other, out_other[:depth, cols]).astype(BF16).astype(F32)
        return (x_ref[here, :].astype(F32) + (first + second)).astype(BF16)

    m_own = mid(own_cols, x_own)
    m_other = mid(other_cols, x_other)
    keep = rows - EDGE

    @pl.when(h == 0)
    def _():
        mid_keep[...] = m_own[:keep]
        mid_send[...] = m_other[:keep]

    @pl.when(h == 1)
    def _():
        mid_keep[...] = m_own[EDGE:]
        mid_send[...] = m_other[EDGE:]

    n_own, n_other = normalize_halves(
        m_own.astype(F32), m_other.astype(F32), gain_ref[h], gain_ref[1 - h]
    )
    run = run_ref[here, :]
    valid = run[:, 1:2] > run[:, 0:1]
    glus = []
    for w_ref in (in_own, in_other):
        value = dot(n_own, w_ref[0, own_cols, :]) + dot(n_other, w_ref[0, other_cols, :])
        gate = dot(n_own, w_ref[1, own_cols, :]) + dot(n_other, w_ref[1, other_cols, :])
        glu = value / (1.0 + jnp.exp(-gate))
        glus.append(jnp.where(valid, glu, 0.0).astype(BF16))
    chan = glus[0].shape[1]
    glu_ref[:, :chan] = glus[0]
    glu_ref[:, chan:] = glus[1]

    @pl.when(h == 0)
    def _():
        edge_ref[:, :chan] = glus[1][:SENT]
        edge_ref[:, chan:] = glus[0][:SENT]

    @pl.when(h == 1)
    def _():
        edge_ref[:, :chan] = glus[1][rows - SENT :]
        edge_ref[:, chan:] = glus[0][rows - SENT :]


def gated(meta, contexts, x_own, x_other, out_own, out_other, gain, in_own, in_other, runs):
    rows = x_own.shape[0] // 2 + EDGE
    half = x_own.shape[1]
    chan = in_own.shape[2]
    vmem = pl.BlockSpec(memory_space=pltpu.VMEM)
    return pl.pallas_call(
        gate_kernel,
        in_specs=[pl.BlockSpec(memory_space=pltpu.SMEM)] + [vmem] * 12,
        out_specs=[vmem] * 4,
        out_shape=[
            jax.ShapeDtypeStruct((rows, 2 * chan), BF16),
            jax.ShapeDtypeStruct((SENT, 2 * chan), BF16),
            jax.ShapeDtypeStruct((rows - EDGE, half), BF16),
            jax.ShapeDtypeStruct((rows - EDGE, half), BF16),
        ],
        compiler_params=pltpu.CompilerParams(vmem_limit_bytes=VMEM_LIMIT),
        cost_estimate=traffic(3),
        name="gated",
    )(meta, *contexts, x_own, x_other, out_own, out_other,
      gain.reshape(2, 1, half), in_own, in_other, runs)


def conv_rows(shifted, low, high, taps, out_ref, rows):
    width = out_ref.shape[1]
    chan = width // 2
    reach = KERNEL // 2
    step = min(32, rows)
    cols = range(0, width, 128)
    weights = [
        [
            (taps[0] if col < chan else taps[1])[tap : tap + 1, col % chan : col % chan + 128]
            for col in cols
        ]
        for tap in range(KERNEL + 1)
    ]
    for base in range(0, rows, step):
        totals = [jnp.zeros((step, 128), F32) for _ in cols]
        for tap in range(KERNEL):
            shift = tap - reach
            same = (low[base : base + step] <= shift) & (high[base : base + step] > shift)
            row = base + EDGE + shift
            first = row - row % 8
            for index, col in enumerate(cols):
                piece = shifted[row % 8, first : first + step, col : col + 128]
                totals[index] = totals[index] + jnp.where(same, piece, 0.0) * weights[tap][index]
        mean = jnp.sum(sum(totals), axis=1, keepdims=True) / CONV_CH
        square = jnp.sum(sum(t * t for t in totals), axis=1, keepdims=True) / CONV_CH
        scale = lax.rsqrt(square - mean * mean + 1e-05)
        for index, col in enumerate(cols):
            y = (totals[index] - mean) * scale * weights[KERNEL][index]
            out_ref[base : base + step, col : col + 128] = (y / (1.0 + jnp.exp(-y))).astype(BF16)


def run_offsets(run_ref, first, rows):
    run = run_ref[pl.ds(first, rows), :]
    at = lax.broadcasted_iota(jnp.int32, (rows, 128), 0) + first
    low = jnp.broadcast_to(run[:, 0:1], (rows, 128)) - at
    high = jnp.broadcast_to(run[:, 1:2], (rows, 128)) - at
    return low, high


def conv_kernel(meta, glu_ref, run_ref, taps_own, taps_other, act_ref, ext, shifted):
    h = meta[0]
    rows, width = act_ref.shape
    got = glu_ref.shape[0]
    ext[pl.ds(pl.multiple_of(h * got, EDGE), EDGE), :] = jnp.zeros((EDGE, width), F32)
    ext[pl.ds(pl.multiple_of((1 - h) * EDGE, EDGE), got), :] = glu_ref[...].astype(F32)
    size = shifted.shape[1]
    for s in range(8):
        shifted[s] = ext[s : s + size, :]
    low, high = run_offsets(run_ref, pl.multiple_of(h * rows, rows), rows)
    conv_rows(shifted, low, high, (taps_own, taps_other), act_ref, rows)


def convolve(meta, glu, runs, taps_own, taps_other):
    rows = glu.shape[0] - EDGE
    width = glu.shape[1]
    vmem = pl.BlockSpec(memory_space=pltpu.VMEM)
    return pl.pallas_call(
        conv_kernel,
        in_specs=[pl.BlockSpec(memory_space=pltpu.SMEM)] + [vmem] * 4,
        out_specs=vmem,
        out_shape=jax.ShapeDtypeStruct((rows, width), BF16),
        scratch_shapes=[
            pltpu.VMEM((rows + 2 * EDGE, width), F32),
            pltpu.VMEM((8, rows + 2 * EDGE - 8, width), F32),
        ],
        compiler_params=pltpu.CompilerParams(vmem_limit_bytes=VMEM_LIMIT),
        cost_estimate=weight(3),
        name="convolve",
    )(meta, glu, runs, taps_own, taps_other)


def rim_kernel(meta, glu_ref, edge_ref, run_ref, taps_own, taps_other, act_ref, ext, shifted):
    h = meta[0]
    got = glu_ref.shape[0]
    near = 2 * EDGE
    ext[pl.ds(pl.multiple_of(h * near, EDGE), EDGE), :] = edge_ref[
        pl.ds(pl.multiple_of((1 - h) * (SENT - EDGE), EDGE), EDGE), :
    ].astype(F32)
    ext[pl.ds(pl.multiple_of((1 - h) * EDGE, EDGE), near), :] = glu_ref[
        pl.ds(pl.multiple_of(h * (got - near), EDGE), near), :
    ].astype(F32)
    size = shifted.shape[1]
    for s in range(8):
        shifted[s] = ext[s : s + size, :]
    first = pl.multiple_of(h * (run_ref.shape[0] - EDGE), EDGE)
    low, high = run_offsets(run_ref, first, EDGE)
    conv_rows(shifted, low, high, (taps_own, taps_other), act_ref, EDGE)


def rim(meta, glu, edge, runs, taps_own, taps_other):
    width = glu.shape[1]
    vmem = pl.BlockSpec(memory_space=pltpu.VMEM)
    return pl.pallas_call(
        rim_kernel,
        in_specs=[pl.BlockSpec(memory_space=pltpu.SMEM)] + [vmem] * 5,
        out_specs=vmem,
        out_shape=jax.ShapeDtypeStruct((EDGE, width), BF16),
        scratch_shapes=[
            pltpu.VMEM((3 * EDGE, width), F32),
            pltpu.VMEM((8, 3 * EDGE - 8, width), F32),
        ],
        compiler_params=pltpu.CompilerParams(vmem_limit_bytes=VMEM_LIMIT),
        cost_estimate=weight(1),
        name="rim",
    )(meta, glu, edge, runs, taps_own, taps_other)


def last_product(act_ref, rim_ref, rim_at, mid_ref, w_first, w_second, cols, act):
    chan = act_ref.shape[1] // 2
    act[...] = act_ref[...]
    act[pl.ds(rim_at, EDGE), :] = rim_ref[...]
    below = w_first.shape[0] - chan
    first = dot(act[:, :chan], w_first[below:, cols]).astype(BF16).astype(F32)
    second = dot(act[:, chan:], w_second[below:, cols]).astype(BF16).astype(F32)
    return (mid_ref[...].astype(F32) + (first + second)).astype(BF16)


def finish_own_kernel(meta, act_ref, rim_ref, mid_ref, w_own, w_other, out_ref, act):
    h = meta[0]
    rows, half = out_ref.shape
    out_ref[...] = last_product(
        act_ref, rim_ref, pl.multiple_of(h * (rows - EDGE), EDGE), mid_ref, w_own, w_other,
        pl.ds(pl.multiple_of(h * half, half), half), act,
    )


def finish_kernel(meta, act_ref, rim_ref, mid_ref, w_own, w_other, done_ref, out_ref, act):
    h = meta[0]
    rows, half = done_ref.shape
    out_ref[pl.ds(pl.multiple_of(h * rows, rows), rows), :] = done_ref[...]
    out_ref[pl.ds(pl.multiple_of((1 - h) * rows, rows), rows), :] = last_product(
        act_ref, rim_ref, pl.multiple_of((1 - h) * (rows - EDGE), EDGE), mid_ref, w_other, w_own,
        pl.ds(pl.multiple_of(h * half, half), half), act,
    )


def finish(meta, act, rim_act, mid, w_own, w_other, done=None):
    rows, half = mid.shape
    vmem = pl.BlockSpec(memory_space=pltpu.VMEM)
    args = (act, rim_act, mid, w_own, w_other) + (() if done is None else (done,))
    return pl.pallas_call(
        finish_own_kernel if done is None else finish_kernel,
        in_specs=[pl.BlockSpec(memory_space=pltpu.SMEM)] + [vmem] * len(args),
        out_specs=vmem,
        out_shape=jax.ShapeDtypeStruct((rows if done is None else 2 * rows, half), BF16),
        scratch_shapes=[pltpu.VMEM(act.shape, BF16)],
        compiler_params=pltpu.CompilerParams(vmem_limit_bytes=VMEM_LIMIT),
        cost_estimate=weight(1.2),
        name="finish_own" if done is None else "finish",
    )(meta, *args)


def local(
    blocks,
    frames,
    segment_ids,
    utt_valid,
    attn_gain,
    qkv_weight,
    out_weight,
    conv_gain,
    pointwise_in,
    depthwise,
    mid_gain,
    pointwise_out,
):
    rows = frames.shape[0]

    def swap(value):
        return lax.ppermute(value, "head", [(0, 1), (1, 0)])

    def shift(value, step):
        pairs = [(i, i - step if i % 2 == 0 else i + step) for i in range(blocks)]
        return lax.ppermute(value, "tm", [p for p in pairs if 0 <= p[1] < blocks])

    def exchange(value):
        return lax.ppermute(value, "tm", [(i, i ^ 1) for i in range(blocks)])

    block = lax.axis_index("tm").astype(jnp.int32)
    column = block % 2
    meta = jnp.stack([
        lax.axis_index("head").astype(jnp.int32),
        column,
        block * rows,
        (block + 1 - 2 * column) * rows,
    ])
    other = swap(frames)
    pointwise = pointwise_in.transpose(1, 0, 2)
    keep, held, send, passed = project(
        meta, frames, other, attn_gain, qkv_weight, pointwise
    )
    pair = exchange(passed)
    far_pair = shift(keep, 2)
    pair_query = exchange(send)

    segment_ids, _ = lax.optimization_barrier((segment_ids, passed))
    ids = jnp.arange(utt_valid.shape[0], dtype=jnp.int32)
    counts = jnp.sum((segment_ids[None, :] == ids[:, None]).astype(jnp.int32), axis=1)
    counts = lax.all_to_all(
        jnp.broadcast_to(counts[None, :], (blocks, counts.shape[0])), "tm", 0, 0
    )
    pair, counts = lax.optimization_barrier((pair, counts))
    far_own = shift(pair, -2)
    taps = jnp.concatenate([depthwise, mid_gain[None, :]], axis=0)
    out_weight, pointwise, taps, keep = lax.optimization_barrier(
        (out_weight, pointwise, taps, keep)
    )
    pointwise_other = swap(pointwise)
    out_other = swap(out_weight)
    runs, pair_runs = bounds(meta, counts, utt_valid, rows)
    taps, pointwise_out, runs = lax.optimization_barrier((taps, pointwise_out, runs))
    taps_other = swap(taps)
    pointwise_out_other = swap(pointwise_out)
    pair, pair_query, far_pair, runs, pair_runs = lax.optimization_barrier(
        (pair, pair_query, far_pair, runs, pair_runs)
    )
    pair_context = attend(column.reshape(1), pair_query, pair, held, far_pair, pair_runs)
    pair_context = exchange(pair_context)
    context = attend((1 - column).reshape(1), held, held, pair, far_own, runs)
    context, pair_context = lax.optimization_barrier((context, pair_context))
    contexts = (context, pair_context, swap(context), swap(pair_context))
    glu, edge, mid_keep, mid_send = gated(
        meta, contexts, frames, other, out_weight, out_other, conv_gain,
        pointwise, pointwise_other, runs,
    )
    edges = [(2 * i, 2 * (i - 1) + 1) for i in range(1, blocks)]
    edges += [(2 * i + 1, 2 * (i + 1)) for i in range(blocks - 1)]
    edge = lax.ppermute(edge, ("tm", "head"), edges)
    mid_other = swap(mid_send)
    act = convolve(meta, glu, runs, taps, taps_other)
    act_other = swap(act)
    rim_act = rim(meta, glu, edge, runs, taps, taps_other)
    rim_other = swap(rim_act)
    done = finish(meta, act, rim_act, mid_keep, pointwise_out, pointwise_out_other)
    return finish(
        meta, act_other, rim_other, mid_other, pointwise_out, pointwise_out_other, done
    )


def solution(mesh):
    in_specs = (
        P(("grp", "tm"), "head"),
        P(("grp", "tm")),
        P("grp"),
        P(),
        P(None, None, "head"),
        P("head", None),
        P(),
        P(None, None, "head"),
        P(None, "head"),
        P("head"),
        P("head", None),
    )
    out_specs = P(("grp", "tm"), "head")
    return jax.shard_map(
        functools.partial(local, mesh.shape["tm"]),
        mesh=mesh,
        in_specs=in_specs,
        out_specs=out_specs,
        check_vma=False,
    )
```

```python
import functools
import math

import jax
import jax.numpy as jnp
from jax import lax
from jax.experimental import pallas as pl
from jax.experimental.pallas import tpu as pltpu
from jax.sharding import PartitionSpec as P

HEAD_DIM = 64
CONV_CH = 512
KERNEL = 31
WIN = 512
EDGE = 16
SENT = 64
NEG = -1e30
EXP_SCALE = HEAD_DIM ** (-0.5) * math.log2(math.e)
F32 = jnp.float32
BF16 = jnp.bfloat16
VMEM_LIMIT = 16 * 1024 * 1024


def weight(microseconds):
    return pl.CostEstimate(
        flops=int(microseconds * 1.15e9), bytes_accessed=0, transcendentals=0
    )


def traffic(microseconds):
    return pl.CostEstimate(
        flops=0, bytes_accessed=int(microseconds * 3.69e6), transcendentals=0
    )


def dot(a, b):
    return jnp.dot(a, b, preferred_element_type=F32)


def normalize_halves(own, other, gain_own, gain_other):
    width = own.shape[1] + other.shape[1]
    mean = (
        jnp.sum(own, axis=1, keepdims=True) + jnp.sum(other, axis=1, keepdims=True)
    ) / width
    own = own - mean
    other = other - mean
    spread = (
        jnp.sum(own * own, axis=1, keepdims=True) + jnp.sum(other * other, axis=1, keepdims=True)
    ) / width
    scale = lax.rsqrt(spread + 1e-05)
    return (own * scale * gain_own).astype(BF16), (other * scale * gain_other).astype(BF16)


def qkv_kernel(
    meta, own_ref, other_ref, gain_ref, w_ref, _, keep_ref, hold_ref, send_ref, pass_ref
):
    h = meta[0]
    first = meta[1] == 0
    rows = own_ref.shape[0]
    tile = 256
    for at in range(0, rows, tile):
        here = slice(at, at + tile)
        n_own, n_other = normalize_halves(
            own_ref[here, :].astype(F32), other_ref[here, :].astype(F32),
            gain_ref[h], gain_ref[1 - h],
        )
        for slot, part in enumerate((1, 2, 0)):
            value = (dot(n_own, w_ref[part, h]) + dot(n_other, w_ref[part, 1 - h])).astype(BF16)
            sub = value.shape[1] // 2
            cols = slice(slot * sub, slot * sub + sub)
            keep = jnp.where(first, value[:, :sub], value[:, sub:])
            send = jnp.where(first, value[:, sub:], value[:, :sub])
            send_ref[here, cols] = send
            hold_ref[here, cols] = keep
            if slot < 2:
                keep_ref[here, cols] = keep
                pass_ref[here, cols] = send


def project(meta, frames, other, gain, qkv, early):
    rows, half = frames.shape
    width = qkv.shape[2]
    vmem = pl.BlockSpec(memory_space=pltpu.VMEM)
    return pl.pallas_call(
        qkv_kernel,
        in_specs=[pl.BlockSpec(memory_space=pltpu.SMEM)]
        + [vmem] * 4
        + [pl.BlockSpec(memory_space=pl.ANY)],
        out_specs=[vmem] * 4,
        out_shape=[
            jax.ShapeDtypeStruct((rows, width), BF16),
            jax.ShapeDtypeStruct((rows, 3 * width // 2), BF16),
            jax.ShapeDtypeStruct((rows, 3 * width // 2), BF16),
            jax.ShapeDtypeStruct((rows, width), BF16),
        ],
        compiler_params=pltpu.CompilerParams(vmem_limit_bytes=VMEM_LIMIT),
        name="project",
    )(meta, frames, other, gain.reshape(2, 1, half),
      qkv.transpose(1, 0, 2).reshape(3, 2, half, width), early)


def bounds_kernel(meta, counts, valid, own_ref, pair_ref):
    utts = valid.shape[1]
    rows = own_ref.shape[0]
    square = (utts, utts)
    sub = lax.broadcasted_iota(jnp.int32, square, 0)
    lane = lax.broadcasted_iota(jnp.int32, square, 1)
    total = jnp.sum(counts[...].astype(F32), axis=0, keepdims=True)
    limit = jnp.broadcast_to(jnp.minimum(total, valid[...].astype(F32)), square)
    total = jnp.broadcast_to(total, square)
    start = jnp.sum(jnp.where(lane < sub, total, 0.0), axis=1, keepdims=True)
    stop = start + jnp.sum(jnp.where(lane == sub, limit, 0.0), axis=1, keepdims=True)
    at = lax.broadcasted_iota(jnp.int32, (utts, rows), 1).astype(F32)
    for slot, ref in enumerate((own_ref, pair_ref)):
        origin = meta[2 + slot].astype(F32)
        lo = start - origin
        hi = stop - origin
        inside = (at >= lo) & (at < hi)
        low = jnp.sum(jnp.where(inside, lo, 0.0), axis=0, keepdims=True)
        high = jnp.sum(jnp.where(inside, hi, 0.0), axis=0, keepdims=True)
        both = jnp.concatenate([low, high, jnp.zeros((126, rows), F32)], axis=0)
        ref[...] = both.T.astype(jnp.int32)


def bounds(meta, counts, valid, rows):
    vmem = pl.BlockSpec(memory_space=pltpu.VMEM)
    return pl.pallas_call(
        bounds_kernel,
        in_specs=[pl.BlockSpec(memory_space=pltpu.SMEM), vmem, vmem],
        out_specs=[vmem] * 2,
        out_shape=[jax.ShapeDtypeStruct((rows, 128), jnp.int32)] * 2,
        compiler_params=pltpu.CompilerParams(vmem_limit_bytes=VMEM_LIMIT),
        name="bounds",
    )(meta, counts, valid.reshape(1, -1))


def attend_kernel(a_high, query, center, side_a, side_b, run_ref, *refs):
    out_ref = refs[-1]
    rows = center.shape[0]
    width = center.shape[1] // 3
    q_cols = slice(query.shape[1] - width, query.shape[1])
    tile = rows // 2
    lane = lax.broadcasted_iota(jnp.int32, (tile, width), 1)

    def run(low_ref, high_ref):
        for block in range(2):
            at = block * tile
            pieces = (
                ((low_ref, 0, rows, -rows), (center, 0, rows, 0), (high_ref, 0, tile, rows))
                if block == 0
                else ((low_ref, tile, tile, -rows), (center, 0, rows, 0), (high_ref, 0, rows, rows))
            )
            position = lax.broadcasted_iota(jnp.int32, (tile, 1), 0) + at
            lo = run_ref[at : at + tile, 0:1]
            hi = run_ref[at : at + tile, 1:2]
            near_lo = jnp.maximum(lo, position - WIN)
            near_hi = jnp.minimum(hi, position + (WIN + 1))
            biases = []
            for _, first, size, origin in pieces:
                u = lax.broadcasted_iota(jnp.int32, (tile, size), 1) + (origin + first)
                biases.append(jnp.where((u >= near_lo) & (u < near_hi), 0.0, NEG))
            q = query[at : at + tile, q_cols]
            outs = []
            for sub in range(2):
                q_sub = jnp.where((lane >= HEAD_DIM) == (sub == 1), q, jnp.zeros_like(q))
                scores = []
                for (ref, first, size, _), bias in zip(pieces, biases):
                    s = lax.dot_general(
                        q_sub, ref[first : first + size, :width], (((1,), (1,)), ((), ())),
                        preferred_element_type=F32,
                    )
                    scores.append(s + bias)
                peak = functools.reduce(
                    jnp.maximum, [jnp.max(s, axis=1, keepdims=True) for s in scores]
                )
                total = jnp.zeros((tile, 1), F32)
                context = jnp.zeros((tile, width), F32)
                for (ref, first, size, _), s in zip(pieces, scores):
                    expw = jnp.exp2((s - peak) * EXP_SCALE)
                    total = total + jnp.sum(expw, axis=1, keepdims=True)
                    context = context + dot(
                        expw.astype(BF16), ref[first : first + size, width : 2 * width]
                    )
                outs.append(context / jnp.maximum(total, 1.0))
            joined = jnp.where(lane >= HEAD_DIM, outs[1], outs[0])
            out_ref[at : at + tile, :] = jnp.where(hi > lo, joined, 0.0).astype(BF16)

    @pl.when(a_high[0] == 1)
    def _():
        run(side_b, side_a)

    @pl.when(a_high[0] == 0)
    def _():
        run(side_a, side_b)


def attend(a_high, query, center, side_a, side_b, runs, held):
    anywhere = [pl.BlockSpec(memory_space=pl.ANY)] * len(held)
    rows, width = side_b.shape[0], side_b.shape[1] // 2
    vmem = pl.BlockSpec(memory_space=pltpu.VMEM)
    return pl.pallas_call(
        attend_kernel,
        in_specs=[pl.BlockSpec(memory_space=pltpu.SMEM)] + [vmem] * 5 + anywhere,
        out_specs=vmem,
        out_shape=jax.ShapeDtypeStruct((rows, width), BF16),
        compiler_params=pltpu.CompilerParams(vmem_limit_bytes=VMEM_LIMIT),
        cost_estimate=traffic(3),
        name="attend",
    )(a_high, query, center, side_a, side_b, runs, *held)


def gate_kernel(
    meta,
    mine_own, pair_own, mine_other, pair_other,
    x_own, x_other,
    out_own, out_other,
    gain_ref,
    in_own, in_other,
    run_ref,
    glu_ref, edge_ref, mid_keep, mid_send,
):
    h = meta[0]
    first = meta[1] == 0
    half = x_own.shape[1]
    rows = glu_ref.shape[0]
    here = pl.ds(pl.multiple_of(h * (rows - 2 * EDGE), EDGE), rows)

    def joined(mine, pair):
        mine = mine[here, :]
        pair = pair[here, :]
        return jnp.concatenate(
            [jnp.where(first, mine, pair), jnp.where(first, pair, mine)], axis=1
        )

    depth = 2 * mine_own.shape[1]
    c_own = joined(mine_own, pair_own)
    c_other = joined(mine_other, pair_other)
    own_cols = pl.ds(pl.multiple_of(h * half, half), half)
    other_cols = pl.ds(pl.multiple_of((1 - h) * half, half), half)

    def mid(cols, x_ref):
        first = dot(c_own, out_own[:depth, cols]).astype(BF16).astype(F32)
        second = dot(c_other, out_other[:depth, cols]).astype(BF16).astype(F32)
        return (x_ref[here, :].astype(F32) + (first + second)).astype(BF16)

    m_own = mid(own_cols, x_own)
    m_other = mid(other_cols, x_other)
    keep = rows - EDGE

    @pl.when(h == 0)
    def _():
        mid_keep[...] = m_own[:keep]
        mid_send[...] = m_other[:keep]

    @pl.when(h == 1)
    def _():
        mid_keep[...] = m_own[EDGE:]
        mid_send[...] = m_other[EDGE:]

    n_own, n_other = normalize_halves(
        m_own.astype(F32), m_other.astype(F32), gain_ref[h], gain_ref[1 - h]
    )
    run = run_ref[here, :]
    valid = run[:, 1:2] > run[:, 0:1]
    glus = []
    for w_ref in (in_own, in_other):
        value = dot(n_own, w_ref[0, own_cols, :]) + dot(n_other, w_ref[0, other_cols, :])
        gate = dot(n_own, w_ref[1, own_cols, :]) + dot(n_other, w_ref[1, other_cols, :])
        glu = value / (1.0 + jnp.exp(-gate))
        glus.append(jnp.where(valid, glu, 0.0).astype(BF16))
    chan = glus[0].shape[1]
    glu_ref[:, :chan] = glus[0]
    glu_ref[:, chan:] = glus[1]

    @pl.when(h == 0)
    def _():
        edge_ref[:, :chan] = glus[1][:SENT]
        edge_ref[:, chan:] = glus[0][:SENT]

    @pl.when(h == 1)
    def _():
        edge_ref[:, :chan] = glus[1][rows - SENT :]
        edge_ref[:, chan:] = glus[0][rows - SENT :]


def gated(meta, contexts, x_own, x_other, out_own, out_other, gain, in_own, in_other, runs):
    rows = x_own.shape[0] // 2 + EDGE
    half = x_own.shape[1]
    chan = in_own.shape[2]
    vmem = pl.BlockSpec(memory_space=pltpu.VMEM)
    return pl.pallas_call(
        gate_kernel,
        in_specs=[pl.BlockSpec(memory_space=pltpu.SMEM)] + [vmem] * 12,
        out_specs=[vmem] * 4,
        out_shape=[
            jax.ShapeDtypeStruct((rows, 2 * chan), BF16),
            jax.ShapeDtypeStruct((SENT, 2 * chan), BF16),
            jax.ShapeDtypeStruct((rows - EDGE, half), BF16),
            jax.ShapeDtypeStruct((rows - EDGE, half), BF16),
        ],
        compiler_params=pltpu.CompilerParams(vmem_limit_bytes=VMEM_LIMIT),
        cost_estimate=traffic(3),
        name="gated",
    )(meta, *contexts, x_own, x_other, out_own, out_other,
      gain.reshape(2, 1, half), in_own, in_other, runs)


def conv_rows(shifted, low, high, taps, out_ref, rows):
    width = out_ref.shape[1]
    chan = width // 2
    reach = KERNEL // 2
    step = min(32, rows)
    cols = range(0, width, 128)
    weights = [
        [
            (taps[0] if col < chan else taps[1])[tap : tap + 1, col % chan : col % chan + 128]
            for col in cols
        ]
        for tap in range(KERNEL + 1)
    ]
    for base in range(0, rows, step):
        totals = [jnp.zeros((step, 128), F32) for _ in cols]
        for tap in range(KERNEL):
            shift = tap - reach
            same = (low[base : base + step] <= shift) & (high[base : base + step] > shift)
            row = base + EDGE + shift
            first = row - row % 8
            for index, col in enumerate(cols):
                piece = shifted[row % 8, first : first + step, col : col + 128]
                totals[index] = totals[index] + jnp.where(same, piece, 0.0) * weights[tap][index]
        mean = jnp.sum(sum(totals), axis=1, keepdims=True) / CONV_CH
        square = jnp.sum(sum(t * t for t in totals), axis=1, keepdims=True) / CONV_CH
        scale = lax.rsqrt(square - mean * mean + 1e-05)
        for index, col in enumerate(cols):
            y = (totals[index] - mean) * scale * weights[KERNEL][index]
            out_ref[base : base + step, col : col + 128] = (y / (1.0 + jnp.exp(-y))).astype(BF16)


def run_offsets(run_ref, first, rows):
    run = run_ref[pl.ds(first, rows), :]
    at = lax.broadcasted_iota(jnp.int32, (rows, 128), 0) + first
    low = jnp.broadcast_to(run[:, 0:1], (rows, 128)) - at
    high = jnp.broadcast_to(run[:, 1:2], (rows, 128)) - at
    return low, high


def conv_kernel(meta, glu_ref, run_ref, taps_own, taps_other, act_ref, ext, shifted):
    h = meta[0]
    rows, width = act_ref.shape
    got = glu_ref.shape[0]
    ext[pl.ds(pl.multiple_of(h * got, EDGE), EDGE), :] = jnp.zeros((EDGE, width), F32)
    ext[pl.ds(pl.multiple_of((1 - h) * EDGE, EDGE), got), :] = glu_ref[...].astype(F32)
    size = shifted.shape[1]
    for s in range(8):
        shifted[s] = ext[s : s + size, :]
    low, high = run_offsets(run_ref, pl.multiple_of(h * rows, rows), rows)
    conv_rows(shifted, low, high, (taps_own, taps_other), act_ref, rows)


def convolve(meta, glu, runs, taps_own, taps_other):
    rows = glu.shape[0] - EDGE
    width = glu.shape[1]
    vmem = pl.BlockSpec(memory_space=pltpu.VMEM)
    return pl.pallas_call(
        conv_kernel,
        in_specs=[pl.BlockSpec(memory_space=pltpu.SMEM)] + [vmem] * 4,
        out_specs=vmem,
        out_shape=jax.ShapeDtypeStruct((rows, width), BF16),
        scratch_shapes=[
            pltpu.VMEM((rows + 2 * EDGE, width), F32),
            pltpu.VMEM((8, rows + 2 * EDGE - 8, width), F32),
        ],
        compiler_params=pltpu.CompilerParams(vmem_limit_bytes=VMEM_LIMIT),
        cost_estimate=weight(3),
        name="convolve",
    )(meta, glu, runs, taps_own, taps_other)


def rim_kernel(meta, glu_ref, edge_ref, run_ref, taps_own, taps_other, act_ref, ext, shifted):
    h = meta[0]
    got = glu_ref.shape[0]
    near = 2 * EDGE
    ext[pl.ds(pl.multiple_of(h * near, EDGE), EDGE), :] = edge_ref[
        pl.ds(pl.multiple_of((1 - h) * (SENT - EDGE), EDGE), EDGE), :
    ].astype(F32)
    ext[pl.ds(pl.multiple_of((1 - h) * EDGE, EDGE), near), :] = glu_ref[
        pl.ds(pl.multiple_of(h * (got - near), EDGE), near), :
    ].astype(F32)
    size = shifted.shape[1]
    for s in range(8):
        shifted[s] = ext[s : s + size, :]
    first = pl.multiple_of(h * (run_ref.shape[0] - EDGE), EDGE)
    low, high = run_offsets(run_ref, first, EDGE)
    conv_rows(shifted, low, high, (taps_own, taps_other), act_ref, EDGE)


def rim(meta, glu, edge, runs, taps_own, taps_other):
    width = glu.shape[1]
    vmem = pl.BlockSpec(memory_space=pltpu.VMEM)
    return pl.pallas_call(
        rim_kernel,
        in_specs=[pl.BlockSpec(memory_space=pltpu.SMEM)] + [vmem] * 5,
        out_specs=vmem,
        out_shape=jax.ShapeDtypeStruct((EDGE, width), BF16),
        scratch_shapes=[
            pltpu.VMEM((3 * EDGE, width), F32),
            pltpu.VMEM((8, 3 * EDGE - 8, width), F32),
        ],
        compiler_params=pltpu.CompilerParams(vmem_limit_bytes=VMEM_LIMIT),
        cost_estimate=weight(1),
        name="rim",
    )(meta, glu, edge, runs, taps_own, taps_other)


def last_product(act_ref, rim_ref, rim_at, mid_ref, w_first, w_second, cols, act):
    chan = act_ref.shape[1] // 2
    act[...] = act_ref[...]
    act[pl.ds(rim_at, EDGE), :] = rim_ref[...]
    below = w_first.shape[0] - chan
    first = dot(act[:, :chan], w_first[below:, cols]).astype(BF16).astype(F32)
    second = dot(act[:, chan:], w_second[below:, cols]).astype(BF16).astype(F32)
    return (mid_ref[...].astype(F32) + (first + second)).astype(BF16)


def finish_own_kernel(meta, act_ref, rim_ref, mid_ref, w_own, w_other, out_ref, act):
    h = meta[0]
    rows, half = out_ref.shape
    out_ref[...] = last_product(
        act_ref, rim_ref, pl.multiple_of(h * (rows - EDGE), EDGE), mid_ref, w_own, w_other,
        pl.ds(pl.multiple_of(h * half, half), half), act,
    )


def finish_kernel(meta, act_ref, rim_ref, mid_ref, w_own, w_other, done_ref, out_ref, act):
    h = meta[0]
    rows, half = done_ref.shape
    out_ref[pl.ds(pl.multiple_of(h * rows, rows), rows), :] = done_ref[...]
    out_ref[pl.ds(pl.multiple_of((1 - h) * rows, rows), rows), :] = last_product(
        act_ref, rim_ref, pl.multiple_of((1 - h) * (rows - EDGE), EDGE), mid_ref, w_other, w_own,
        pl.ds(pl.multiple_of(h * half, half), half), act,
    )


def finish(meta, act, rim_act, mid, w_own, w_other, done=None):
    rows, half = mid.shape
    vmem = pl.BlockSpec(memory_space=pltpu.VMEM)
    args = (act, rim_act, mid, w_own, w_other) + (() if done is None else (done,))
    return pl.pallas_call(
        finish_own_kernel if done is None else finish_kernel,
        in_specs=[pl.BlockSpec(memory_space=pltpu.SMEM)] + [vmem] * len(args),
        out_specs=vmem,
        out_shape=jax.ShapeDtypeStruct((rows if done is None else 2 * rows, half), BF16),
        scratch_shapes=[pltpu.VMEM(act.shape, BF16)],
        compiler_params=pltpu.CompilerParams(vmem_limit_bytes=VMEM_LIMIT),
        cost_estimate=weight(1.2),
        name="finish_own" if done is None else "finish",
    )(meta, *args)


def local(
    blocks,
    frames,
    segment_ids,
    utt_valid,
    attn_gain,
    qkv_weight,
    out_weight,
    conv_gain,
    pointwise_in,
    depthwise,
    mid_gain,
    pointwise_out,
):
    rows = frames.shape[0]

    def swap(value):
        return lax.ppermute(value, "head", [(0, 1), (1, 0)])

    def shift(value, step):
        pairs = [(i, i - step if i % 2 == 0 else i + step) for i in range(blocks)]
        return lax.ppermute(value, "tm", [p for p in pairs if 0 <= p[1] < blocks])

    def exchange(value):
        return lax.ppermute(value, "tm", [(i, i ^ 1) for i in range(blocks)])

    block = lax.axis_index("tm").astype(jnp.int32)
    column = block % 2
    meta = jnp.stack([
        lax.axis_index("head").astype(jnp.int32),
        column,
        block * rows,
        (block + 1 - 2 * column) * rows,
    ])
    other = swap(frames)
    pointwise = pointwise_in.transpose(1, 0, 2)
    keep, held, send, passed = project(
        meta, frames, other, attn_gain, qkv_weight, pointwise
    )
    far_own = shift(passed, 1)
    pair = exchange(send)
    far_pair = shift(keep, 2)

    segment_ids, _ = lax.optimization_barrier((segment_ids, passed))
    ids = jnp.arange(utt_valid.shape[0], dtype=jnp.int32)
    counts = jnp.sum((segment_ids[None, :] == ids[:, None]).astype(jnp.int32), axis=1)
    counts = lax.all_to_all(
        jnp.broadcast_to(counts[None, :], (blocks, counts.shape[0])), "tm", 0, 0
    )
    taps = jnp.concatenate([depthwise, mid_gain[None, :]], axis=0)
    out_weight, pointwise, taps, keep = lax.optimization_barrier(
        (out_weight, pointwise, taps, keep)
    )
    pointwise_other = swap(pointwise)
    out_other = swap(out_weight)
    runs, pair_runs = bounds(meta, counts, utt_valid, rows)
    taps, pointwise_out, runs = lax.optimization_barrier((taps, pointwise_out, runs))
    taps_other = swap(taps)
    pointwise_out_other = swap(pointwise_out)
    pair, far_pair, runs, pair_runs = lax.optimization_barrier(
        (pair, far_pair, runs, pair_runs)
    )
    pair_context = attend(column.reshape(1), pair, pair, held, far_pair, pair_runs, ())
    pair_context = exchange(pair_context)
    context = attend((1 - column).reshape(1), held, held, pair, far_own, runs, (out_other,))
    contexts = (context, pair_context, swap(context), swap(pair_context))
    glu, edge, mid_keep, mid_send = gated(
        meta, contexts, frames, other, out_weight, out_other, conv_gain,
        pointwise, pointwise_other, runs,
    )
    edges = [(2 * i, 2 * (i - 1) + 1) for i in range(1, blocks)]
    edges += [(2 * i + 1, 2 * (i + 1)) for i in range(blocks - 1)]
    edge = lax.ppermute(edge, ("tm", "head"), edges)
    mid_other = swap(mid_send)
    act = convolve(meta, glu, runs, taps, taps_other)
    act_other = swap(act)
    rim_act = rim(meta, glu, edge, runs, taps, taps_other)
    rim_other = swap(rim_act)
    done = finish(meta, act, rim_act, mid_keep, pointwise_out, pointwise_out_other)
    return finish(
        meta, act_other, rim_other, mid_other, pointwise_out, pointwise_out_other, done
    )


def solution(mesh):
    in_specs = (
        P(("grp", "tm"), "head"),
        P(("grp", "tm")),
        P("grp"),
        P(),
        P(None, None, "head"),
        P("head", None),
        P(),
        P(None, None, "head"),
        P(None, "head"),
        P("head"),
        P("head", None),
    )
    out_specs = P(("grp", "tm"), "head")
    return jax.shard_map(
        functools.partial(local, mesh.shape["tm"]),
        mesh=mesh,
        in_specs=in_specs,
        out_specs=out_specs,
        check_vma=False,
    )
```
